32 devices in a mesh: group: 2 (over x), expert: 8 (over z, y), dp: 2 (over core).
Axes of the slice: x: 2, y: 2, z: 4, core: 2. Of those that a mesh axis runs over, the one named last changes fastest.
Arguments:
- tokens: bfloat16 [4096, 2048], P(('group', 'expert', 'dp')), parts along dimension 0, may hold values from -6 to 6
- cotangent: bfloat16 [4096, 2048], P(('group', 'expert', 'dp')), parts along dimension 0, may hold values from -6 to 6
- routes: int32 [4096, 2], P(('group', 'expert', 'dp')), parts along dimension 0, may hold values from 0 to 7, all different within a row; in each aligned block of 128 rows (0 to 127, 128 to 255, ...) at most 64 rows name the same one
- route_weight: float32 [4096, 2], P(('group', 'expert', 'dp')), parts along dimension 0, may hold values from 0.1 to 1
- ratio_advantage: float32 [4096], P(('group', 'expert', 'dp')), parts along dimension 0, may hold values from -4 to 4
- clip_mask: int32 [4096], P(('group', 'expert', 'dp')), parts along dimension 0, may hold values 0 or 1
- shadow_plan: int32 [2], P('group'), parts along dimension 0, may hold values from 0 to 7
- gate_up: bfloat16 [8, 2048, 1536], P('expert'), may hold values from -0.125 to 0.125
- down: bfloat16 [8, 768, 2048], P('expert'), may hold values from -0.21875 to 0.21875
Outputs:
- token_grad: bfloat16 [4096, 2048], P(('group', 'expert', 'dp')), parts along dimension 0
- expert_grad: float32 [16, 2048, 2304], P(('group', 'expert'), 'dp'), parts along dimension 0
- shadow_grad: float32 [4096, 2304], P(('group', 'dp'), 'expert'), parts along dimension 0
The draws below stay inside these ranges and needn't reach their ends.
There are 2 independent parts, one for each index of `group`. The reference program is written for one: setup_inputs(seed, part) draws one part's arguments, and reference() takes and returns one part's arrays. A program takes and returns all parts, laid end to end along the dimension named above; an argument that names none is the same for every part. Nothing has to cross between parts.
Inputs may be any that keep to these rules, and one draw needn't show every extreme that they name: `routes`: within the rows of one device's 128 tokens no expert is named more than 64 times, a bound that some block reaches; a token names 2 different experts.
All inputs are finite; a program needn't handle non-finite values. No bound on the sum of `clip_mask` on one device may be relied on, other than what follows from the above.
Results may differ from the reference program's by a relative error of at most 0.012.
Values may be sent and summed in bfloat16 or wider, within the bound.
No kernel may reach another device: no remote copies, remote signals or barrier semaphores. Data moves between devices by JAX's collectives and lax.ppermute only.
A program may use at most 384 MiB of HBM per device.

```python
import math
import jax
import jax.numpy as jnp
import numpy as np
from jax import lax

D = 2048
FF = 768
TOP = 2
TOK_DEV = 128
EXPERTS = 8
CAP = 64
TOKENS = 2048
N_EXPERT = 8
N_DP = 2


def place_ends(entries, key, smallest, largest):
    longest = entries.shape.index(max(entries.shape))
    spots = []
    for shift in (0, 1):
        where = [jax.random.randint(jax.random.fold_in(key, axis), (), 0, length) for axis, length in enumerate(entries.shape)]
        where[longest] = (where[longest] + shift) % entries.shape[longest]
        spots.append(tuple(where))
    return entries.at[spots[0]].set(smallest).at[spots[1]].set(largest)


def strengthened(drawn, key, source, target, parts, factor):
    owner, partner = [(jnp.arange(drawn.shape[axis_at]) // (drawn.shape[axis_at] // parts)).reshape([-1 if axis == axis_at else 1 for axis in range(drawn.ndim)]) for axis_at in (source, target)]
    chosen = jax.random.permutation(key, parts)[partner]
    strong = (owner == chosen) | (owner == (partner + parts // 2) % parts)
    return jnp.where(strong, factor * drawn, drawn)


def block_levels(stream_key, extent, split, smallest, largest):
    level, own = 1.0, jax.random.fold_in(stream_key, 6)
    for dim, parts in split:
        heights = jnp.exp(jax.random.uniform(jax.random.fold_in(own, dim), (parts,), jnp.float32, smallest / len(split), largest / len(split)))
        level = level * jnp.repeat(heights, extent[dim] // parts).reshape([-1 if axis == dim else 1 for axis in range(len(extent))])
    return level


def assign_block(own_key, own, number, rows, count, top, most, lean):
    ranking = jax.random.permutation(own_key, count)
    crowded, usual = portions_of(count, rows * top, most, lean, True), portions_of(count, rows * top, most, lean, False)
    places = jnp.arange(count)

    def named(sizes, offset_by):
        used = int((sizes > 0).sum())
        fixed = max(1, used // 4)
        shifted = fixed + (places - fixed + offset_by * (used - fixed)) % max(1, count - fixed)
        return jnp.zeros((count,), jnp.int32).at[ranking[jnp.where(places < fixed, places, shifted)]].set(jnp.asarray(sizes, jnp.int32))

    sizes = jnp.where(number % 4 == 0, named(crowded, number // 4), named(usual, number - number // 4 - 1))
    mixed = jax.random.permutation(jax.random.fold_in(own, 3), count)
    source_of, sink = mixed[0:count // 2 * 2:2], mixed[1:count // 2 * 2:2]
    margin = jnp.minimum(sizes[source_of] - 1, most - sizes[sink]) // 2
    margin = jnp.where((source_of == ranking[0]) | (sink == ranking[0]) | (sizes[sink] == 0), 0, jnp.maximum(margin, 0))
    shifted = jax.random.randint(jax.random.fold_in(own, 4), (count // 2,), 0, 1 << 20) % (margin + 1)
    sizes = sizes.at[source_of].add(-shifted).at[sink].add(shifted)
    items = jnp.searchsorted(jnp.cumsum(sizes), jnp.arange(rows * top), side="right").astype(jnp.int32)
    table = items.reshape(top, rows).T
    table = table[jax.random.permutation(jax.random.fold_in(own, 1), rows)]
    offset_by = jax.random.randint(jax.random.fold_in(own, 2), (rows, 1), 0, top)
    return jnp.take_along_axis(table, (jnp.arange(top)[None, :] + offset_by) % top, axis=1)


def portions_of(number_of, total, most, lean, full):
    loads = [(1 << 20) // math.isqrt(rank ** lean) + 1 for rank in range(1, number_of + 1)]
    largest = most if full else min(most, max(-(-total // number_of), total * loads[0] // sum(loads)))
    least = 1 if total - largest >= number_of - 1 else 0
    holding, rest = [largest] + [least] * (number_of - 1), total - largest - least * (number_of - 1)
    while rest > 0:
        candidates = [i for i in range(1, number_of) if holding[i] < largest] or [i for i in range(1, number_of) if holding[i] < most]
        whole, remaining = sum([loads[i] for i in candidates]), rest
        for i in candidates:
            more = min(most - holding[i], max(1, remaining * loads[i] // whole), rest)
            holding[i] = holding[i] + more
            rest = rest - more
    return np.array(holding)


def gaussian(rng, extent, scale, bound, cuts=(), kind=jnp.bfloat16):
    result = jax.random.normal(rng, extent, jnp.float32) * scale
    if len(cuts) > 0:
        result = block_levels(rng, extent, cuts, -0.22, 0.18) * result
    return jnp.clip(result, min=-bound, max=bound).astype(kind)


def gaussian_with(rng, dims, spread, most, split, heavy, kind=jnp.bfloat16):
    entries = spread * jax.random.normal(rng, dims, jnp.float32)
    if split:
        entries = entries * block_levels(rng, dims, split, -0.22, 0.18)
    return jnp.clip(strengthened(entries, jax.random.fold_in(rng, 3), *heavy), -most, most).astype(kind)


def setup_inputs(seed: int = 0, part: int = 0) -> dict:
    key_list = jax.random.split(jax.random.key(seed), 10)
    part_keys = jax.random.split(jax.random.fold_in(key_list[9], part), 10)
    tokens = gaussian_with(part_keys[0], (TOKENS, D), 1.0, 6.0, ((0, 16),), (0, 1, 16, 2.0))
    cotangent = gaussian(part_keys[1], (TOKENS, D), 1.0, 6.0, ((0, 16),))
    routes_keys = jax.random.split(jax.random.fold_in(part_keys[2], 1), TOKENS // TOK_DEV)
    routes_turns = jax.random.permutation(jax.random.fold_in(part_keys[2], 3), TOKENS // TOK_DEV)
    routes = jax.vmap(lambda own, number: assign_block(jax.random.fold_in(part_keys[2], 2), own, number, TOK_DEV, EXPERTS, TOP, CAP, 2))(routes_keys, routes_turns).reshape((TOKENS, TOP))
    route_weight = jnp.clip(0.1 + 0.9 * jax.random.uniform(part_keys[3], (TOKENS, TOP), jnp.float32) ** block_levels(part_keys[3], (TOKENS, TOP), ((0, 16),), -0.2, 0.2), 0.1, 1.0)
    ratio_advantage = gaussian(part_keys[4], (TOKENS,), 1.0, 4.0, ((0, 16),), jnp.float32)
    clip_mask = place_ends((jax.random.randint(part_keys[5], (TOKENS,), 0, 4) < 3).astype(jnp.int32), jax.random.fold_in(part_keys[5], 1), 0, 1)
    shadow_plan = jax.random.randint(part_keys[6], (1,), 0, EXPERTS).astype(jnp.int32)
    gate_up = gaussian(key_list[7], (EXPERTS, D, 2 * FF), D ** -0.5, 0.125, ((0, 8),))
    down = gaussian(key_list[8], (EXPERTS, FF, D), FF ** -0.5, 0.21875, ((0, 8),))
    return {"tokens": tokens, "cotangent": cotangent, "routes": routes, "route_weight": route_weight, "ratio_advantage": ratio_advantage, "clip_mask": clip_mask, "shadow_plan": shadow_plan, "gate_up": gate_up, "down": down}


def take_rows(source, index):
    return jax.vmap(lambda source_rows, chosen: source_rows[chosen])(source, index)


def expert_pass(rows_in, rows_cot, weights_gu, weights_down):
    hidden_units = weights_down.shape[0]
    projected = jnp.dot(rows_in, weights_gu, preferred_element_type=jnp.float32)
    gate_pre = projected[:, :hidden_units]
    up_pre = projected[:, hidden_units:]
    sigmoid_gate = jax.nn.sigmoid(gate_pre)
    activation = gate_pre * sigmoid_gate
    hidden = (activation * up_pre).astype(jnp.bfloat16)
    hidden_grad = lax.dot_general(rows_cot, weights_down, (((1,), (1,)), ((), ())), preferred_element_type=jnp.float32)
    gate_grad = hidden_grad * up_pre * sigmoid_gate * (1.0 + gate_pre * (1.0 - sigmoid_gate))
    up_grad = hidden_grad * activation
    gate_up_grad = jnp.concatenate([gate_grad, up_grad], axis=1).astype(jnp.bfloat16)
    input_rows = lax.dot_general(gate_up_grad, weights_gu, (((1,), (1,)), ((), ())), preferred_element_type=jnp.float32)
    return input_rows.astype(jnp.bfloat16), gate_up_grad, hidden


def source_sums(rows_in, rows_cot, gate_up_grad, hidden):
    model_width = rows_in.shape[2]
    span_rows = min(model_width, 256)
    pieces = []
    for offset in range(0, model_width, span_rows):
        part_in = rows_in[:, :, offset:offset + span_rows]
        part_cot = rows_cot[:, :, offset:offset + span_rows]
        input_part = jnp.einsum("scd,scf->sdf", part_in, gate_up_grad, preferred_element_type=jnp.float32)
        down_part = jnp.einsum("scd,scf->sdf", part_cot, hidden, preferred_element_type=jnp.float32)
        rounded = lax.optimization_barrier(jnp.concatenate([input_part, down_part], axis=2).astype(jnp.bfloat16))
        pieces.append(jnp.sum(rounded.astype(jnp.float32), axis=0))
    return jnp.concatenate(pieces, axis=0)


def reference(tokens, cotangent, routes, route_weight, ratio_advantage, clip_mask, shadow_plan, gate_up, down):
    blocks = N_EXPERT * N_DP
    slot_count = TOK_DEV * TOP
    buffer_rows = EXPERTS * CAP
    slot_weight = route_weight * ratio_advantage[:, None] * clip_mask[:, None].astype(jnp.float32)
    slot_cot = (slot_weight[:, :, None] * cotangent[:, None, :].astype(jnp.float32)).astype(jnp.bfloat16)
    flat_routes = routes.reshape(blocks, slot_count)
    onehot = (flat_routes[:, :, None] == jnp.arange(EXPERTS, dtype=jnp.int32)[None, None, :]).astype(jnp.int32)
    hottest = shadow_plan[0].astype(jnp.int32)
    position = jnp.sum(jnp.cumsum(onehot, axis=1) * onehot, axis=2) - 1
    target = (flat_routes * CAP + position).astype(jnp.int32)
    block_ids = jnp.broadcast_to(jnp.arange(blocks, dtype=jnp.int32)[:, None], (blocks, slot_count))
    slot_ids = jnp.broadcast_to(jnp.arange(slot_count, dtype=jnp.int32)[None, :], (blocks, slot_count))
    slot_table = jnp.full((blocks, buffer_rows), slot_count, jnp.int32).at[block_ids, target].set(slot_ids)
    filled = (slot_table < slot_count)[:, :, None]
    clamped = jnp.minimum(slot_table, slot_count - 1).astype(jnp.int32)
    blank = jnp.zeros((), jnp.bfloat16)
    rows_in = jnp.where(filled, take_rows(tokens.reshape(blocks, TOK_DEV, D), clamped // TOP), blank)
    rows_cot = jnp.where(filled, take_rows(slot_cot.reshape(blocks, slot_count, D), clamped), blank)
    rows_in = rows_in.reshape(blocks, EXPERTS, CAP, D).transpose(1, 0, 2, 3)
    rows_cot = rows_cot.reshape(blocks, EXPERTS, CAP, D).transpose(1, 0, 2, 3)

    def one_expert(operands):
        part_in, part_cot, weights_gu, weights_down = operands
        input_rows, gate_up_grad, hidden = expert_pass(part_in.reshape(blocks * CAP, D), part_cot.reshape(blocks * CAP, D), weights_gu, weights_down)
        gradients = source_sums(part_in, part_cot, gate_up_grad.reshape(blocks, CAP, 2 * FF), hidden.reshape(blocks, CAP, FF))
        return input_rows.reshape(blocks, CAP, D), gradients

    input_rows, gradients = lax.map(one_expert, (rows_in, rows_cot, gate_up, down))
    returned = input_rows.transpose(1, 0, 2, 3).reshape(blocks, buffer_rows, D)
    slot_rows = take_rows(returned, target).reshape(TOKENS, TOP, D)
    token_grad = jnp.sum(slot_rows.astype(jnp.float32), axis=1).astype(jnp.bfloat16)
    hot_mask = (jnp.arange(EXPERTS, dtype=jnp.int32) == hottest)[:, None, None]
    expert_grad = jnp.where(hot_mask, jnp.zeros((), jnp.float32), gradients)
    shadow_grad = lax.dynamic_index_in_dim(gradients, hottest, 0, keepdims=False)
    return token_grad, expert_grad, shadow_grad
```

```python
import functools

import jax
import jax.numpy as jnp
from jax import lax
from jax.experimental import pallas as pl
from jax.experimental.pallas import tpu as pltpu
from jax.sharding import PartitionSpec as P

BF16 = jnp.bfloat16
F32 = jnp.float32
VMEM_BYTES = 56 * 1024 * 1024


def snaked(experts):
    return experts <= 8


def to_ring(expert, experts):
    if not snaked(experts):
        return expert
    down = experts - 1 - (expert - 1) // 2
    return jnp.where(expert % 2 == 0, expert // 2, down)


def from_ring(place, experts):
    if not snaked(experts):
        return place
    return jnp.where(place < experts // 2, 2 * place, 2 * (experts - 1 - place) + 1)


def ring_order(experts):
    if not snaked(experts):
        return list(range(experts))
    return list(range(0, experts, 2)) + list(range(experts - 1, 0, -2))


def distances(experts):
    half = experts // 2
    return [[0]] + [[-step, step] for step in range(1, half)] + [[half]]


def slot_place(distance, experts):
    half = experts // 2
    near = jnp.where(distance < half, 2 * distance, 2 * (experts - distance) - 1)
    near = jnp.where(distance == half, experts - 1, near)
    return jnp.where(distance == 0, 0, near)


def dot(a, b, dims):
    return lax.dot_general(a, b, ((dims[:1], dims[1:]), ((), ())), preferred_element_type=F32)


def selection(meta, expert, fanout, capacity):
    tokens = meta.shape[1]
    hit = meta[:fanout] == expert.astype(F32)
    named = jnp.sum(jnp.where(hit, 1.0, 0.0), axis=0, keepdims=True)
    weight = jnp.sum(jnp.where(hit, meta[fanout : 2 * fanout], 0.0), axis=0, keepdims=True)
    upto = lax.broadcasted_iota(jnp.int32, (tokens, tokens), 0) <= lax.broadcasted_iota(
        jnp.int32, (tokens, tokens), 1
    )
    upto = jnp.where(upto, 1.0, 0.0).astype(BF16)
    place = dot(jnp.broadcast_to(named, (8, tokens)).astype(BF16), upto, (1, 0))[:1]
    row = lax.broadcasted_iota(jnp.int32, (capacity, tokens), 0).astype(F32) + 1.0
    onehot = jnp.where((row == place) & (named > 0.5), 1.0, 0.0)
    return onehot, weight


def pick(onehot, weight, tokens, cotangent):
    rows_in = dot(onehot.astype(BF16), tokens, (1, 0)).astype(BF16)
    scale = jnp.sum(onehot * weight, axis=1, keepdims=True)
    rows_cot = (scale * dot(onehot.astype(BF16), cotangent, (1, 0))).astype(BF16)
    return rows_in, rows_cot


def step_kernel(steps, experts, fanout, capacity, local, scal, meta, *refs):
    count = len(steps)
    tok, cot = refs[:count], refs[count : 2 * count]
    gate_up, down = refs[2 * count : 2 * count + 2]
    mine, theirs, grads, hot_in, hot_cot = refs[2 * count + 2 : 2 * count + 7]
    back = refs[2 * count + 7 : 3 * count + 7]
    rows_in, rows_cot = refs[3 * count + 7 :]
    own, half, hottest = scal[0], scal[1], scal[2]
    units = down.shape[0]
    width = down.shape[1]
    for at, step in enumerate(steps):
        rows = pl.ds(at * capacity, capacity)
        if local:
            table = meta[0]
        else:
            place = (to_ring(own, experts) + step + experts) % experts
            table = meta[from_ring(place, experts)]
        onehot, weight = selection(table, own, fanout, capacity)
        rows_in[rows, :], rows_cot[rows, :] = pick(onehot, weight, tok[at][...], cot[at][...])
        onehot, weight = selection(table, hottest, fanout, capacity)
        hot_in[rows, :], hot_cot[rows, :] = pick(onehot, weight, tok[at][...], cot[at][...])
    here = pl.ds(pl.multiple_of(half * (width // 2), width // 2), width // 2)
    there = pl.ds(pl.multiple_of((1 - half) * (width // 2), width // 2), width // 2)
    mine[:, : width // 2] = rows_in[:, here]
    mine[:, width // 2 :] = rows_cot[:, here]
    theirs[:, : width // 2] = rows_in[:, there]
    theirs[:, width // 2 :] = rows_cot[:, there]
    projected = dot(rows_in[...], gate_up[...], (1, 0))
    gate_pre, up_pre = projected[:, :units], projected[:, units:]
    hidden_grad = dot(rows_cot[...], down[...], (1, 1))
    sigmoid_gate = jax.nn.sigmoid(gate_pre)
    activation = gate_pre * sigmoid_gate
    gate_grad = hidden_grad * up_pre * sigmoid_gate * (1.0 + gate_pre * (1.0 - sigmoid_gate))
    grads[:, :units] = gate_grad.astype(BF16)
    grads[:, units : 2 * units] = (hidden_grad * activation).astype(BF16)
    grads[:, 2 * units :] = (activation * up_pre).astype(BF16)
    input_rows = dot(grads[:, : 2 * units], gate_up[...], (1, 1)).astype(BF16)
    for at in range(count):
        back[at][...] = input_rows[at * capacity : (at + 1) * capacity]


def run_step(steps, experts, fanout, capacity, local, scal, meta, tok, cot, gate_up, down):
    count, rows = len(steps), len(steps) * capacity
    width, units = down.shape[1], down.shape[0]
    vmem = pl.BlockSpec(memory_space=pltpu.VMEM)
    shapes = [(rows, width), (rows, width), (rows, 3 * units), (rows, width), (rows, width)]
    shapes += [(capacity, width)] * count
    out = pl.pallas_call(
        functools.partial(step_kernel, steps, experts, fanout, capacity, local),
        out_shape=[jax.ShapeDtypeStruct(shape, BF16) for shape in shapes],
        in_specs=[pl.BlockSpec(memory_space=pltpu.SMEM)] + [vmem] * (2 * count + 3),
        out_specs=[vmem] * len(shapes),
        scratch_shapes=[pltpu.VMEM((rows, width), BF16)] * 2,
        compiler_params=pltpu.CompilerParams(vmem_limit_bytes=VMEM_BYTES),
        cost_estimate=pl.CostEstimate(
            flops=2 * 256 * 5 * width * units, bytes_accessed=3 * 2 * width * units, transcendentals=0
        ),
        name="expert_step",
    )(scal, meta, *tok, *cot, gate_up, down)
    return out[:5], out[5:]


def combine_kernel(experts, fanout, capacity, scal, meta, *refs):
    rows, out = refs[:experts], refs[experts]
    place = to_ring(scal[0], experts)
    total = jnp.zeros(out.shape, F32)
    for step in range(experts):
        expert = from_ring((place - step + experts) % experts, experts)
        onehot, _ = selection(meta[0], expert, fanout, capacity)
        total += dot(onehot.astype(BF16), rows[step][...], (0, 0))
    out[...] = total.astype(BF16)


def combine(experts, fanout, capacity, scal, meta, rows):
    vmem = pl.BlockSpec(memory_space=pltpu.VMEM)
    tokens, width = meta.shape[2], rows[0].shape[1]
    return pl.pallas_call(
        functools.partial(combine_kernel, experts, fanout, capacity),
        out_shape=jax.ShapeDtypeStruct((tokens, width), BF16),
        in_specs=[pl.BlockSpec(memory_space=pltpu.SMEM)] + [vmem] * (experts + 1),
        out_specs=vmem,
        compiler_params=pltpu.CompilerParams(vmem_limit_bytes=VMEM_BYTES),
        cost_estimate=pl.CostEstimate(
            flops=2 * experts * capacity * tokens * width, bytes_accessed=2 * experts * capacity * width, transcendentals=0
        ),
        name="token_sum",
    )(scal, meta, *rows)


def gradient_kernel(units, scal, *refs):
    count = (len(refs) - 1) // 3
    ins, cots, grads = refs[:count], refs[count : 2 * count], refs[2 * count : 3 * count]
    out = refs[3 * count]
    keep = scal[0] != scal[2]
    left = jnp.concatenate([ref[...] for ref in ins], axis=0)
    right = jnp.concatenate([ref[:, : 2 * units] for ref in grads], axis=0)
    out[0, :, : 2 * units] = jnp.where(keep, dot(left, right, (0, 0)), 0.0)
    left = jnp.concatenate([ref[...] for ref in cots], axis=0)
    right = jnp.concatenate([ref[:, 2 * units :] for ref in grads], axis=0)
    out[0, :, 2 * units :] = jnp.where(keep, dot(left, right, (0, 0)), 0.0)


def expert_gradient(scal, rows, grads):
    width, columns = rows[0].shape[1], grads[0].shape[1]
    tile = 256
    tiles = width // 2 // tile
    total = sum(part.shape[0] for part in rows)
    in_specs = [pl.BlockSpec(memory_space=pltpu.SMEM)]
    in_specs += [pl.BlockSpec((part.shape[0], tile), lambda i: (0, i)) for part in rows]
    in_specs += [pl.BlockSpec((part.shape[0], tile), lambda i: (0, i + tiles)) for part in rows]
    in_specs += [pl.BlockSpec(part.shape, lambda i: (0, 0)) for part in grads]
    return pl.pallas_call(
        functools.partial(gradient_kernel, columns // 3),
        grid=(tiles,),
        out_shape=jax.ShapeDtypeStruct((1, width // 2, columns), F32),
        in_specs=in_specs,
        out_specs=pl.BlockSpec((1, tile, columns), lambda i: (0, i, 0)),
        compiler_params=pltpu.CompilerParams(vmem_limit_bytes=VMEM_BYTES),
        cost_estimate=pl.CostEstimate(
            flops=width * columns * total, bytes_accessed=3 * width * columns, transcendentals=0
        ),
        name="expert_gradient",
    )(scal, *rows, *rows, *grads)


def turn_kernel(*refs):
    out, at = refs[-1], 0
    turned = jnp.concatenate([ref[...] for ref in refs[:-1]], axis=0)
    out[...] = turned.T


def turned_grads(grads):
    rows, columns = sum(part.shape[0] for part in grads), grads[0].shape[1]
    vmem = pl.BlockSpec(memory_space=pltpu.VMEM)
    return pl.pallas_call(
        turn_kernel,
        out_shape=jax.ShapeDtypeStruct((columns, rows), BF16),
        in_specs=[vmem] * len(grads),
        out_specs=vmem,
        compiler_params=pltpu.CompilerParams(vmem_limit_bytes=VMEM_BYTES),
        cost_estimate=pl.CostEstimate(flops=0, bytes_accessed=4 * rows * columns, transcendentals=0),
        name="turned_grads",
    )(*grads)


def shadow_kernel(plan, experts, capacity, scal, columns, *refs):
    count = len(plan)
    ins, cots = refs[:count], refs[count : 2 * count]
    mine, theirs, rows_in, rows_cot, total = refs[2 * count :]
    own, half, hottest = scal[0], scal[1], scal[2]
    shift = to_ring(own, experts) - to_ring(hottest, experts)
    for steps, part_in, part_cot in zip(plan, ins, cots):
        for at, step in enumerate(steps):
            place = slot_place((shift + step + 2 * experts) % experts, experts)
            there = pl.ds(pl.multiple_of(place * capacity, capacity), capacity)
            rows_in[there, :] = part_in[at * capacity : (at + 1) * capacity, :]
            rows_cot[there, :] = part_cot[at * capacity : (at + 1) * capacity, :]
    taken = columns.shape[0]
    column = own * taken + lax.broadcasted_iota(jnp.int32, columns.shape, 0)
    gate_part = column < taken * experts * 2 // 3
    blank = jnp.zeros((), BF16)
    total[...] = dot(jnp.where(gate_part, columns[...], blank), rows_in[...], (1, 0)) + dot(
        jnp.where(gate_part, blank, columns[...]), rows_cot[...], (1, 0)
    )
    width = total.shape[1] // 2
    mine[...] = total[:, pl.ds(pl.multiple_of(half * width, width), width)]
    theirs[...] = total[:, pl.ds(pl.multiple_of((1 - half) * width, width), width)].astype(BF16)


def shadow_gradient(plan, experts, capacity, scal, columns, ins, cots):
    vmem = pl.BlockSpec(memory_space=pltpu.VMEM)
    taken, rows = columns.shape
    width = ins[0].shape[1]
    return pl.pallas_call(
        functools.partial(shadow_kernel, plan, experts, capacity),
        out_shape=[
            jax.ShapeDtypeStruct((taken, width // 2), F32),
            jax.ShapeDtypeStruct((taken, width // 2), BF16),
        ],
        in_specs=[pl.BlockSpec(memory_space=pltpu.SMEM)] + [vmem] * (2 * len(ins) + 1),
        out_specs=[vmem] * 2,
        scratch_shapes=[pltpu.VMEM((rows, width), BF16)] * 2 + [pltpu.VMEM((taken, width), F32)],
        compiler_params=pltpu.CompilerParams(vmem_limit_bytes=VMEM_BYTES),
        cost_estimate=pl.CostEstimate(
            flops=4 * taken * rows * width, bytes_accessed=4 * rows * width, transcendentals=0
        ),
        name="shadow_gradient",
    )(scal, columns, *ins, *cots)


def on_device(
    tokens, cotangent, routes, route_weight, ratio_advantage, clip_mask, shadow_plan, gate_up, down
):
    experts = lax.axis_size("expert")
    tok_rows = tokens.shape[0]
    fanout = routes.shape[1]
    units = down.shape[1]
    capacity = 2 * tok_rows * fanout // experts
    gate_up, down = gate_up[0], down[0]
    order = ring_order(experts)
    half = experts // 2

    def shift(block, step):
        pairs = [(order[i], order[(i + step) % experts]) for i in range(experts)]
        return lax.ppermute(block, "expert", pairs)

    def swap(block):
        return lax.ppermute(block, "dp", [(0, 1), (1, 0)])

    own = lax.axis_index("expert")
    hottest = shadow_plan[0]
    scal = jnp.stack([own, lax.axis_index("dp"), hottest]).astype(jnp.int32)
    slot_weight = route_weight * ratio_advantage[:, None] * clip_mask[:, None].astype(F32)
    meta = jnp.concatenate([routes.astype(F32), slot_weight], axis=1).T
    meta = jnp.pad(meta, ((0, -meta.shape[0] % 8), (0, 0)))[None]
    meta_all = lax.all_gather(meta, "expert", axis=0, tiled=True)

    plan = distances(experts)
    rows_mine, rows_other, grads_mine, grads_other, hot_in, hot_cot = [], [], [], [], [], []
    returned = {}

    def work(steps, local, table, tok, cot):
        (mine, theirs, grads, hot_rows, hot_cots), back = run_step(
            steps, experts, fanout, capacity, local, scal, table, tok, cot, gate_up, down
        )
        for step, rows in zip(steps, back):
            returned[step % experts] = shift(rows, step) if step else rows
        rows_mine.append(mine)
        rows_other.append(swap(theirs))
        grads_mine.append(grads)
        grads_other.append(swap(grads))
        hot_in.append(hot_rows)
        hot_cot.append(hot_cots)

    up, below = (tokens, cotangent), (tokens, cotangent)
    held = [(tokens,), (cotangent,)]
    for number, steps in enumerate(plan):
        if number + 1 < half:
            next_up = tuple(shift(block, 1) for block in up)
            next_below = tuple(shift(block, -1) for block in below)
            following = [(next_up[0], next_below[0]), (next_up[1], next_below[1])]
        elif number + 1 == half:
            following = [(shift(up[0], 1),), (shift(below[1], -1),)]
        work(steps, number == 0, meta if number == 0 else meta_all, *held)
        if number + 1 < half:
            up, below = next_up, next_below
        held = following

    expert_grad = expert_gradient(scal, rows_mine + rows_other, grads_mine + grads_other)

    turned = turned_grads(grads_mine)
    taken = 3 * units // experts
    ring_hot = to_ring(hottest, experts)
    is_hot = own == hottest

    def chunk(distance):
        owner = from_ring((ring_hot + distance + experts) % experts, experts)
        return lax.dynamic_slice_in_dim(turned, owner * taken, taken, axis=0)

    ahead, behind = None, None
    for number in range(half):
        mine = chunk(half - number)
        ahead = shift(mine if ahead is None else jnp.where(is_hot, mine, ahead), 1)
        if number < half - 1:
            mine = chunk(number + 1 - half)
            behind = shift(mine if behind is None else jnp.where(is_hot, mine, behind), -1)
    away = (to_ring(own, experts) - ring_hot + experts) % experts
    columns = jnp.where(away == 0, chunk(0), jnp.where(away <= half, ahead, behind))
    shadow_mine, shadow_theirs = shadow_gradient(
        plan, experts, capacity, scal, columns, hot_in, hot_cot
    )
    shadow_grad = (shadow_mine + swap(shadow_theirs).astype(F32)).T

    token_grad = combine(experts, fanout, capacity, scal, meta, [returned[d] for d in range(experts)])
    return (token_grad, expert_grad, shadow_grad)


def solution(mesh):
    placed = (
        P(("group", "expert", "dp"), None),
        P(("group", "expert", "dp"), None),
        P(("group", "expert", "dp"), None),
        P(("group", "expert", "dp"), None),
        P(("group", "expert", "dp")),
        P(("group", "expert", "dp")),
        P("group"),
        P("expert", None, None),
        P("expert", None, None),
    )
    return jax.shard_map(
        on_device,
        mesh=mesh,
        in_specs=placed,
        out_specs=(
            P(("group", "expert", "dp"), None),
            P(("group", "expert"), "dp", None),
            P(("group", "dp"), "expert"),
        ),
        check_vma=False,
    )
```

```python
import functools

import jax
import jax.numpy as jnp
from jax import lax
from jax.experimental import pallas as pl
from jax.experimental.pallas import tpu as pltpu
from jax.sharding import PartitionSpec as P

BF16 = jnp.bfloat16
F32 = jnp.float32
VMEM_BYTES = 56 * 1024 * 1024


def snaked(experts):
    return experts <= 8


def to_ring(expert, experts):
    if not snaked(experts):
        return expert
    down = experts - 1 - (expert - 1) // 2
    return jnp.where(expert % 2 == 0, expert // 2, down)


def from_ring(place, experts):
    if not snaked(experts):
        return place
    return jnp.where(place < experts // 2, 2 * place, 2 * (experts - 1 - place) + 1)


def ring_order(experts):
    if not snaked(experts):
        return list(range(experts))
    return list(range(0, experts, 2)) + list(range(experts - 1, 0, -2))


def distances(experts):
    half = experts // 2
    return [[0]] + [[-step, step] for step in range(1, half)] + [[half]]


def slot_place(distance, experts):
    half = experts // 2
    near = jnp.where(distance < half, 2 * distance - 1, 2 * (experts - distance) - 2)
    near = jnp.where(distance == half, experts - 1, near)
    return jnp.where(distance == 0, experts - 2, near)


def dot(a, b, dims):
    return lax.dot_general(a, b, ((dims[:1], dims[1:]), ((), ())), preferred_element_type=F32)


def selection(table, expert, fanout, capacity):
    tokens = table.shape[1]
    hit = table[:fanout] == expert.astype(F32)
    named = jnp.sum(jnp.where(hit, 1.0, 0.0), axis=0, keepdims=True)
    parts = table[fanout : 4 * fanout]
    weights = parts[:fanout] + parts[fanout : 2 * fanout] + parts[2 * fanout :]
    weight = jnp.sum(jnp.where(hit, weights, 0.0), axis=0, keepdims=True)
    upto = lax.broadcasted_iota(jnp.int32, (tokens, tokens), 0) <= lax.broadcasted_iota(
        jnp.int32, (tokens, tokens), 1
    )
    upto = jnp.where(upto, 1.0, 0.0).astype(BF16)
    place = dot(jnp.broadcast_to(named, (8, tokens)).astype(BF16), upto, (1, 0))[:1]
    row = lax.broadcasted_iota(jnp.int32, (capacity, tokens), 0).astype(F32) + 1.0
    onehot = jnp.where((row == place) & (named > 0.5), 1.0, 0.0)
    return onehot, weight


def step_kernel(steps, fanout, capacity, joined, scal, *refs):
    count = len(steps)
    blocks, refs = refs[: max(count, 1 + joined)], refs[max(count, 1 + joined) :]
    if joined:
        first, refs = refs[0], refs[1:]
        blocks = [jnp.concatenate([block[...] for block in blocks], axis=1)]
    weights_gu, weights_down, mine, pack, hot_in, hot_cot = refs[:6]
    back, refs = refs[6 : 6 + count], refs[6 + count :]
    if len(refs) > 5:
        turned, refs = refs[0], refs[1:]
    else:
        turned = None
    rows_in, rows_cot, gate_up, down, sems = refs
    own, half, hottest = scal[0], scal[1], scal[2]
    units, width = down.shape
    load_gu = pltpu.make_async_copy(weights_gu, gate_up, sems.at[0])
    load_down = pltpu.make_async_copy(weights_down, down, sems.at[1])
    load_gu.start()
    load_down.start()
    for at, block in enumerate(blocks):
        rows = slice(at * capacity, (at + 1) * capacity)
        table = block[:, 2 * width :].astype(F32).T
        own_hot, own_weight = selection(table, own, fanout, capacity)
        all_hot, all_weight = selection(table, hottest, fanout, capacity)
        scale = jnp.concatenate(
            [
                jnp.sum(own_hot * own_weight, axis=1, keepdims=True),
                jnp.sum(all_hot * all_weight, axis=1, keepdims=True),
            ],
            axis=0,
        )
        onehot = jnp.concatenate([own_hot, all_hot], axis=0).astype(BF16)
        picked = dot(onehot, block[:, :width], (1, 0)).astype(BF16)
        rows_in[rows, :] = picked[:capacity]
        hot_in[rows, :] = picked[capacity:]
        picked = (scale * dot(onehot, block[:, width : 2 * width], (1, 0))).astype(BF16)
        rows_cot[rows, :] = picked[:capacity]
        hot_cot[rows, :] = picked[capacity:]
    part = width // 2
    here = pl.ds(pl.multiple_of(half * part, part), part)
    there = pl.ds(pl.multiple_of((1 - half) * part, part), part)
    mine[:, :part] = rows_in[:, here]
    mine[:, part:] = rows_cot[:, here]
    pack[:, :part] = rows_in[:, there]
    pack[:, part:width] = rows_cot[:, there]
    load_gu.wait()
    projected = dot(rows_in[...], gate_up[...], (1, 0))
    gate_pre, up_pre = projected[:, :units], projected[:, units:]
    load_down.wait()
    hidden_grad = dot(rows_cot[...], down[...], (1, 1))
    sigmoid_gate = jax.nn.sigmoid(gate_pre)
    activation = gate_pre * sigmoid_gate
    gate_grad = hidden_grad * up_pre * sigmoid_gate * (1.0 + gate_pre * (1.0 - sigmoid_gate))
    pack[:, width : width + units] = gate_grad.astype(BF16)
    pack[:, width + units : width + 2 * units] = (hidden_grad * activation).astype(BF16)
    pack[:, width + 2 * units :] = (activation * up_pre).astype(BF16)
    input_rows = dot(pack[:, width : width + 2 * units], gate_up[...], (1, 1)).astype(BF16)
    for at in range(count):
        back[at][...] = input_rows[at * capacity : (at + 1) * capacity]
    if turned is not None:
        grads = pack[:, width:]
        if joined:
            grads = jnp.concatenate([first[:, width:], grads], axis=0)
        turned[...] = grads.T


def run_step(steps, fanout, capacity, scal, blocks, first, gate_up, down):
    count, rows = len(steps), len(steps) * capacity
    units, width = down.shape
    vmem = pl.BlockSpec(memory_space=pltpu.VMEM)
    far = pl.BlockSpec(memory_space=pl.ANY)
    shapes = [(rows, width), (rows, width + 3 * units), (rows, width), (rows, width)]
    shapes += [(capacity, width)] * count
    joined = first is not None
    if joined or count > 1:
        shapes += [(3 * units, 2 * capacity)]
    firsts = [first] if joined else []
    out = pl.pallas_call(
        functools.partial(step_kernel, steps, fanout, capacity, joined),
        out_shape=[jax.ShapeDtypeStruct(shape, BF16) for shape in shapes],
        in_specs=[pl.BlockSpec(memory_space=pltpu.SMEM)] + [vmem] * (len(blocks) + len(firsts)) + [far] * 2,
        out_specs=[vmem] * len(shapes),
        scratch_shapes=[pltpu.VMEM((rows, width), BF16)] * 2
        + [
            pltpu.VMEM(gate_up.shape, BF16),
            pltpu.VMEM(down.shape, BF16),
            pltpu.SemaphoreType.DMA((2,)),
        ],
        compiler_params=pltpu.CompilerParams(vmem_limit_bytes=VMEM_BYTES),
        cost_estimate=pl.CostEstimate(
            flops=2 * 256 * 5 * width * units, bytes_accessed=3 * 2 * width * units, transcendentals=0
        ),
        name="expert_step",
    )(scal, *blocks, *firsts, gate_up, down)
    return out[:4], out[4 : 4 + count], out[4 + count :]


def combine_kernel(experts, fanout, capacity, scal, meta, *refs):
    rows, out = refs[:experts], refs[experts]
    place = to_ring(scal[0], experts)
    table = meta[...].astype(F32).T
    picks = []
    for step in range(experts):
        expert = from_ring((place - step + experts) % experts, experts)
        picks.append(selection(table, expert, fanout, capacity)[0])
    onehot = jnp.concatenate(picks, axis=0).astype(BF16)
    out[...] = dot(onehot, jnp.concatenate([part[...] for part in rows], axis=0), (0, 0)).astype(BF16)


def combine(experts, fanout, capacity, scal, meta, rows):
    vmem = pl.BlockSpec(memory_space=pltpu.VMEM)
    tokens, width = meta.shape[0], rows[0].shape[1]
    return pl.pallas_call(
        functools.partial(combine_kernel, experts, fanout, capacity),
        out_shape=jax.ShapeDtypeStruct((tokens, width), BF16),
        in_specs=[pl.BlockSpec(memory_space=pltpu.SMEM)] + [vmem] * (experts + 1),
        out_specs=vmem,
        compiler_params=pltpu.CompilerParams(vmem_limit_bytes=VMEM_BYTES),
        cost_estimate=pl.CostEstimate(
            flops=2 * experts * capacity * tokens * width, bytes_accessed=2 * experts * capacity * width, transcendentals=0
        ),
        name="token_sum",
    )(scal, meta, *rows)


def gradient_kernel(units, count, scal, *refs):
    ins, cots, packs = refs[: 2 * count], refs[2 * count : 4 * count], refs[4 * count : 6 * count]
    out = refs[6 * count]
    keep = scal[0] != scal[2]
    width = packs[0].shape[1] - 3 * units
    left = jnp.concatenate([ref[...] for ref in ins], axis=0)
    right = jnp.concatenate([ref[:, width : width + 2 * units] for ref in packs], axis=0)
    out[0, :, : 2 * units] = jnp.where(keep, dot(left, right, (0, 0)), 0.0)
    left = jnp.concatenate([ref[...] for ref in cots], axis=0)
    right = jnp.concatenate([ref[:, width + 2 * units :] for ref in packs], axis=0)
    out[0, :, 2 * units :] = jnp.where(keep, dot(left, right, (0, 0)), 0.0)


def expert_gradient(units, scal, mine, packs, others):
    width, columns, count = mine[0].shape[1], 3 * units, len(mine)
    tile = 256
    tiles = width // 2 // tile
    total = 2 * sum(part.shape[0] for part in mine)
    rows = mine + others
    in_specs = [pl.BlockSpec(memory_space=pltpu.SMEM)]
    in_specs += [pl.BlockSpec((part.shape[0], tile), lambda i: (0, i)) for part in rows]
    in_specs += [pl.BlockSpec((part.shape[0], tile), lambda i: (0, i + tiles)) for part in rows]
    in_specs += [pl.BlockSpec(part.shape, lambda i: (0, 0)) for part in packs + others]
    return pl.pallas_call(
        functools.partial(gradient_kernel, units, count),
        grid=(tiles,),
        out_shape=jax.ShapeDtypeStruct((1, width // 2, columns), F32),
        in_specs=in_specs,
        out_specs=pl.BlockSpec((1, tile, columns), lambda i: (0, i, 0)),
        compiler_params=pltpu.CompilerParams(vmem_limit_bytes=VMEM_BYTES),
        cost_estimate=pl.CostEstimate(
            flops=width * columns * total, bytes_accessed=3 * width * columns, transcendentals=0
        ),
        name="expert_gradient",
    )(scal, *rows, *rows, *packs, *others)


def shadow_kernel(plan, experts, capacity, scal, columns, *refs):
    count = len(plan)
    ins, cots = refs[:count], refs[count : 2 * count]
    mine, theirs, rows_in, rows_cot, total = refs[2 * count :]
    own, half, hottest = scal[0], scal[1], scal[2]
    shift = to_ring(own, experts) - to_ring(hottest, experts)
    taken = columns.shape[0]
    gates = taken * experts * 2 // 3
    column = own * taken + lax.broadcasted_iota(jnp.int32, columns.shape, 0)
    blank = jnp.zeros((), BF16)

    def in_order(parts, rows):
        for steps, part in zip(plan, parts):
            for at, step in enumerate(steps):
                place = slot_place((shift + step + 2 * experts) % experts, experts)
                there = pl.ds(pl.multiple_of(place * capacity, capacity), capacity)
                rows[there, :] = part[at * capacity : (at + 1) * capacity, :]

    @pl.when(own * taken < gates)
    def _():
        in_order(ins, rows_in)
        total[...] = dot(jnp.where(column < gates, columns[...], blank), rows_in[...], (1, 0))

    @pl.when(own * taken >= gates)
    def _():
        total[...] = jnp.zeros(total.shape, F32)

    @pl.when((own + 1) * taken > gates)
    def _():
        in_order(cots, rows_cot)
        total[...] += dot(jnp.where(column < gates, blank, columns[...]), rows_cot[...], (1, 0))

    width = total.shape[1] // 2
    mine[...] = total[:, pl.ds(pl.multiple_of(half * width, width), width)]
    theirs[...] = total[:, pl.ds(pl.multiple_of((1 - half) * width, width), width)].astype(BF16)


def shadow_gradient(plan, experts, capacity, scal, columns, ins, cots):
    vmem = pl.BlockSpec(memory_space=pltpu.VMEM)
    taken, rows = columns.shape
    width = ins[0].shape[1]
    return pl.pallas_call(
        functools.partial(shadow_kernel, plan, experts, capacity),
        out_shape=[
            jax.ShapeDtypeStruct((taken, width // 2), F32),
            jax.ShapeDtypeStruct((taken, width // 2), BF16),
        ],
        in_specs=[pl.BlockSpec(memory_space=pltpu.SMEM)] + [vmem] * (2 * len(ins) + 1),
        out_specs=[vmem] * 2,
        scratch_shapes=[pltpu.VMEM((rows, width), BF16)] * 2 + [pltpu.VMEM((taken, width), F32)],
        compiler_params=pltpu.CompilerParams(vmem_limit_bytes=VMEM_BYTES),
        cost_estimate=pl.CostEstimate(
            flops=4 * taken * rows * width, bytes_accessed=4 * rows * width, transcendentals=0
        ),
        name="shadow_gradient",
    )(scal, columns, *ins, *cots)


def on_device(
    tokens, cotangent, routes, route_weight, ratio_advantage, clip_mask, shadow_plan, gate_up, down
):
    experts = lax.axis_size("expert")
    tok_rows, width = tokens.shape
    fanout = routes.shape[1]
    units = down.shape[1]
    capacity = 2 * tok_rows * fanout // experts
    gate_up, down = gate_up[0], down[0]
    order = ring_order(experts)
    half = experts // 2

    def shift(block, step):
        pairs = [(order[i], order[(i + step) % experts]) for i in range(experts)]
        return lax.ppermute(block, "expert", pairs)

    def swap(block):
        return lax.ppermute(block, "dp", [(0, 1), (1, 0)])

    own = lax.axis_index("expert")
    hottest = shadow_plan[0]
    scal = jnp.stack([own, lax.axis_index("dp"), hottest]).astype(jnp.int32)
    slot_weight = route_weight * ratio_advantage[:, None] * clip_mask[:, None].astype(F32)
    first = lax.reduce_precision(slot_weight, 8, 7)
    rest = slot_weight - first
    second = lax.reduce_precision(rest, 8, 7)
    meta = jnp.concatenate([routes.astype(F32), first, second, rest - second], axis=1)
    meta = jnp.pad(meta, ((0, 0), (0, 128 - meta.shape[1]))).astype(BF16)
    message = jnp.concatenate([tokens, cotangent, meta], axis=1)

    plan = distances(experts)
    mine, packs, others, hot_in, hot_cot, turned, late = [], [], [], [], [], [], []
    returned = {}
    up, below, held = message, message, [message]
    for number, steps in enumerate(plan):
        if number + 1 < half:
            following = [shift(up, 1), shift(below, -1)]
        elif number + 1 == half:
            following = [shift(up[:, :width], 1), shift(below[:, width:], -1)]
        if number > 1:
            held, late[number - 2] = lax.optimization_barrier((held, late[number - 2]))
        (rows, pack, hot_rows, hot_cots), back, turn = run_step(
            steps, fanout, capacity, scal, held, packs[0] if number == half else None, gate_up, down
        )
        following, back = lax.optimization_barrier((following, back))
        sent = [shift(part, step) if step else part for step, part in zip(steps, back)]
        late.append((sent, swap(pack)))
        mine.append(rows)
        packs.append(pack)
        hot_in.append(hot_rows)
        hot_cot.append(hot_cots)
        turned += turn
        held = following
        if number < half:
            up, below = following
    taken = 3 * units // experts
    ring_hot = to_ring(hottest, experts)
    is_hot = own == hottest

    def chunk(distance):
        owner = from_ring((ring_hot + distance + experts) % experts, experts)
        parts = [lax.dynamic_slice_in_dim(part, owner * taken, taken, axis=0) for part in turned]
        return jnp.concatenate(parts, axis=1)

    ahead, behind = None, None
    for number in range(half):
        part = chunk(half - number)
        if 0 < number < 3:
            at = half - 2 + number
            (ahead, behind), late[at] = lax.optimization_barrier(((ahead, behind), late[at]))
        ahead = shift(part if ahead is None else jnp.where(is_hot, part, ahead), 1)
        if number < half - 1:
            part = chunk(number + 1 - half)
            behind = shift(part if behind is None else jnp.where(is_hot, part, behind), -1)
    for steps, (sent, other) in zip(plan, late):
        others.append(other)
        for step, part in zip(steps, sent):
            returned[step % experts] = part

    expert_grad = expert_gradient(units, scal, mine, packs, others)

    away = (to_ring(own, experts) - ring_hot + experts) % experts
    columns = jnp.where(away == 0, chunk(0), jnp.where(away <= half, ahead, behind))
    columns, expert_grad = lax.optimization_barrier((columns, expert_grad))
    shadow_mine, shadow_theirs = shadow_gradient(
        plan, experts, capacity, scal, columns, hot_in, hot_cot
    )
    shadow_grad = (shadow_mine + swap(shadow_theirs).astype(F32)).T

    token_grad = combine(experts, fanout, capacity, scal, meta, [returned[d] for d in range(experts)])
    return (token_grad, expert_grad, shadow_grad)


def solution(mesh):
    placed = (
        P(("group", "expert", "dp"), None),
        P(("group", "expert", "dp"), None),
        P(("group", "expert", "dp"), None),
        P(("group", "expert", "dp"), None),
        P(("group", "expert", "dp")),
        P(("group", "expert", "dp")),
        P("group"),
        P("expert", None, None),
        P("expert", None, None),
    )
    return jax.shard_map(
        on_device,
        mesh=mesh,
        in_specs=placed,
        out_specs=(
            P(("group", "expert", "dp"), None),
            P(("group", "expert"), "dp", None),
            P(("group", "dp"), "expert"),
        ),
        check_vma=False,
    )
```

```python
import functools

import jax
import jax.numpy as jnp
from jax import lax
from jax.experimental import pallas as pl
from jax.experimental.pallas import tpu as pltpu
from jax.sharding import PartitionSpec as P

BF16 = jnp.bfloat16
F32 = jnp.float32
VMEM_BYTES = 56 * 1024 * 1024


def snaked(experts):
    return experts <= 8


def to_ring(expert, experts):
    if not snaked(experts):
        return expert
    down = experts - 1 - (expert - 1) // 2
    return jnp.where(expert % 2 == 0, expert // 2, down)


def from_ring(place, experts):
    if not snaked(experts):
        return place
    return jnp.where(place < experts // 2, 2 * place, 2 * (experts - 1 - place) + 1)


def ring_order(experts):
    if not snaked(experts):
        return list(range(experts))
    return list(range(0, experts, 2)) + list(range(experts - 1, 0, -2))


def distances(experts):
    half = experts // 2
    return [[0]] + [[-step, step] for step in range(1, half)] + [[half]]


def slot_place(distance, experts):
    half = experts // 2
    near = jnp.where(distance < half, 2 * distance - 1, 2 * (experts - distance) - 2)
    near = jnp.where(distance == half, experts - 1, near)
    return jnp.where(distance == 0, experts - 2, near)


def dot(a, b, dims):
    return lax.dot_general(a, b, ((dims[:1], dims[1:]), ((), ())), preferred_element_type=F32)


def selection(table, expert, fanout, capacity):
    tokens = table.shape[1]
    hit = table[:fanout] == expert.astype(F32)
    named = jnp.sum(jnp.where(hit, 1.0, 0.0), axis=0, keepdims=True)
    parts = table[fanout : 4 * fanout]
    weights = parts[:fanout] + parts[fanout : 2 * fanout] + parts[2 * fanout :]
    weight = jnp.sum(jnp.where(hit, weights, 0.0), axis=0, keepdims=True)
    upto = lax.broadcasted_iota(jnp.int32, (tokens, tokens), 0) <= lax.broadcasted_iota(
        jnp.int32, (tokens, tokens), 1
    )
    upto = jnp.where(upto, 1.0, 0.0).astype(BF16)
    place = dot(jnp.broadcast_to(named, (8, tokens)).astype(BF16), upto, (1, 0))[:1]
    row = lax.broadcasted_iota(jnp.int32, (capacity, tokens), 0).astype(F32) + 1.0
    onehot = jnp.where((row == place) & (named > 0.5), 1.0, 0.0)
    return onehot, weight


def step_kernel(steps, fanout, capacity, joined, scal, *refs):
    count = len(steps)
    blocks, refs = refs[: max(count, 1 + joined)], refs[max(count, 1 + joined) :]
    if joined:
        first, refs = refs[0], refs[1:]
        blocks = [jnp.concatenate([block[...] for block in blocks], axis=1)]
    weights_gu, weights_down, mine, pack, hot_in, hot_cot = refs[:6]
    back, refs = refs[6 : 6 + count], refs[6 + count :]
    if len(refs) > 5:
        turned, refs = refs[0], refs[1:]
    else:
        turned = None
    rows_in, rows_cot, gate_up, down, sems = refs
    own, half, hottest = scal[0], scal[1], scal[2]
    units, width = down.shape
    load_gu = pltpu.make_async_copy(weights_gu, gate_up, sems.at[0])
    load_down = pltpu.make_async_copy(weights_down, down, sems.at[1])
    load_gu.start()
    load_down.start()
    for at, block in enumerate(blocks):
        rows = slice(at * capacity, (at + 1) * capacity)
        table = block[:, 2 * width :].astype(F32).T
        own_hot, own_weight = selection(table, own, fanout, capacity)
        all_hot, all_weight = selection(table, hottest, fanout, capacity)
        scale = jnp.concatenate(
            [
                jnp.sum(own_hot * own_weight, axis=1, keepdims=True),
                jnp.sum(all_hot * all_weight, axis=1, keepdims=True),
            ],
            axis=0,
        )
        onehot = jnp.concatenate([own_hot, all_hot], axis=0).astype(BF16)
        picked = dot(onehot, block[:, :width], (1, 0)).astype(BF16)
        rows_in[rows, :] = picked[:capacity]
        hot_in[rows, :] = picked[capacity:]
        picked = (scale * dot(onehot, block[:, width : 2 * width], (1, 0))).astype(BF16)
        rows_cot[rows, :] = picked[:capacity]
        hot_cot[rows, :] = picked[capacity:]
    part = width // 2
    here = pl.ds(pl.multiple_of(half * part, part), part)
    there = pl.ds(pl.multiple_of((1 - half) * part, part), part)
    mine[:, :part] = rows_in[:, here]
    mine[:, part:] = rows_cot[:, here]
    pack[:, :part] = rows_in[:, there]
    pack[:, part:width] = rows_cot[:, there]
    load_gu.wait()
    projected = dot(rows_in[...], gate_up[...], (1, 0))
    gate_pre, up_pre = projected[:, :units], projected[:, units:]
    load_down.wait()
    hidden_grad = dot(rows_cot[...], down[...], (1, 1))
    sigmoid_gate = jax.nn.sigmoid(gate_pre)
    activation = gate_pre * sigmoid_gate
    gate_grad = hidden_grad * up_pre * sigmoid_gate * (1.0 + gate_pre * (1.0 - sigmoid_gate))
    pack[:, width : width + units] = gate_grad.astype(BF16)
    pack[:, width + units : width + 2 * units] = (hidden_grad * activation).astype(BF16)
    pack[:, width + 2 * units :] = (activation * up_pre).astype(BF16)
    input_rows = dot(pack[:, width : width + 2 * units], gate_up[...], (1, 1)).astype(BF16)
    for at in range(count):
        back[at][...] = input_rows[at * capacity : (at + 1) * capacity]
    if turned is not None:
        grads = pack[:, width:]
        if joined:
            grads = jnp.concatenate([first[:, width:], grads], axis=0)
        turned[...] = grads.T


def run_step(steps, fanout, capacity, scal, blocks, first, gate_up, down):
    count, rows = len(steps), len(steps) * capacity
    units, width = down.shape
    vmem = pl.BlockSpec(memory_space=pltpu.VMEM)
    far = pl.BlockSpec(memory_space=pl.ANY)
    shapes = [(rows, width), (rows, width + 3 * units), (rows, width), (rows, width)]
    shapes += [(capacity, width)] * count
    joined = first is not None
    if joined or count > 1:
        shapes += [(3 * units, 2 * capacity)]
    firsts = [first] if joined else []
    out = pl.pallas_call(
        functools.partial(step_kernel, steps, fanout, capacity, joined),
        out_shape=[jax.ShapeDtypeStruct(shape, BF16) for shape in shapes],
        in_specs=[pl.BlockSpec(memory_space=pltpu.SMEM)] + [vmem] * (len(blocks) + len(firsts)) + [far] * 2,
        out_specs=[vmem] * len(shapes),
        scratch_shapes=[pltpu.VMEM((rows, width), BF16)] * 2
        + [
            pltpu.VMEM(gate_up.shape, BF16),
            pltpu.VMEM(down.shape, BF16),
            pltpu.SemaphoreType.DMA((2,)),
        ],
        compiler_params=pltpu.CompilerParams(vmem_limit_bytes=VMEM_BYTES),
        cost_estimate=pl.CostEstimate(
            flops=2 * 256 * 5 * width * units, bytes_accessed=3 * 2 * width * units, transcendentals=0
        ),
        name="expert_step",
    )(scal, *blocks, *firsts, gate_up, down)
    return out[:4], out[4 : 4 + count], out[4 + count :]


def combine_kernel(experts, fanout, capacity, scal, meta, *refs):
    rows, out = refs[:experts], refs[experts]
    place = to_ring(scal[0], experts)
    table = meta[...].astype(F32).T
    picks = []
    for step in range(experts):
        expert = from_ring((place - step + experts) % experts, experts)
        picks.append(selection(table, expert, fanout, capacity)[0])
    onehot = jnp.concatenate(picks, axis=0).astype(BF16)
    out[...] = dot(onehot, jnp.concatenate([part[...] for part in rows], axis=0), (0, 0)).astype(BF16)


def combine(experts, fanout, capacity, scal, meta, rows):
    vmem = pl.BlockSpec(memory_space=pltpu.VMEM)
    tokens, width = meta.shape[0], rows[0].shape[1]
    return pl.pallas_call(
        functools.partial(combine_kernel, experts, fanout, capacity),
        out_shape=jax.ShapeDtypeStruct((tokens, width), BF16),
        in_specs=[pl.BlockSpec(memory_space=pltpu.SMEM)] + [vmem] * (experts + 1),
        out_specs=vmem,
        compiler_params=pltpu.CompilerParams(vmem_limit_bytes=VMEM_BYTES),
        cost_estimate=pl.CostEstimate(
            flops=2 * experts * capacity * tokens * width, bytes_accessed=2 * experts * capacity * width, transcendentals=0
        ),
        name="token_sum",
    )(scal, meta, *rows)


def gradient_kernel(units, count, scal, *refs):
    ins, cots, packs = refs[: 2 * count], refs[2 * count : 4 * count], refs[4 * count : 6 * count]
    out = refs[6 * count]
    keep = scal[0] != scal[2]
    width = packs[0].shape[1] - 3 * units
    left = jnp.concatenate([ref[...] for ref in ins], axis=0)
    right = jnp.concatenate([ref[:, width : width + 2 * units] for ref in packs], axis=0)
    out[0, :, : 2 * units] = jnp.where(keep, dot(left, right, (0, 0)), 0.0)
    left = jnp.concatenate([ref[...] for ref in cots], axis=0)
    right = jnp.concatenate([ref[:, width + 2 * units :] for ref in packs], axis=0)
    out[0, :, 2 * units :] = jnp.where(keep, dot(left, right, (0, 0)), 0.0)


def expert_gradient(units, scal, mine, packs, others):
    width, columns, count = mine[0].shape[1], 3 * units, len(mine)
    tile = 256
    tiles = width // 2 // tile
    total = 2 * sum(part.shape[0] for part in mine)
    rows = mine + others
    in_specs = [pl.BlockSpec(memory_space=pltpu.SMEM)]
    in_specs += [pl.BlockSpec((part.shape[0], tile), lambda i: (0, i)) for part in rows]
    in_specs += [pl.BlockSpec((part.shape[0], tile), lambda i: (0, i + tiles)) for part in rows]
    in_specs += [pl.BlockSpec(part.shape, lambda i: (0, 0)) for part in packs + others]
    return pl.pallas_call(
        functools.partial(gradient_kernel, units, count),
        grid=(tiles,),
        out_shape=jax.ShapeDtypeStruct((1, width // 2, columns), F32),
        in_specs=in_specs,
        out_specs=pl.BlockSpec((1, tile, columns), lambda i: (0, i, 0)),
        compiler_params=pltpu.CompilerParams(vmem_limit_bytes=VMEM_BYTES),
        cost_estimate=pl.CostEstimate(
            flops=width * columns * total, bytes_accessed=3 * width * columns, transcendentals=0
        ),
        name="expert_gradient",
    )(scal, *rows, *rows, *packs, *others)


def shadow_kernel(plan, experts, capacity, scal, kept, ahead, behind, *refs):
    count = len(plan)
    ins, cots = refs[:count], refs[count : 2 * count]
    mine, theirs, rows_in, rows_cot, total = refs[2 * count :]
    own, half, hottest = scal[0], scal[1], scal[2]
    shift = to_ring(own, experts) - to_ring(hottest, experts)
    taken = kept.shape[0]
    gates = taken * experts * 2 // 3
    column = own * taken + lax.broadcasted_iota(jnp.int32, kept.shape, 0)
    blank = jnp.zeros((), BF16)
    away = (shift + experts) % experts
    received = jnp.where(away <= experts // 2, ahead[...], behind[...])
    columns = jnp.where(away == 0, kept[...], received)

    def in_order(parts, rows):
        for steps, part in zip(plan, parts):
            for at, step in enumerate(steps):
                place = slot_place((shift + step + 2 * experts) % experts, experts)
                there = pl.ds(pl.multiple_of(place * capacity, capacity), capacity)
                rows[there, :] = part[at * capacity : (at + 1) * capacity, :]

    @pl.when(own * taken < gates)
    def _():
        in_order(ins, rows_in)
        total[...] = dot(jnp.where(column < gates, columns, blank), rows_in[...], (1, 0))

    @pl.when(own * taken >= gates)
    def _():
        total[...] = jnp.zeros(total.shape, F32)

    @pl.when((own + 1) * taken > gates)
    def _():
        in_order(cots, rows_cot)
        total[...] += dot(jnp.where(column < gates, blank, columns), rows_cot[...], (1, 0))

    width = total.shape[1] // 2
    mine[...] = total[:, pl.ds(pl.multiple_of(half * width, width), width)]
    theirs[...] = total[:, pl.ds(pl.multiple_of((1 - half) * width, width), width)].astype(BF16)


def shadow_gradient(plan, experts, capacity, scal, columns, ins, cots):
    vmem = pl.BlockSpec(memory_space=pltpu.VMEM)
    taken, rows = columns[0].shape
    width = ins[0].shape[1]
    return pl.pallas_call(
        functools.partial(shadow_kernel, plan, experts, capacity),
        out_shape=[
            jax.ShapeDtypeStruct((taken, width // 2), F32),
            jax.ShapeDtypeStruct((taken, width // 2), BF16),
        ],
        in_specs=[pl.BlockSpec(memory_space=pltpu.SMEM)] + [vmem] * (2 * len(ins) + 3),
        out_specs=[vmem] * 2,
        scratch_shapes=[pltpu.VMEM((rows, width), BF16)] * 2 + [pltpu.VMEM((taken, width), F32)],
        compiler_params=pltpu.CompilerParams(vmem_limit_bytes=VMEM_BYTES),
        cost_estimate=pl.CostEstimate(
            flops=4 * taken * rows * width, bytes_accessed=4 * rows * width, transcendentals=0
        ),
        name="shadow_gradient",
    )(scal, *columns, *ins, *cots)


def on_device(
    tokens, cotangent, routes, route_weight, ratio_advantage, clip_mask, shadow_plan, gate_up, down
):
    experts = lax.axis_size("expert")
    tok_rows, width = tokens.shape
    fanout = routes.shape[1]
    units = down.shape[1]
    capacity = 2 * tok_rows * fanout // experts
    gate_up, down = gate_up[0], down[0]
    order = ring_order(experts)
    half = experts // 2

    def shift(block, step):
        pairs = [(order[i], order[(i + step) % experts]) for i in range(experts)]
        return lax.ppermute(block, "expert", pairs)

    def swap(block):
        return lax.ppermute(block, "dp", [(0, 1), (1, 0)])

    own = lax.axis_index("expert")
    hottest = shadow_plan[0]
    scal = jnp.stack([own, lax.axis_index("dp"), hottest]).astype(jnp.int32)
    slot_weight = route_weight * ratio_advantage[:, None] * clip_mask[:, None].astype(F32)
    first = lax.reduce_precision(slot_weight, 8, 7)
    rest = slot_weight - first
    second = lax.reduce_precision(rest, 8, 7)
    meta = jnp.concatenate([routes.astype(F32), first, second, rest - second], axis=1)
    meta = jnp.pad(meta, ((0, 0), (0, 128 - meta.shape[1]))).astype(BF16)
    message = jnp.concatenate([tokens, cotangent, meta], axis=1)

    plan = distances(experts)
    mine, packs, others, hot_in, hot_cot, turned, late = [], [], [], [], [], [], []
    returned = {}
    up, below, held = message, message, [message]
    for number, steps in enumerate(plan):
        if number + 1 < half:
            following = [shift(up, 1), shift(below, -1)]
        elif number + 1 == half:
            following = [shift(up[:, :width], 1), shift(below[:, width:], -1)]
        if 0 < number < half:
            held, late[number - 1] = lax.optimization_barrier((held, late[number - 1]))
        (rows, pack, hot_rows, hot_cots), back, turn = run_step(
            steps, fanout, capacity, scal, held, packs[0] if number == half else None, gate_up, down
        )
        following, back = lax.optimization_barrier((following, back))
        sent = [shift(part, step) if step else part for step, part in zip(steps, back)]
        late.append((sent, swap(pack)))
        mine.append(rows)
        packs.append(pack)
        hot_in.append(hot_rows)
        hot_cot.append(hot_cots)
        turned += turn
        held = following
        if number < half:
            up, below = following
    taken = 3 * units // experts
    ring_hot = to_ring(hottest, experts)
    is_hot = own == hottest

    def chunk(distance):
        owner = from_ring((ring_hot + distance + experts) % experts, experts)
        parts = [lax.dynamic_slice_in_dim(part, owner * taken, taken, axis=0) for part in turned]
        return jnp.concatenate(parts, axis=1)

    own_part = chunk(0)
    first_parts = [chunk(half), chunk(1 - half)]
    first_parts, late[half - 1] = lax.optimization_barrier((first_parts, late[half - 1]))
    around = [shift(first_parts[0], 1), shift(first_parts[1], -1)]
    for number in range(1, half):
        if number == 1:
            around, late[half] = lax.optimization_barrier((around, (late[half][0], late[half][1])))
            others = [other for _, other in late]
            expert_grad = expert_gradient(units, scal, mine, packs, others)
        if number == 2:
            around, expert_grad = lax.optimization_barrier((around, expert_grad))
        ahead = jnp.where(is_hot, chunk(half - number), around[0])
        if number < half - 1:
            behind = jnp.where(is_hot, chunk(number + 1 - half), around[1])
            around = [shift(ahead, 1), shift(behind, -1)]
        else:
            around = [shift(ahead, 1), around[1]]
    for steps, (sent, _) in zip(plan, late):
        for step, part in zip(steps, sent):
            returned[step % experts] = part
    token_grad = combine(experts, fanout, capacity, scal, meta, [returned[d] for d in range(experts)])
    around, token_grad = lax.optimization_barrier((around, token_grad))
    shadow_mine, shadow_theirs = shadow_gradient(
        plan, experts, capacity, scal, [own_part] + around, hot_in, hot_cot
    )
    shadow_grad = (shadow_mine + swap(shadow_theirs).astype(F32)).T
    return (token_grad, expert_grad, shadow_grad)


def solution(mesh):
    placed = (
        P(("group", "expert", "dp"), None),
        P(("group", "expert", "dp"), None),
        P(("group", "expert", "dp"), None),
        P(("group", "expert", "dp"), None),
        P(("group", "expert", "dp")),
        P(("group", "expert", "dp")),
        P("group"),
        P("expert", None, None),
        P("expert", None, None),
    )
    return jax.shard_map(
        on_device,
        mesh=mesh,
        in_specs=placed,
        out_specs=(
            P(("group", "expert", "dp"), None),
            P(("group", "expert"), "dp", None),
            P(("group", "dp"), "expert"),
        ),
        check_vma=False,
    )
```

```python
import functools

import jax
import jax.numpy as jnp
from jax import lax
from jax.experimental import pallas as pl
from jax.experimental.pallas import tpu as pltpu
from jax.sharding import PartitionSpec as P

BF16 = jnp.bfloat16
F32 = jnp.float32
VMEM_BYTES = 56 * 1024 * 1024


def snaked(experts):
    return experts <= 8


def to_ring(expert, experts):
    if not snaked(experts):
        return expert
    down = experts - 1 - (expert - 1) // 2
    return jnp.where(expert % 2 == 0, expert // 2, down)


def from_ring(place, experts):
    if not snaked(experts):
        return place
    return jnp.where(place < experts // 2, 2 * place, 2 * (experts - 1 - place) + 1)


def ring_order(experts):
    if not snaked(experts):
        return list(range(experts))
    return list(range(0, experts, 2)) + list(range(experts - 1, 0, -2))


def distances(experts):
    half = experts // 2
    return [[0]] + [[-step, step] for step in range(1, half)] + [[half]]


def slot_place(distance, experts):
    half = experts // 2
    near = jnp.where(distance < half, 2 * distance - 1, 2 * (experts - distance) - 2)
    near = jnp.where(distance == half, experts - 1, near)
    return jnp.where(distance == 0, experts - 2, near)


def dot(a, b, dims):
    return lax.dot_general(a, b, ((dims[:1], dims[1:]), ((), ())), preferred_element_type=F32)


def selection(table, expert, fanout, capacity):
    tokens = table.shape[1]
    hit = table[:fanout] == expert.astype(F32)
    named = jnp.sum(jnp.where(hit, 1.0, 0.0), axis=0, keepdims=True)
    parts = table[fanout : 4 * fanout]
    weights = parts[:fanout] + parts[fanout : 2 * fanout] + parts[2 * fanout :]
    weight = jnp.sum(jnp.where(hit, weights, 0.0), axis=0, keepdims=True)
    upto = lax.broadcasted_iota(jnp.int32, (tokens, tokens), 0) <= lax.broadcasted_iota(
        jnp.int32, (tokens, tokens), 1
    )
    upto = jnp.where(upto, 1.0, 0.0).astype(BF16)
    place = dot(jnp.broadcast_to(named, (8, tokens)).astype(BF16), upto, (1, 0))[:1]
    row = lax.broadcasted_iota(jnp.int32, (capacity, tokens), 0).astype(F32) + 1.0
    onehot = jnp.where((row == place) & (named > 0.5), 1.0, 0.0)
    return onehot, weight


def step_kernel(steps, fanout, capacity, joined, scal, *refs):
    count = len(steps)
    blocks, refs = refs[: max(count, 1 + joined)], refs[max(count, 1 + joined) :]
    if joined:
        first, refs = refs[0], refs[1:]
        blocks = [jnp.concatenate([block[...] for block in blocks], axis=1)]
    weights_gu, weights_down, mine, pack, hot_in, hot_cot = refs[:6]
    back, refs = refs[6 : 6 + count], refs[6 + count :]
    if len(refs) > 5:
        turned, refs = refs[0], refs[1:]
    else:
        turned = None
    rows_in, rows_cot, gate_up, down, sems = refs
    own, half, hottest = scal[0], scal[1], scal[2]
    units, width = down.shape
    load_gu = pltpu.make_async_copy(weights_gu, gate_up, sems.at[0])
    load_down = pltpu.make_async_copy(weights_down, down, sems.at[1])
    load_gu.start()
    load_down.start()
    for at, block in enumerate(blocks):
        rows = slice(at * capacity, (at + 1) * capacity)
        table = block[:, 2 * width :].astype(F32).T
        own_hot, own_weight = selection(table, own, fanout, capacity)
        all_hot, all_weight = selection(table, hottest, fanout, capacity)
        scale = jnp.concatenate(
            [
                jnp.sum(own_hot * own_weight, axis=1, keepdims=True),
                jnp.sum(all_hot * all_weight, axis=1, keepdims=True),
            ],
            axis=0,
        )
        onehot = jnp.concatenate([own_hot, all_hot], axis=0).astype(BF16)
        picked = dot(onehot, block[:, :width], (1, 0)).astype(BF16)
        rows_in[rows, :] = picked[:capacity]
        hot_in[rows, :] = picked[capacity:]
        picked = (scale * dot(onehot, block[:, width : 2 * width], (1, 0))).astype(BF16)
        rows_cot[rows, :] = picked[:capacity]
        hot_cot[rows, :] = picked[capacity:]
    part = width // 2
    here = pl.ds(pl.multiple_of(half * part, part), part)
    there = pl.ds(pl.multiple_of((1 - half) * part, part), part)
    mine[:, :part] = rows_in[:, here]
    mine[:, part:] = rows_cot[:, here]
    pack[:, :part] = rows_in[:, there]
    pack[:, part:width] = rows_cot[:, there]
    load_gu.wait()
    projected = dot(rows_in[...], gate_up[...], (1, 0))
    gate_pre, up_pre = projected[:, :units], projected[:, units:]
    load_down.wait()
    hidden_grad = dot(rows_cot[...], down[...], (1, 1))
    sigmoid_gate = jax.nn.sigmoid(gate_pre)
    activation = gate_pre * sigmoid_gate
    gate_grad = hidden_grad * up_pre * sigmoid_gate * (1.0 + gate_pre * (1.0 - sigmoid_gate))
    pack[:, width : width + units] = gate_grad.astype(BF16)
    pack[:, width + units : width + 2 * units] = (hidden_grad * activation).astype(BF16)
    pack[:, width + 2 * units :] = (activation * up_pre).astype(BF16)
    input_rows = dot(pack[:, width : width + 2 * units], gate_up[...], (1, 1)).astype(BF16)
    for at in range(count):
        back[at][...] = input_rows[at * capacity : (at + 1) * capacity]
    if turned is not None:
        grads = pack[:, width:]
        if joined:
            grads = jnp.concatenate([first[:, width:], grads], axis=0)
        turned[...] = grads.T


def run_step(steps, fanout, capacity, scal, blocks, first, gate_up, down):
    count, rows = len(steps), len(steps) * capacity
    units, width = down.shape
    vmem = pl.BlockSpec(memory_space=pltpu.VMEM)
    far = pl.BlockSpec(memory_space=pl.ANY)
    shapes = [(rows, width), (rows, width + 3 * units), (rows, width), (rows, width)]
    shapes += [(capacity, width)] * count
    joined = first is not None
    if joined or count > 1:
        shapes += [(3 * units, 2 * capacity)]
    firsts = [first] if joined else []
    out = pl.pallas_call(
        functools.partial(step_kernel, steps, fanout, capacity, joined),
        out_shape=[jax.ShapeDtypeStruct(shape, BF16) for shape in shapes],
        in_specs=[pl.BlockSpec(memory_space=pltpu.SMEM)] + [vmem] * (len(blocks) + len(firsts)) + [far] * 2,
        out_specs=[vmem] * len(shapes),
        scratch_shapes=[pltpu.VMEM((rows, width), BF16)] * 2
        + [
            pltpu.VMEM(gate_up.shape, BF16),
            pltpu.VMEM(down.shape, BF16),
            pltpu.SemaphoreType.DMA((2,)),
        ],
        compiler_params=pltpu.CompilerParams(vmem_limit_bytes=VMEM_BYTES),
        cost_estimate=pl.CostEstimate(
            flops=2 * 256 * 5 * width * units, bytes_accessed=3 * 2 * width * units, transcendentals=0
        ),
        name="expert_step",
    )(scal, *blocks, *firsts, gate_up, down)
    return out[:4], out[4 : 4 + count], out[4 + count :]


def combine_kernel(experts, fanout, capacity, scal, meta, *refs):
    rows, out = refs[:experts], refs[experts]
    place = to_ring(scal[0], experts)
    table = meta[...].astype(F32).T
    picks = []
    for step in range(experts):
        expert = from_ring((place - step + experts) % experts, experts)
        picks.append(selection(table, expert, fanout, capacity)[0])
    onehot = jnp.concatenate(picks, axis=0).astype(BF16)
    out[...] = dot(onehot, jnp.concatenate([part[...] for part in rows], axis=0), (0, 0)).astype(BF16)


def combine(experts, fanout, capacity, scal, meta, rows):
    vmem = pl.BlockSpec(memory_space=pltpu.VMEM)
    tokens, width = meta.shape[0], rows[0].shape[1]
    return pl.pallas_call(
        functools.partial(combine_kernel, experts, fanout, capacity),
        out_shape=jax.ShapeDtypeStruct((tokens, width), BF16),
        in_specs=[pl.BlockSpec(memory_space=pltpu.SMEM)] + [vmem] * (experts + 1),
        out_specs=vmem,
        compiler_params=pltpu.CompilerParams(vmem_limit_bytes=VMEM_BYTES),
        cost_estimate=pl.CostEstimate(
            flops=2 * experts * capacity * tokens * width, bytes_accessed=2 * experts * capacity * width, transcendentals=0
        ),
        name="token_sum",
    )(scal, meta, *rows)


def gradient_kernel(units, count, scal, *refs):
    ins, cots, packs = refs[: 2 * count], refs[2 * count : 4 * count], refs[4 * count : 6 * count]
    out = refs[6 * count]
    keep = scal[0] != scal[2]
    width = packs[0].shape[1] - 3 * units
    left = jnp.concatenate([ref[...] for ref in ins], axis=0)
    right = jnp.concatenate([ref[:, width : width + 2 * units] for ref in packs], axis=0)
    out[0, :, : 2 * units] = jnp.where(keep, dot(left, right, (0, 0)), 0.0)
    left = jnp.concatenate([ref[...] for ref in cots], axis=0)
    right = jnp.concatenate([ref[:, width + 2 * units :] for ref in packs], axis=0)
    out[0, :, 2 * units :] = jnp.where(keep, dot(left, right, (0, 0)), 0.0)


def expert_gradient(units, scal, mine, packs, others):
    width, columns, count = mine[0].shape[1], 3 * units, len(mine)
    tile = 256
    tiles = width // 2 // tile
    total = 2 * sum(part.shape[0] for part in mine)
    rows = mine + others
    in_specs = [pl.BlockSpec(memory_space=pltpu.SMEM)]
    in_specs += [pl.BlockSpec((part.shape[0], tile), lambda i: (0, i)) for part in rows]
    in_specs += [pl.BlockSpec((part.shape[0], tile), lambda i: (0, i + tiles)) for part in rows]
    in_specs += [pl.BlockSpec(part.shape, lambda i: (0, 0)) for part in packs + others]
    return pl.pallas_call(
        functools.partial(gradient_kernel, units, count),
        grid=(tiles,),
        out_shape=jax.ShapeDtypeStruct((1, width // 2, columns), F32),
        in_specs=in_specs,
        out_specs=pl.BlockSpec((1, tile, columns), lambda i: (0, i, 0)),
        compiler_params=pltpu.CompilerParams(vmem_limit_bytes=VMEM_BYTES),
        cost_estimate=pl.CostEstimate(
            flops=width * columns * total, bytes_accessed=3 * width * columns, transcendentals=0
        ),
        name="expert_gradient",
    )(scal, *rows, *rows, *packs, *others)


def order_kernel(plan, experts, capacity, scal, *refs):
    count = len(plan)
    shift = to_ring(scal[0], experts) - to_ring(scal[2], experts)
    for parts, out in ((refs[:count], refs[2 * count]), (refs[count : 2 * count], refs[2 * count + 1])):
        for steps, part in zip(plan, parts):
            for at, step in enumerate(steps):
                place = slot_place((shift + step + 2 * experts) % experts, experts)
                there = pl.ds(pl.multiple_of(place * capacity, capacity), capacity)
                out[there, :] = part[at * capacity : (at + 1) * capacity, :]


def ordered(plan, experts, capacity, scal, ins, cots):
    vmem = pl.BlockSpec(memory_space=pltpu.VMEM)
    rows, width = experts * capacity, ins[0].shape[1]
    return pl.pallas_call(
        functools.partial(order_kernel, plan, experts, capacity),
        out_shape=[jax.ShapeDtypeStruct((rows, width), BF16)] * 2,
        in_specs=[pl.BlockSpec(memory_space=pltpu.SMEM)] + [vmem] * (2 * len(ins)),
        out_specs=[vmem] * 2,
        compiler_params=pltpu.CompilerParams(vmem_limit_bytes=VMEM_BYTES),
        cost_estimate=pl.CostEstimate(flops=0, bytes_accessed=8 * rows * width, transcendentals=0),
        name="hot_rows_ordered",
    )(scal, *ins, *cots)


def shadow_kernel(experts, scal, kept, ahead, behind, rows_in, rows_cot, out, total):
    own = scal[0]
    away = (to_ring(own, experts) - to_ring(scal[2], experts) + experts) % experts
    taken, rows = kept.shape
    gates = taken * experts * 2 // 3
    column = own * taken + lax.broadcasted_iota(jnp.int32, kept.shape, 0)
    blank = jnp.zeros((), BF16)
    lane = lax.broadcasted_iota(jnp.int32, kept.shape, 1)
    reach = jnp.where(lane < rows // 2, experts // 2, experts // 2 - 1)
    received = jnp.where(away <= reach, ahead[...], behind[...])
    columns = jnp.where(away == 0, kept[...], received)

    @pl.when(own * taken < gates)
    def _():
        total[...] = dot(jnp.where(column < gates, columns, blank), rows_in[...], (1, 0))

    @pl.when(own * taken >= gates)
    def _():
        total[...] = jnp.zeros(total.shape, F32)

    @pl.when((own + 1) * taken > gates)
    def _():
        total[...] += dot(jnp.where(column < gates, blank, columns), rows_cot[...], (1, 0))

    out[...] = total[...].astype(out.dtype)


def shadow_gradient(experts, scal, columns, hot_in, hot_cot, kind):
    taken, rows = columns[0].shape
    width = hot_in.shape[1] // 2
    sends = kind == BF16
    whole = pl.BlockSpec((taken, rows), lambda i, scal: (0, 0))
    part = pl.BlockSpec((rows, width), lambda i, scal: (0, 1 - scal[1] if sends else scal[1]))
    return pl.pallas_call(
        functools.partial(shadow_kernel, experts),
        out_shape=jax.ShapeDtypeStruct((taken, width), kind),
        grid_spec=pltpu.PrefetchScalarGridSpec(
            num_scalar_prefetch=1,
            grid=(1,),
            in_specs=[whole] * 3 + [part] * 2,
            out_specs=pl.BlockSpec((taken, width), lambda i, scal: (0, 0)),
            scratch_shapes=[pltpu.VMEM((taken, width), F32)],
        ),
        compiler_params=pltpu.CompilerParams(vmem_limit_bytes=VMEM_BYTES),
        cost_estimate=pl.CostEstimate(
            flops=4 * taken * rows * width, bytes_accessed=4 * rows * width, transcendentals=0
        ),
        name="shadow_sent" if sends else "shadow_kept",
    )(scal, *columns, hot_in, hot_cot)


def on_device(
    tokens, cotangent, routes, route_weight, ratio_advantage, clip_mask, shadow_plan, gate_up, down
):
    experts = lax.axis_size("expert")
    tok_rows, width = tokens.shape
    fanout = routes.shape[1]
    units = down.shape[1]
    capacity = 2 * tok_rows * fanout // experts
    gate_up, down = gate_up[0], down[0]
    order = ring_order(experts)
    half = experts // 2

    def shift(block, step):
        pairs = [(order[i], order[(i + step) % experts]) for i in range(experts)]
        return lax.ppermute(block, "expert", pairs)

    def swap(block):
        return lax.ppermute(block, "dp", [(0, 1), (1, 0)])

    own = lax.axis_index("expert")
    hottest = shadow_plan[0]
    scal = jnp.stack([own, lax.axis_index("dp"), hottest]).astype(jnp.int32)
    slot_weight = route_weight * ratio_advantage[:, None] * clip_mask[:, None].astype(F32)
    first = lax.reduce_precision(slot_weight, 8, 7)
    rest = slot_weight - first
    second = lax.reduce_precision(rest, 8, 7)
    meta = jnp.concatenate([routes.astype(F32), first, second, rest - second], axis=1)
    meta = jnp.pad(meta, ((0, 0), (0, 128 - meta.shape[1]))).astype(BF16)
    message = jnp.concatenate([tokens, cotangent, meta], axis=1)

    plan = distances(experts)
    mine, packs, others, hot_in, hot_cot, turned, late = [], [], [], [], [], [], []
    returned = {}
    up, below, held = message, message, [message]
    for number, steps in enumerate(plan):
        if number + 1 < half:
            following = [shift(up, 1), shift(below, -1)]
        elif number + 1 == half:
            following = [shift(up[:, :width], 1), shift(below[:, width:], -1)]
        if number == half:
            held, late[half - 2] = lax.optimization_barrier((held, late[half - 2]))
        elif 0 < number < half - 1:
            held, late[number - 1] = lax.optimization_barrier((held, late[number - 1]))
        (rows, pack, hot_rows, hot_cots), back, turn = run_step(
            steps, fanout, capacity, scal, held, packs[0] if number == half else None, gate_up, down
        )
        following, back = lax.optimization_barrier((following, back))
        sent = [shift(part, step) if step else part for step, part in zip(steps, back)]
        late.append((sent, swap(pack)))
        mine.append(rows)
        packs.append(pack)
        hot_in.append(hot_rows)
        hot_cot.append(hot_cots)
        turned += turn
        held = following
        if number < half:
            up, below = following
    (back_behind, back_ahead), other = late[half - 1]
    turned[-1], back_ahead = lax.optimization_barrier((turned[-1], back_ahead))

    taken = 3 * units // experts
    ring_hot = to_ring(hottest, experts)
    is_hot = own == hottest

    def chunk(distance):
        owner = from_ring((ring_hot + distance + experts) % experts, experts)
        parts = [lax.dynamic_slice_in_dim(part, owner * taken, taken, axis=0) for part in turned]
        return jnp.concatenate(parts, axis=1)

    own_part, far = chunk(0), chunk(half)
    lanes = far.shape[1] // 2
    around = [far[:, :lanes], far[:, lanes:]]
    around, other = lax.optimization_barrier((around, other))
    around = [shift(around[0], 1), shift(around[1], -1)]
    others = [part for _, part in late[: half - 1]] + [other, late[half][1]]
    expert_grad = expert_gradient(units, scal, mine, packs, others)
    back_far = late[half][0]
    for number in range(1, half):
        if number == 1:
            around, expert_grad, back_behind = lax.optimization_barrier(
                (around, expert_grad, back_behind)
            )
            around = [jnp.concatenate([part, part], axis=1) for part in around]
        if number == 2:
            around, back_far = lax.optimization_barrier((around, back_far))
        ahead = jnp.where(is_hot, chunk(half - number), around[0])
        behind = jnp.where(is_hot, chunk(number - half), around[1])
        around = [shift(ahead, 1), shift(behind, -1)]
    sent = [rows for rows, _ in late[: half - 1]] + [[back_behind, back_ahead], back_far]
    for steps, parts in zip(plan, sent):
        for step, part in zip(steps, parts):
            returned[step % experts] = part
    hot_in, hot_cot = ordered(plan, experts, capacity, scal, hot_in, hot_cot)
    token_grad = combine(experts, fanout, capacity, scal, meta, [returned[d] for d in range(experts)])
    around, token_grad, hot_in, hot_cot = lax.optimization_barrier(
        (around, token_grad, hot_in, hot_cot)
    )
    columns = [own_part] + around
    theirs = swap(shadow_gradient(experts, scal, columns, hot_in, hot_cot, BF16))
    kept = shadow_gradient(experts, scal, columns, hot_in, hot_cot, F32)
    shadow_grad = (kept + theirs.astype(F32)).T
    return (token_grad, expert_grad, shadow_grad)


def solution(mesh):
    placed = (
        P(("group", "expert", "dp"), None),
        P(("group", "expert", "dp"), None),
        P(("group", "expert", "dp"), None),
        P(("group", "expert", "dp"), None),
        P(("group", "expert", "dp")),
        P(("group", "expert", "dp")),
        P("group"),
        P("expert", None, None),
        P("expert", None, None),
    )
    return jax.shard_map(
        on_device,
        mesh=mesh,
        in_specs=placed,
        out_specs=(
            P(("group", "expert", "dp"), None),
            P(("group", "expert"), "dp", None),
            P(("group", "dp"), "expert"),
        ),
        check_vma=False,
    )
```

```python
import functools

import jax
import jax.numpy as jnp
from jax import lax
from jax.experimental import pallas as pl
from jax.experimental.pallas import tpu as pltpu
from jax.sharding import PartitionSpec as P

BF16 = jnp.bfloat16
F32 = jnp.float32
VMEM_BYTES = 56 * 1024 * 1024


def snaked(experts):
    return experts <= 8


def to_ring(expert, experts):
    if not snaked(experts):
        return expert
    down = experts - 1 - (expert - 1) // 2
    return jnp.where(expert % 2 == 0, expert // 2, down)


def from_ring(place, experts):
    if not snaked(experts):
        return place
    return jnp.where(place < experts // 2, 2 * place, 2 * (experts - 1 - place) + 1)


def ring_order(experts):
    if not snaked(experts):
        return list(range(experts))
    return list(range(0, experts, 2)) + list(range(experts - 1, 0, -2))


def distances(experts):
    half = experts // 2
    return [[0]] + [[-step, step] for step in range(1, half)] + [[half]]


def slot_place(distance, experts):
    half = experts // 2
    near = jnp.where(distance < half, 2 * distance - 1, 2 * (experts - distance) - 2)
    near = jnp.where(distance == half, experts - 1, near)
    return jnp.where(distance == 0, experts - 2, near)


def dot(a, b, dims):
    return lax.dot_general(a, b, ((dims[:1], dims[1:]), ((), ())), preferred_element_type=F32)


def selection(table, expert, fanout, capacity):
    tokens = table.shape[1]
    hit = table[:fanout] == expert.astype(F32)
    named = jnp.sum(jnp.where(hit, 1.0, 0.0), axis=0, keepdims=True)
    parts = table[fanout : 4 * fanout]
    weights = parts[:fanout] + parts[fanout : 2 * fanout] + parts[2 * fanout :]
    weight = jnp.sum(jnp.where(hit, weights, 0.0), axis=0, keepdims=True)
    upto = lax.broadcasted_iota(jnp.int32, (tokens, tokens), 0) <= lax.broadcasted_iota(
        jnp.int32, (tokens, tokens), 1
    )
    upto = jnp.where(upto, 1.0, 0.0).astype(BF16)
    place = dot(jnp.broadcast_to(named, (8, tokens)).astype(BF16), upto, (1, 0))[:1]
    row = lax.broadcasted_iota(jnp.int32, (capacity, tokens), 0).astype(F32) + 1.0
    onehot = jnp.where((row == place) & (named > 0.5), 1.0, 0.0)
    return onehot, weight


def step_kernel(steps, fanout, capacity, joined, scal, *refs):
    count = len(steps)
    blocks, refs = refs[: max(count, 1 + joined)], refs[max(count, 1 + joined) :]
    if joined:
        first, refs = refs[0], refs[1:]
        blocks = [jnp.concatenate([block[...] for block in blocks], axis=1)]
    weights_gu, weights_down, mine, pack, hot = refs[:5]
    back, refs = refs[5 : 5 + count], refs[5 + count :]
    if len(refs) > 7:
        turned, refs = refs[0], refs[1:]
    else:
        turned = None
    rows_in, rows_cot, hot_in, hot_cot, gate_up, down, sems = refs
    own, half, hottest = scal[0], scal[1], scal[2]
    units, width = down.shape
    load_gu = pltpu.make_async_copy(weights_gu, gate_up, sems.at[0])
    load_down = pltpu.make_async_copy(weights_down, down, sems.at[1])
    load_gu.start()
    load_down.start()
    for at, block in enumerate(blocks):
        rows = slice(at * capacity, (at + 1) * capacity)
        table = block[:, 2 * width :].astype(F32).T
        own_hot, own_weight = selection(table, own, fanout, capacity)
        all_hot, all_weight = selection(table, hottest, fanout, capacity)
        scale = jnp.concatenate(
            [
                jnp.sum(own_hot * own_weight, axis=1, keepdims=True),
                jnp.sum(all_hot * all_weight, axis=1, keepdims=True),
            ],
            axis=0,
        )
        onehot = jnp.concatenate([own_hot, all_hot], axis=0).astype(BF16)
        picked = dot(onehot, block[:, :width], (1, 0)).astype(BF16)
        rows_in[rows, :] = picked[:capacity]
        hot_in[rows, :] = picked[capacity:]
        picked = (scale * dot(onehot, block[:, width : 2 * width], (1, 0))).astype(BF16)
        rows_cot[rows, :] = picked[:capacity]
        hot_cot[rows, :] = picked[capacity:]
    part = width // 2
    here = pl.ds(pl.multiple_of(half * part, part), part)
    there = pl.ds(pl.multiple_of((1 - half) * part, part), part)
    at = 3 * units
    for kept, rows_x, rows_c in ((mine, rows_in, rows_cot), (hot, hot_in, hot_cot)):
        kept[:, :part] = rows_x[:, here]
        kept[:, part:] = rows_c[:, here]
        pack[:, at : at + part] = rows_x[:, there]
        pack[:, at + part : at + width] = rows_c[:, there]
        at += width
    load_gu.wait()
    projected = dot(rows_in[...], gate_up[...], (1, 0))
    gate_pre, up_pre = projected[:, :units], projected[:, units:]
    load_down.wait()
    hidden_grad = dot(rows_cot[...], down[...], (1, 1))
    sigmoid_gate = jax.nn.sigmoid(gate_pre)
    activation = gate_pre * sigmoid_gate
    gate_grad = hidden_grad * up_pre * sigmoid_gate * (1.0 + gate_pre * (1.0 - sigmoid_gate))
    pack[:, :units] = gate_grad.astype(BF16)
    pack[:, units : 2 * units] = (hidden_grad * activation).astype(BF16)
    pack[:, 2 * units : 3 * units] = (activation * up_pre).astype(BF16)
    input_rows = dot(pack[:, : 2 * units], gate_up[...], (1, 1)).astype(BF16)
    for at in range(count):
        back[at][...] = input_rows[at * capacity : (at + 1) * capacity]
    if turned is not None:
        grads = pack[:, : 3 * units]
        if joined:
            grads = jnp.concatenate([first[:, : 3 * units], grads], axis=0)
        turned[...] = grads.T


def run_step(steps, fanout, capacity, scal, blocks, first, gate_up, down):
    count, rows = len(steps), len(steps) * capacity
    units, width = down.shape
    vmem = pl.BlockSpec(memory_space=pltpu.VMEM)
    far = pl.BlockSpec(memory_space=pl.ANY)
    shapes = [(rows, width), (rows, 3 * units + 2 * width), (rows, width)]
    shapes += [(capacity, width)] * count
    joined = first is not None
    if joined or count > 1:
        shapes += [(3 * units, 2 * capacity)]
    firsts = [first] if joined else []
    out = pl.pallas_call(
        functools.partial(step_kernel, steps, fanout, capacity, joined),
        out_shape=[jax.ShapeDtypeStruct(shape, BF16) for shape in shapes],
        in_specs=[pl.BlockSpec(memory_space=pltpu.SMEM)] + [vmem] * (len(blocks) + len(firsts)) + [far] * 2,
        out_specs=[vmem] * len(shapes),
        scratch_shapes=[pltpu.VMEM((rows, width), BF16)] * 4
        + [
            pltpu.VMEM(gate_up.shape, BF16),
            pltpu.VMEM(down.shape, BF16),
            pltpu.SemaphoreType.DMA((2,)),
        ],
        compiler_params=pltpu.CompilerParams(vmem_limit_bytes=VMEM_BYTES),
        cost_estimate=pl.CostEstimate(
            flops=2 * 256 * 5 * width * units, bytes_accessed=3 * 2 * width * units, transcendentals=0
        ),
        name="expert_step",
    )(scal, *blocks, *firsts, gate_up, down)
    return out[:3], out[3 : 3 + count], out[3 + count :]


def combine_kernel(experts, fanout, capacity, scal, meta, *refs):
    rows, out = refs[:experts], refs[experts]
    place = to_ring(scal[0], experts)
    table = meta[...].astype(F32).T
    picks = []
    for step in range(experts):
        expert = from_ring((place - step + experts) % experts, experts)
        picks.append(selection(table, expert, fanout, capacity)[0])
    onehot = jnp.concatenate(picks, axis=0).astype(BF16)
    out[...] = dot(onehot, jnp.concatenate([part[...] for part in rows], axis=0), (0, 0)).astype(BF16)


def combine(experts, fanout, capacity, scal, meta, rows):
    vmem = pl.BlockSpec(memory_space=pltpu.VMEM)
    tokens, width = meta.shape[0], rows[0].shape[1]
    return pl.pallas_call(
        functools.partial(combine_kernel, experts, fanout, capacity),
        out_shape=jax.ShapeDtypeStruct((tokens, width), BF16),
        in_specs=[pl.BlockSpec(memory_space=pltpu.SMEM)] + [vmem] * (experts + 1),
        out_specs=vmem,
        compiler_params=pltpu.CompilerParams(vmem_limit_bytes=VMEM_BYTES),
        cost_estimate=pl.CostEstimate(
            flops=2 * experts * capacity * tokens * width, bytes_accessed=2 * experts * capacity * width, transcendentals=0
        ),
        name="token_sum",
    )(scal, meta, *rows)


def gradient_kernel(units, count, scal, *refs):
    ins, cots, grads = refs[: 2 * count], refs[2 * count : 4 * count], refs[4 * count : 6 * count]
    out = refs[6 * count]
    keep = scal[0] != scal[2]
    left = jnp.concatenate([ref[...] for ref in ins], axis=0)
    right = jnp.concatenate([ref[:, : 2 * units] for ref in grads], axis=0)
    out[0, :, : 2 * units] = jnp.where(keep, dot(left, right, (0, 0)), 0.0)
    left = jnp.concatenate([ref[...] for ref in cots], axis=0)
    right = jnp.concatenate([ref[:, 2 * units :] for ref in grads], axis=0)
    out[0, :, 2 * units :] = jnp.where(keep, dot(left, right, (0, 0)), 0.0)


def expert_gradient(units, scal, mine, packs, others):
    width, columns, count = mine[0].shape[1], 3 * units, len(mine)
    tile = 256
    tiles, skip = width // 2 // tile, columns // tile
    total = 2 * sum(part.shape[0] for part in mine)
    rows = mine + others

    def tiled(first):
        specs = [pl.BlockSpec((part.shape[0], tile), lambda i: (0, i + first)) for part in mine]
        return specs + [
            pl.BlockSpec((part.shape[0], tile), lambda i: (0, i + first + skip)) for part in others
        ]

    in_specs = [pl.BlockSpec(memory_space=pltpu.SMEM)] + tiled(0) + tiled(tiles)
    in_specs += [pl.BlockSpec((part.shape[0], columns), lambda i: (0, 0)) for part in packs + others]
    return pl.pallas_call(
        functools.partial(gradient_kernel, units, count),
        grid=(tiles,),
        out_shape=jax.ShapeDtypeStruct((1, width // 2, columns), F32),
        in_specs=in_specs,
        out_specs=pl.BlockSpec((1, tile, columns), lambda i: (0, i, 0)),
        compiler_params=pltpu.CompilerParams(vmem_limit_bytes=VMEM_BYTES),
        cost_estimate=pl.CostEstimate(
            flops=width * columns * total, bytes_accessed=3 * width * columns, transcendentals=0
        ),
        name="expert_gradient",
    )(scal, *rows, *rows, *packs, *others)


def message_kernel(fanout, tokens, cotangent, routes, route_weight, ratio, clip, message, meta):
    count, width = tokens.shape
    message[:, :width] = tokens[...]
    message[:, width : 2 * width] = cotangent[...]
    weight = route_weight[...] * ratio[...] * clip[...].astype(F32)
    first = weight.astype(BF16).astype(F32)
    rest = weight - first
    second = rest.astype(BF16).astype(F32)
    lines = -(-4 * fanout // 8) * 8
    row = lax.broadcasted_iota(jnp.int32, (lines, count), 0)
    table = jnp.zeros((lines, count), F32)
    for number, part in enumerate([routes[...].astype(F32), first, second, rest - second]):
        for k in range(fanout):
            table = jnp.where(row == number * fanout + k, part[k : k + 1], table)
    table = jnp.concatenate([table, jnp.zeros((128 - lines, count), F32)], axis=0)
    columns = table.T.astype(BF16)
    message[:, 2 * width :] = columns
    meta[...] = columns


def build_message(tokens, cotangent, routes, route_weight, ratio, clip):
    count, width = tokens.shape
    vmem = pl.BlockSpec(memory_space=pltpu.VMEM)
    return pl.pallas_call(
        functools.partial(message_kernel, routes.shape[1]),
        out_shape=[
            jax.ShapeDtypeStruct((count, 2 * width + 128), BF16),
            jax.ShapeDtypeStruct((count, 128), BF16),
        ],
        in_specs=[vmem] * 6,
        out_specs=[vmem] * 2,
        cost_estimate=pl.CostEstimate(flops=0, bytes_accessed=8 * count * width, transcendentals=0),
        name="ring_message",
    )(tokens, cotangent, routes.T, route_weight.T, ratio[None], clip[None])


def order_kernel(plan, experts, capacity, scal, *refs):
    count = len(plan)
    mine, others, out, sems = refs[:count], refs[count : 2 * count], refs[-2], refs[-1]
    shift = to_ring(scal[0], experts) - to_ring(scal[2], experts)
    width = out.shape[1]
    copies = []
    for side, parts in enumerate((mine, others)):
        for steps, part in zip(plan, parts):
            columns = pl.ds(part.shape[1] - width, width)
            for at, step in enumerate(steps):
                place = slot_place((shift + step + 2 * experts) % experts, experts)
                there = pl.multiple_of((place + side * experts) * capacity, capacity)
                copies.append(
                    pltpu.make_async_copy(
                        part.at[pl.ds(at * capacity, capacity), columns],
                        out.at[pl.ds(there, capacity)],
                        sems.at[len(copies)],
                    )
                )
    for copy in copies:
        copy.start()
    for copy in copies:
        copy.wait()


def ordered(plan, experts, capacity, scal, mine, others):
    far = pl.BlockSpec(memory_space=pl.ANY)
    rows, width = 2 * experts * capacity, mine[0].shape[1]
    return pl.pallas_call(
        functools.partial(order_kernel, plan, experts, capacity),
        out_shape=jax.ShapeDtypeStruct((rows, width), BF16),
        in_specs=[pl.BlockSpec(memory_space=pltpu.SMEM)] + [far] * (2 * len(mine)),
        out_specs=far,
        scratch_shapes=[pltpu.SemaphoreType.DMA((2 * experts,))],
        cost_estimate=pl.CostEstimate(flops=0, bytes_accessed=4 * rows * width, transcendentals=0),
        name="hot_rows_ordered",
    )(scal, *mine, *others)


def shadow_kernel(experts, scal, mine, theirs, hot, out):
    own = scal[0]
    taken, rows = mine.shape
    width = out.shape[1]
    gates = taken * experts * 2 // 3
    column = own * taken + lax.broadcasted_iota(jnp.int32, (taken, 1), 0)

    def product(first):
        columns = pl.ds(first, width)
        return dot(mine[...], hot[:rows, columns], (1, 0)) + dot(theirs[...], hot[rows:, columns], (1, 0))

    @pl.when((own + 1) * taken <= gates)
    def _():
        out[...] = product(0)

    @pl.when(own * taken >= gates)
    def _():
        out[...] = product(width)

    @pl.when((own * taken < gates) & ((own + 1) * taken > gates))
    def _():
        out[...] = jnp.where(column < gates, product(0), product(width))


def shadow_gradient(experts, scal, mine, theirs, hot):
    taken, rows = mine.shape
    width = hot.shape[1] // 2
    vmem = pl.BlockSpec(memory_space=pltpu.VMEM)
    return pl.pallas_call(
        functools.partial(shadow_kernel, experts),
        out_shape=jax.ShapeDtypeStruct((taken, width), F32),
        in_specs=[pl.BlockSpec(memory_space=pltpu.SMEM)] + [vmem] * 3,
        out_specs=vmem,
        compiler_params=pltpu.CompilerParams(vmem_limit_bytes=24 * 1024 * 1024),
        cost_estimate=pl.CostEstimate(
            flops=4 * taken * rows * width, bytes_accessed=4 * rows * width, transcendentals=0
        ),
        name="shadow_gradient",
    )(scal, mine, theirs, hot)


def on_device(
    tokens, cotangent, routes, route_weight, ratio_advantage, clip_mask, shadow_plan, gate_up, down
):
    experts = lax.axis_size("expert")
    tok_rows, width = tokens.shape
    fanout = routes.shape[1]
    units = down.shape[1]
    capacity = 2 * tok_rows * fanout // experts
    gate_up, down = gate_up[0], down[0]
    order = ring_order(experts)
    half = experts // 2

    def shift(block, step):
        pairs = [(order[i], order[(i + step) % experts]) for i in range(experts)]
        return lax.ppermute(block, "expert", pairs)

    def swap(block):
        return lax.ppermute(block, "dp", [(0, 1), (1, 0)])

    own = lax.axis_index("expert")
    hottest = shadow_plan[0]
    scal = jnp.stack([own, lax.axis_index("dp"), hottest]).astype(jnp.int32)
    message, meta = build_message(
        tokens, cotangent, routes, route_weight, ratio_advantage, clip_mask
    )

    plan = distances(experts)
    mine, packs, hot, turned, late = [], [], [], [], []
    returned = {}
    up, below, held = message, message, [message]
    for number, steps in enumerate(plan):
        if number + 1 < half:
            following = [shift(up, 1), shift(below, -1)]
        elif number + 1 == half:
            following = [shift(up[:, :width], 1), shift(below[:, width:], -1)]
        if number == half:
            held, late[half - 2] = lax.optimization_barrier((held, late[half - 2]))
        elif 0 < number < half - 1:
            held, late[number - 1] = lax.optimization_barrier((held, late[number - 1]))
        (rows, pack, hot_rows), back, turn = run_step(
            steps, fanout, capacity, scal, held, packs[0] if number == half else None, gate_up, down
        )
        following, back = lax.optimization_barrier((following, back))
        if number < half:
            sent = [shift(part, step) if step else part for step, part in zip(steps, back)]
        else:
            sent = back
        late.append((sent, swap(pack)))
        mine.append(rows)
        packs.append(pack)
        hot.append(hot_rows)
        turned += turn
        held = following
        if number < half:
            up, below = following
    (back_behind, back_ahead), other = late[half - 1]
    turned[-1], back_ahead = lax.optimization_barrier((turned[-1], back_ahead))

    taken = 3 * units // experts
    ring_hot = to_ring(hottest, experts)
    is_hot = own == hottest

    def chunk(distance):
        owner = from_ring((ring_hot + distance + experts) % experts, experts)
        parts = [lax.dynamic_slice_in_dim(part, owner * taken, taken, axis=0) for part in turned]
        return jnp.concatenate(parts, axis=1)

    far = chunk(half)
    lanes = far.shape[1] // 2
    around = [far[:, :lanes], far[:, lanes:]]
    around, other = lax.optimization_barrier((around, other))
    around = [shift(around[0], 1), shift(around[1], -1)]
    others = [part for _, part in late[: half - 1]] + [other, late[half][1]]
    expert_grad = expert_gradient(units, scal, mine, packs, others)
    chunks = [chunk(distance) for distance in range(1 - half, half)]
    (back_far,) = late[half][0]
    for number in range(1, half):
        if number == 1:
            around, expert_grad, back_behind, chunks = lax.optimization_barrier(
                (around, expert_grad, back_behind, chunks)
            )
            around = [jnp.concatenate([part, part], axis=1) for part in around]
        if number == half - 1:
            around, back_far = lax.optimization_barrier((around, back_far))
        ahead = jnp.where(is_hot, chunks[2 * half - 1 - number], around[0])
        behind = jnp.where(is_hot, chunks[number - 1], around[1])
        around = [shift(ahead, 1), shift(behind, -1)]
    back_far = shift(back_far, half)
    hot_rows = ordered(plan, experts, capacity, scal, hot, others)
    around, hot_rows = lax.optimization_barrier((around, hot_rows))
    away = (to_ring(own, experts) - ring_hot + experts) % experts
    lane = lax.broadcasted_iota(jnp.int32, far.shape, 1)
    reach = jnp.where(lane < lanes, half, half - 1)
    columns = jnp.where(
        away == 0, chunks[half - 1], jnp.where(away <= reach, around[0], around[1])
    )
    shadow_grad = shadow_gradient(experts, scal, columns, swap(columns), hot_rows).T
    sent = [rows for rows, _ in late[: half - 1]] + [[back_behind, back_ahead], [back_far]]
    for steps, parts in zip(plan, sent):
        for step, part in zip(steps, parts):
            returned[step % experts] = part
    token_grad = combine(experts, fanout, capacity, scal, meta, [returned[d] for d in range(experts)])
    return (token_grad, expert_grad, shadow_grad)


def solution(mesh):
    placed = (
        P(("group", "expert", "dp"), None),
        P(("group", "expert", "dp"), None),
        P(("group", "expert", "dp"), None),
        P(("group", "expert", "dp"), None),
        P(("group", "expert", "dp")),
        P(("group", "expert", "dp")),
        P("group"),
        P("expert", None, None),
        P("expert", None, None),
    )
    return jax.shard_map(
        on_device,
        mesh=mesh,
        in_specs=placed,
        out_specs=(
            P(("group", "expert", "dp"), None),
            P(("group", "expert"), "dp", None),
            P(("group", "dp"), "expert"),
        ),
        check_vma=False,
    )
```

```python
import functools

import jax
import jax.numpy as jnp
from jax import lax
from jax.experimental import pallas as pl
from jax.experimental.pallas import tpu as pltpu
from jax.sharding import PartitionSpec as P

BF16 = jnp.bfloat16
F32 = jnp.float32
VMEM_BYTES = 56 * 1024 * 1024


def snaked(experts):
    return experts <= 8


def to_ring(expert, experts):
    if not snaked(experts):
        return expert
    down = experts - 1 - (expert - 1) // 2
    return jnp.where(expert % 2 == 0, expert // 2, down)


def from_ring(place, experts):
    if not snaked(experts):
        return place
    return jnp.where(place < experts // 2, 2 * place, 2 * (experts - 1 - place) + 1)


def ring_order(experts):
    if not snaked(experts):
        return list(range(experts))
    return list(range(0, experts, 2)) + list(range(experts - 1, 0, -2))


def distances(experts):
    half = experts // 2
    return [[0]] + [[-step, step] for step in range(1, half)] + [[half]]


def slot_place(distance, experts):
    half = experts // 2
    near = jnp.where(distance < half, 2 * distance - 1, 2 * (experts - distance) - 2)
    near = jnp.where(distance == half, experts - 1, near)
    return jnp.where(distance == 0, experts - 2, near)


def dot(a, b, dims):
    return lax.dot_general(a, b, ((dims[:1], dims[1:]), ((), ())), preferred_element_type=F32)


def selection(table, expert, fanout, capacity):
    tokens = table.shape[1]
    hit = table[:fanout] == expert.astype(F32)
    named = jnp.sum(jnp.where(hit, 1.0, 0.0), axis=0, keepdims=True)
    parts = table[fanout : 4 * fanout]
    weights = parts[:fanout] + parts[fanout : 2 * fanout] + parts[2 * fanout :]
    weight = jnp.sum(jnp.where(hit, weights, 0.0), axis=0, keepdims=True)
    upto = lax.broadcasted_iota(jnp.int32, (tokens, tokens), 0) <= lax.broadcasted_iota(
        jnp.int32, (tokens, tokens), 1
    )
    upto = jnp.where(upto, 1.0, 0.0).astype(BF16)
    place = dot(jnp.broadcast_to(named, (8, tokens)).astype(BF16), upto, (1, 0))[:1]
    row = lax.broadcasted_iota(jnp.int32, (capacity, tokens), 0).astype(F32) + 1.0
    onehot = jnp.where((row == place) & (named > 0.5), 1.0, 0.0)
    return onehot, weight


def step_kernel(steps, fanout, capacity, joined, scal, *refs):
    count = len(steps)
    blocks, refs = refs[: max(count, 1 + joined)], refs[max(count, 1 + joined) :]
    if joined:
        first, refs = refs[0], refs[1:]
        blocks = [jnp.concatenate([block[...] for block in blocks], axis=1)]
    weights_gu, weights_down, mine, pack, hot = refs[:5]
    back, refs = refs[5 : 5 + count], refs[5 + count :]
    if len(refs) > 7:
        turned, refs = refs[0], refs[1:]
    else:
        turned = None
    rows_in, rows_cot, hot_in, hot_cot, gate_up, down, sems = refs
    own, half, hottest = scal[0], scal[1], scal[2]
    units, width = down.shape
    load_gu = pltpu.make_async_copy(weights_gu, gate_up, sems.at[0])
    load_down = pltpu.make_async_copy(weights_down, down, sems.at[1])
    load_gu.start()
    load_down.start()
    for at, block in enumerate(blocks):
        rows = slice(at * capacity, (at + 1) * capacity)
        table = block[:, 2 * width :].astype(F32).T
        own_hot, own_weight = selection(table, own, fanout, capacity)
        all_hot, all_weight = selection(table, hottest, fanout, capacity)
        scale = jnp.concatenate(
            [
                jnp.sum(own_hot * own_weight, axis=1, keepdims=True),
                jnp.sum(all_hot * all_weight, axis=1, keepdims=True),
            ],
            axis=0,
        )
        onehot = jnp.concatenate([own_hot, all_hot], axis=0).astype(BF16)
        picked = dot(onehot, block[:, :width], (1, 0)).astype(BF16)
        rows_in[rows, :] = picked[:capacity]
        hot_in[rows, :] = picked[capacity:]
        picked = (scale * dot(onehot, block[:, width : 2 * width], (1, 0))).astype(BF16)
        rows_cot[rows, :] = picked[:capacity]
        hot_cot[rows, :] = picked[capacity:]
    part = width // 2
    here = pl.ds(pl.multiple_of(half * part, part), part)
    there = pl.ds(pl.multiple_of((1 - half) * part, part), part)
    mine[:, :part] = rows_in[:, here]
    mine[:, part:] = rows_cot[:, here]
    pack[:, 3 * units : 3 * units + part] = rows_in[:, there]
    pack[:, 3 * units + part :] = rows_cot[:, there]
    hot[:, :part] = hot_in[:, here]
    hot[:, part:width] = hot_cot[:, here]
    hot[:, width : width + part] = hot_in[:, there]
    hot[:, width + part :] = hot_cot[:, there]
    load_gu.wait()
    projected = dot(rows_in[...], gate_up[...], (1, 0))
    gate_pre, up_pre = projected[:, :units], projected[:, units:]
    load_down.wait()
    hidden_grad = dot(rows_cot[...], down[...], (1, 1))
    sigmoid_gate = jax.nn.sigmoid(gate_pre)
    activation = gate_pre * sigmoid_gate
    gate_grad = hidden_grad * up_pre * sigmoid_gate * (1.0 + gate_pre * (1.0 - sigmoid_gate))
    pack[:, :units] = gate_grad.astype(BF16)
    pack[:, units : 2 * units] = (hidden_grad * activation).astype(BF16)
    pack[:, 2 * units : 3 * units] = (activation * up_pre).astype(BF16)
    input_rows = dot(pack[:, : 2 * units], gate_up[...], (1, 1)).astype(BF16)
    for at in range(count):
        back[at][...] = input_rows[at * capacity : (at + 1) * capacity]
    if turned is not None:
        grads = pack[:, : 3 * units]
        if joined:
            grads = jnp.concatenate([first[:, : 3 * units], grads], axis=0)
        turned[...] = grads.T


def run_step(steps, fanout, capacity, scal, blocks, first, gate_up, down):
    count, rows = len(steps), len(steps) * capacity
    units, width = down.shape
    vmem = pl.BlockSpec(memory_space=pltpu.VMEM)
    far = pl.BlockSpec(memory_space=pl.ANY)
    shapes = [(rows, width), (rows, 3 * units + width), (rows, 2 * width)]
    shapes += [(capacity, width)] * count
    joined = first is not None
    if joined or count > 1:
        shapes += [(3 * units, 2 * capacity)]
    firsts = [first] if joined else []
    out = pl.pallas_call(
        functools.partial(step_kernel, steps, fanout, capacity, joined),
        out_shape=[jax.ShapeDtypeStruct(shape, BF16) for shape in shapes],
        in_specs=[pl.BlockSpec(memory_space=pltpu.SMEM)] + [vmem] * (len(blocks) + len(firsts)) + [far] * 2,
        out_specs=[vmem] * len(shapes),
        scratch_shapes=[pltpu.VMEM((rows, width), BF16)] * 4
        + [
            pltpu.VMEM(gate_up.shape, BF16),
            pltpu.VMEM(down.shape, BF16),
            pltpu.SemaphoreType.DMA((2,)),
        ],
        compiler_params=pltpu.CompilerParams(vmem_limit_bytes=VMEM_BYTES),
        cost_estimate=pl.CostEstimate(
            flops=2 * 256 * 5 * width * units, bytes_accessed=3 * 2 * width * units, transcendentals=0
        ),
        name="expert_step",
    )(scal, *blocks, *firsts, gate_up, down)
    return out[:3], out[3 : 3 + count], out[3 + count :]


def combine_kernel(experts, fanout, capacity, scal, meta, *refs):
    rows, out = refs[:experts], refs[experts]
    place = to_ring(scal[0], experts)
    table = meta[...].astype(F32).T
    picks = []
    for step in range(experts):
        expert = from_ring((place - step + experts) % experts, experts)
        picks.append(selection(table, expert, fanout, capacity)[0])
    onehot = jnp.concatenate(picks, axis=0).astype(BF16)
    out[...] = dot(onehot, jnp.concatenate([part[...] for part in rows], axis=0), (0, 0)).astype(BF16)


def combine(experts, fanout, capacity, scal, meta, rows):
    vmem = pl.BlockSpec(memory_space=pltpu.VMEM)
    tokens, width = meta.shape[0], rows[0].shape[1]
    return pl.pallas_call(
        functools.partial(combine_kernel, experts, fanout, capacity),
        out_shape=jax.ShapeDtypeStruct((tokens, width), BF16),
        in_specs=[pl.BlockSpec(memory_space=pltpu.SMEM)] + [vmem] * (experts + 1),
        out_specs=vmem,
        compiler_params=pltpu.CompilerParams(vmem_limit_bytes=VMEM_BYTES),
        cost_estimate=pl.CostEstimate(
            flops=2 * experts * capacity * tokens * width, bytes_accessed=2 * experts * capacity * width, transcendentals=0
        ),
        name="token_sum",
    )(scal, meta, *rows)


def gradient_kernel(units, count, scal, *refs):
    ins, cots, grads = refs[: 2 * count], refs[2 * count : 4 * count], refs[4 * count : 6 * count]
    out = refs[6 * count]
    keep = scal[0] != scal[2]
    left = jnp.concatenate([ref[...] for ref in ins], axis=0)
    right = jnp.concatenate([ref[:, : 2 * units] for ref in grads], axis=0)
    out[0, :, : 2 * units] = jnp.where(keep, dot(left, right, (0, 0)), 0.0)
    left = jnp.concatenate([ref[...] for ref in cots], axis=0)
    right = jnp.concatenate([ref[:, 2 * units :] for ref in grads], axis=0)
    out[0, :, 2 * units :] = jnp.where(keep, dot(left, right, (0, 0)), 0.0)


def expert_gradient(units, scal, mine, packs, others):
    width, columns, count = mine[0].shape[1], 3 * units, len(mine)
    tile = 256
    tiles, skip = width // 2 // tile, columns // tile
    total = 2 * sum(part.shape[0] for part in mine)
    rows = mine + others

    def tiled(first):
        specs = [pl.BlockSpec((part.shape[0], tile), lambda i: (0, i + first)) for part in mine]
        return specs + [
            pl.BlockSpec((part.shape[0], tile), lambda i: (0, i + first + skip)) for part in others
        ]

    in_specs = [pl.BlockSpec(memory_space=pltpu.SMEM)] + tiled(0) + tiled(tiles)
    in_specs += [pl.BlockSpec((part.shape[0], columns), lambda i: (0, 0)) for part in packs + others]
    return pl.pallas_call(
        functools.partial(gradient_kernel, units, count),
        grid=(tiles,),
        out_shape=jax.ShapeDtypeStruct((1, width // 2, columns), F32),
        in_specs=in_specs,
        out_specs=pl.BlockSpec((1, tile, columns), lambda i: (0, i, 0)),
        compiler_params=pltpu.CompilerParams(vmem_limit_bytes=VMEM_BYTES),
        cost_estimate=pl.CostEstimate(
            flops=width * columns * total, bytes_accessed=3 * width * columns, transcendentals=0
        ),
        name="expert_gradient",
    )(scal, *rows, *rows, *packs, *others)


def message_kernel(fanout, tokens, cotangent, routes, route_weight, ratio, clip, message, meta):
    count, width = tokens.shape
    message[:, :width] = tokens[...]
    message[:, width : 2 * width] = cotangent[...]
    weight = route_weight[...] * ratio[...] * clip[...].astype(F32)
    first = weight.astype(BF16).astype(F32)
    rest = weight - first
    second = rest.astype(BF16).astype(F32)
    lines = -(-4 * fanout // 8) * 8
    row = lax.broadcasted_iota(jnp.int32, (lines, count), 0)
    table = jnp.zeros((lines, count), F32)
    for number, part in enumerate([routes[...].astype(F32), first, second, rest - second]):
        for k in range(fanout):
            table = jnp.where(row == number * fanout + k, part[k : k + 1], table)
    table = jnp.concatenate([table, jnp.zeros((128 - lines, count), F32)], axis=0)
    columns = table.T.astype(BF16)
    message[:, 2 * width :] = columns
    meta[...] = columns


def build_message(tokens, cotangent, routes, route_weight, ratio, clip):
    count, width = tokens.shape
    vmem = pl.BlockSpec(memory_space=pltpu.VMEM)
    return pl.pallas_call(
        functools.partial(message_kernel, routes.shape[1]),
        out_shape=[
            jax.ShapeDtypeStruct((count, 2 * width + 128), BF16),
            jax.ShapeDtypeStruct((count, 128), BF16),
        ],
        in_specs=[vmem] * 6,
        out_specs=[vmem] * 2,
        cost_estimate=pl.CostEstimate(flops=0, bytes_accessed=8 * count * width, transcendentals=0),
        name="ring_message",
    )(tokens, cotangent, routes.T, route_weight.T, ratio[None], clip[None])


def order_kernel(plan, experts, capacity, scal, *refs):
    parts, mine, theirs = refs[:-2], refs[-2], refs[-1]
    shift = to_ring(scal[0], experts) - to_ring(scal[2], experts)
    width = mine.shape[1]
    for steps, part in zip(plan, parts):
        for at, step in enumerate(steps):
            place = slot_place((shift + step + 2 * experts) % experts, experts)
            there = pl.ds(pl.multiple_of(place * capacity, capacity), capacity)
            mine[there, :] = part[at * capacity : (at + 1) * capacity, :width]
            theirs[there, :] = part[at * capacity : (at + 1) * capacity, width:]


def ordered(plan, experts, capacity, scal, parts):
    vmem = pl.BlockSpec(memory_space=pltpu.VMEM)
    rows, width = experts * capacity, parts[0].shape[1] // 2
    return pl.pallas_call(
        functools.partial(order_kernel, plan, experts, capacity),
        out_shape=[jax.ShapeDtypeStruct((rows, width), BF16)] * 2,
        in_specs=[pl.BlockSpec(memory_space=pltpu.SMEM)] + [vmem] * len(parts),
        out_specs=[vmem] * 2,
        compiler_params=pltpu.CompilerParams(vmem_limit_bytes=VMEM_BYTES),
        cost_estimate=pl.CostEstimate(flops=0, bytes_accessed=8 * rows * width, transcendentals=0),
        name="hot_rows_ordered",
    )(scal, *parts)


def shadow_kernel(experts, scal, mine, theirs, hot_mine, hot_theirs, out):
    own = scal[0]
    taken = mine.shape[0]
    width = out.shape[1]
    gates = taken * experts * 2 // 3
    column = own * taken + lax.broadcasted_iota(jnp.int32, (taken, 1), 0)

    def product(first):
        columns = pl.ds(first, width)
        return dot(mine[...], hot_mine[:, columns], (1, 0)) + dot(theirs[...], hot_theirs[:, columns], (1, 0))

    @pl.when((own + 1) * taken <= gates)
    def _():
        out[...] = product(0)

    @pl.when(own * taken >= gates)
    def _():
        out[...] = product(width)

    @pl.when((own * taken < gates) & ((own + 1) * taken > gates))
    def _():
        out[...] = jnp.where(column < gates, product(0), product(width))


def shadow_gradient(experts, scal, mine, theirs, hot_mine, hot_theirs):
    taken, rows = mine.shape
    width = hot_mine.shape[1] // 2
    vmem = pl.BlockSpec(memory_space=pltpu.VMEM)
    return pl.pallas_call(
        functools.partial(shadow_kernel, experts),
        out_shape=jax.ShapeDtypeStruct((taken, width), F32),
        in_specs=[pl.BlockSpec(memory_space=pltpu.SMEM)] + [vmem] * 4,
        out_specs=vmem,
        compiler_params=pltpu.CompilerParams(vmem_limit_bytes=24 * 1024 * 1024),
        cost_estimate=pl.CostEstimate(
            flops=4 * taken * rows * width, bytes_accessed=4 * rows * width, transcendentals=0
        ),
        name="shadow_gradient",
    )(scal, mine, theirs, hot_mine, hot_theirs)


def on_device(
    tokens, cotangent, routes, route_weight, ratio_advantage, clip_mask, shadow_plan, gate_up, down
):
    experts = lax.axis_size("expert")
    tok_rows, width = tokens.shape
    fanout = routes.shape[1]
    units = down.shape[1]
    capacity = 2 * tok_rows * fanout // experts
    gate_up, down = gate_up[0], down[0]
    order = ring_order(experts)
    half = experts // 2

    def shift(block, step):
        pairs = [(order[i], order[(i + step) % experts]) for i in range(experts)]
        return lax.ppermute(block, "expert", pairs)

    def swap(block):
        return lax.ppermute(block, "dp", [(0, 1), (1, 0)])

    own = lax.axis_index("expert")
    hottest = shadow_plan[0]
    scal = jnp.stack([own, lax.axis_index("dp"), hottest]).astype(jnp.int32)
    message, meta = build_message(
        tokens, cotangent, routes, route_weight, ratio_advantage, clip_mask
    )

    plan = distances(experts)
    mine, packs, hot, turned, late = [], [], [], [], []
    returned = {}
    up, below, held = message, message, [message]
    for number, steps in enumerate(plan):
        if number + 1 < half:
            following = [shift(up, 1), shift(below, -1)]
        elif number + 1 == half:
            following = [shift(up[:, :width], 1), shift(below[:, width:], -1)]
        if number == half:
            held, late[half - 2] = lax.optimization_barrier((held, late[half - 2]))
        elif 0 < number < half - 1:
            held, late[number - 1] = lax.optimization_barrier((held, late[number - 1]))
        (rows, pack, hot_rows), back, turn = run_step(
            steps,
            fanout,
            capacity,
            scal,
            held,
            packs[0] if number == half else None,
            gate_up,
            down,
        )
        following, back = lax.optimization_barrier((following, back))
        sent = [shift(part, step) if step else part for step, part in zip(steps, back)]
        late.append((sent, swap(pack)))
        mine.append(rows)
        packs.append(pack)
        hot.append(hot_rows)
        turned += turn
        held = following
        if number < half:
            up, below = following
    (back_behind, back_ahead), other = late[half - 1]
    turned[-1], back_ahead = lax.optimization_barrier((turned[-1], back_ahead))

    taken = 3 * units // experts
    ring_hot = to_ring(hottest, experts)
    is_hot = own == hottest

    def chunk(distance):
        owner = from_ring((ring_hot + distance + experts) % experts, experts)
        parts = [lax.dynamic_slice_in_dim(part, owner * taken, taken, axis=0) for part in turned]
        return jnp.concatenate(parts, axis=1)

    far = chunk(half)
    lanes = far.shape[1] // 2
    around = [far[:, :lanes], far[:, lanes:]]
    around, other = lax.optimization_barrier((around, other))
    around = [shift(around[0], 1), shift(around[1], -1)]
    others = [part for _, part in late[: half - 1]] + [other, late[half][1]]
    expert_grad = expert_gradient(units, scal, mine, packs, others)
    chunks = [chunk(distance) for distance in range(1 - half, half)]
    (back_far,) = late[half][0]
    hot_mine, hot_theirs = ordered(plan, experts, capacity, scal, hot)
    for number in range(1, half):
        if number == 1:
            around, expert_grad, back_behind, chunks = lax.optimization_barrier(
                (around, expert_grad, back_behind, chunks)
            )
            around = [jnp.concatenate([part, part], axis=1) for part in around]
        if number == 2:
            around, back_far = lax.optimization_barrier((around, back_far))
        if number == half - 1:
            around, hot_mine, hot_theirs = lax.optimization_barrier((around, hot_mine, hot_theirs))
        ahead = jnp.where(is_hot, chunks[2 * half - 1 - number], around[0])
        behind = jnp.where(is_hot, chunks[number - 1], around[1])
        around = [shift(ahead, 1), shift(behind, -1)]
    hot_theirs = swap(hot_theirs)
    away = (to_ring(own, experts) - ring_hot + experts) % experts
    lane = lax.broadcasted_iota(jnp.int32, far.shape, 1)
    reach = jnp.where(lane < lanes, half, half - 1)
    columns = jnp.where(
        away == 0, chunks[half - 1], jnp.where(away <= reach, around[0], around[1])
    )
    shadow_grad = shadow_gradient(
        experts, scal, columns, swap(columns), hot_mine, hot_theirs
    ).T
    sent = [rows for rows, _ in late[: half - 1]] + [[back_behind, back_ahead], [back_far]]
    for steps, parts in zip(plan, sent):
        for step, part in zip(steps, parts):
            returned[step % experts] = part
    token_grad = combine(experts, fanout, capacity, scal, meta, [returned[d] for d in range(experts)])
    return (token_grad, expert_grad, shadow_grad)


def solution(mesh):
    placed = (
        P(("group", "expert", "dp"), None),
        P(("group", "expert", "dp"), None),
        P(("group", "expert", "dp"), None),
        P(("group", "expert", "dp"), None),
        P(("group", "expert", "dp")),
        P(("group", "expert", "dp")),
        P("group"),
        P("expert", None, None),
        P("expert", None, None),
    )
    return jax.shard_map(
        on_device,
        mesh=mesh,
        in_specs=placed,
        out_specs=(
            P(("group", "expert", "dp"), None),
            P(("group", "expert"), "dp", None),
            P(("group", "dp"), "expert"),
        ),
        check_vma=False,
    )
```

```python
import functools

import jax
import jax.numpy as jnp
from jax import lax
from jax.experimental import pallas as pl
from jax.experimental.pallas import tpu as pltpu
from jax.sharding import PartitionSpec as P

BF16 = jnp.bfloat16
F32 = jnp.float32
VMEM_BYTES = 56 * 1024 * 1024


def snaked(experts):
    return experts <= 8


def to_ring(expert, experts):
    if not snaked(experts):
        return expert
    down = experts - 1 - (expert - 1) // 2
    return jnp.where(expert % 2 == 0, expert // 2, down)


def from_ring(place, experts):
    if not snaked(experts):
        return place
    return jnp.where(place < experts // 2, 2 * place, 2 * (experts - 1 - place) + 1)


def ring_order(experts):
    if not snaked(experts):
        return list(range(experts))
    return list(range(0, experts, 2)) + list(range(experts - 1, 0, -2))


def distances(experts):
    half = experts // 2
    return [[0]] + [[-step, step] for step in range(1, half)] + [[half]]


def slot_place(distance, experts):
    half = experts // 2
    near = jnp.where(distance < half, 2 * distance - 1, 2 * (experts - distance) - 2)
    near = jnp.where(distance == half, experts - 1, near)
    return jnp.where(distance == 0, experts - 2, near)


def dot(a, b, dims):
    return lax.dot_general(a, b, ((dims[:1], dims[1:]), ((), ())), preferred_element_type=F32)


def selection(table, expert, fanout, capacity):
    tokens = table.shape[1]
    hit = table[:fanout] == expert.astype(F32)
    named = jnp.sum(jnp.where(hit, 1.0, 0.0), axis=0, keepdims=True)
    parts = table[fanout : 4 * fanout]
    weights = parts[:fanout] + parts[fanout : 2 * fanout] + parts[2 * fanout :]
    weight = jnp.sum(jnp.where(hit, weights, 0.0), axis=0, keepdims=True)
    upto = lax.broadcasted_iota(jnp.int32, (tokens, tokens), 0) <= lax.broadcasted_iota(
        jnp.int32, (tokens, tokens), 1
    )
    upto = jnp.where(upto, 1.0, 0.0).astype(BF16)
    place = dot(jnp.broadcast_to(named, (8, tokens)).astype(BF16), upto, (1, 0))[:1]
    row = lax.broadcasted_iota(jnp.int32, (capacity, tokens), 0).astype(F32) + 1.0
    onehot = jnp.where((row == place) & (named > 0.5), 1.0, 0.0)
    return onehot, weight


def step_kernel(steps, pieces, fanout, capacity, joined, scal, *refs):
    count = len(steps)
    blocks, refs = refs[: max(count, 1 + joined)], refs[max(count, 1 + joined) :]
    if joined:
        first, refs = refs[0], refs[1:]
        blocks = [jnp.concatenate([block[...] for block in blocks], axis=1)]
    weights_gu, weights_down, mine, pack, hot = refs[:5]
    back, refs = refs[5 : 5 + count * pieces], refs[5 + count * pieces :]
    if len(refs) > 7:
        turned, refs = refs[0], refs[1:]
    else:
        turned = None
    rows_in, rows_cot, hot_in, hot_cot, gate_up, down, sems = refs
    own, half, hottest = scal[0], scal[1], scal[2]
    units, width = down.shape
    load_gu = pltpu.make_async_copy(weights_gu, gate_up, sems.at[0])
    load_down = pltpu.make_async_copy(weights_down, down, sems.at[1])
    load_gu.start()
    load_down.start()
    for at, block in enumerate(blocks):
        rows = slice(at * capacity, (at + 1) * capacity)
        table = block[:, 2 * width :].astype(F32).T
        own_hot, own_weight = selection(table, own, fanout, capacity)
        all_hot, all_weight = selection(table, hottest, fanout, capacity)
        scale = jnp.concatenate(
            [
                jnp.sum(own_hot * own_weight, axis=1, keepdims=True),
                jnp.sum(all_hot * all_weight, axis=1, keepdims=True),
            ],
            axis=0,
        )
        onehot = jnp.concatenate([own_hot, all_hot], axis=0).astype(BF16)
        picked = dot(onehot, block[:, :width], (1, 0)).astype(BF16)
        rows_in[rows, :] = picked[:capacity]
        hot_in[rows, :] = picked[capacity:]
        picked = (scale * dot(onehot, block[:, width : 2 * width], (1, 0))).astype(BF16)
        rows_cot[rows, :] = picked[:capacity]
        hot_cot[rows, :] = picked[capacity:]
    part = width // 2
    here = pl.ds(pl.multiple_of(half * part, part), part)
    there = pl.ds(pl.multiple_of((1 - half) * part, part), part)
    mine[:, :part] = rows_in[:, here]
    mine[:, part:] = rows_cot[:, here]
    pack[:, 3 * units : 3 * units + part] = rows_in[:, there]
    pack[:, 3 * units + part :] = rows_cot[:, there]
    hot[:, :part] = hot_in[:, here]
    hot[:, part:width] = hot_cot[:, here]
    hot[:, width : width + part] = hot_in[:, there]
    hot[:, width + part :] = hot_cot[:, there]
    load_gu.wait()
    projected = dot(rows_in[...], gate_up[...], (1, 0))
    gate_pre, up_pre = projected[:, :units], projected[:, units:]
    load_down.wait()
    hidden_grad = dot(rows_cot[...], down[...], (1, 1))
    sigmoid_gate = jax.nn.sigmoid(gate_pre)
    activation = gate_pre * sigmoid_gate
    gate_grad = hidden_grad * up_pre * sigmoid_gate * (1.0 + gate_pre * (1.0 - sigmoid_gate))
    pack[:, :units] = gate_grad.astype(BF16)
    pack[:, units : 2 * units] = (hidden_grad * activation).astype(BF16)
    pack[:, 2 * units : 3 * units] = (activation * up_pre).astype(BF16)
    input_rows = dot(pack[:, : 2 * units], gate_up[...], (1, 1)).astype(BF16)
    for at, part in enumerate(back):
        part[...] = input_rows[at * part.shape[0] : (at + 1) * part.shape[0]]
    if turned is not None:
        grads = pack[:, : 3 * units]
        if joined:
            grads = jnp.concatenate([first[:, : 3 * units], grads], axis=0)
        turned[...] = grads.T


def run_step(steps, fanout, capacity, scal, blocks, first, gate_up, down):
    count, rows = len(steps), len(steps) * capacity
    units, width = down.shape
    vmem = pl.BlockSpec(memory_space=pltpu.VMEM)
    far = pl.BlockSpec(memory_space=pl.ANY)
    shapes = [(rows, width), (rows, 3 * units + width), (rows, 2 * width)]
    joined = first is not None
    pieces = 2 if joined else 1
    shapes += [(capacity // pieces, width)] * (count * pieces)
    if joined or count > 1:
        shapes += [(3 * units, 2 * capacity)]
    firsts = [first] if joined else []
    out = pl.pallas_call(
        functools.partial(step_kernel, steps, pieces, fanout, capacity, joined),
        out_shape=[jax.ShapeDtypeStruct(shape, BF16) for shape in shapes],
        in_specs=[pl.BlockSpec(memory_space=pltpu.SMEM)] + [vmem] * (len(blocks) + len(firsts)) + [far] * 2,
        out_specs=[vmem] * len(shapes),
        scratch_shapes=[pltpu.VMEM((rows, width), BF16)] * 4
        + [
            pltpu.VMEM(gate_up.shape, BF16),
            pltpu.VMEM(down.shape, BF16),
            pltpu.SemaphoreType.DMA((2,)),
        ],
        compiler_params=pltpu.CompilerParams(vmem_limit_bytes=VMEM_BYTES),
        cost_estimate=pl.CostEstimate(
            flops=2 * 256 * 5 * width * units, bytes_accessed=3 * 2 * width * units, transcendentals=0
        ),
        name="expert_step",
    )(scal, *blocks, *firsts, gate_up, down)
    return out[:3], out[3 : 3 + count * pieces], out[3 + count * pieces :]


def combine_kernel(experts, fanout, capacity, scal, meta, *refs):
    rows, out = refs[:-1], refs[-1]
    place = to_ring(scal[0], experts)
    table = meta[...].astype(F32).T
    picks = []
    for step in range(experts):
        expert = from_ring((place - step + experts) % experts, experts)
        picks.append(selection(table, expert, fanout, capacity)[0])
    onehot = jnp.concatenate(picks, axis=0).astype(BF16)
    out[...] = dot(onehot, jnp.concatenate([part[...] for part in rows], axis=0), (0, 0)).astype(BF16)


def combine(experts, fanout, capacity, scal, meta, rows):
    vmem = pl.BlockSpec(memory_space=pltpu.VMEM)
    tokens, width = meta.shape[0], rows[0].shape[1]
    return pl.pallas_call(
        functools.partial(combine_kernel, experts, fanout, capacity),
        out_shape=jax.ShapeDtypeStruct((tokens, width), BF16),
        in_specs=[pl.BlockSpec(memory_space=pltpu.SMEM)] + [vmem] * (len(rows) + 1),
        out_specs=vmem,
        compiler_params=pltpu.CompilerParams(vmem_limit_bytes=VMEM_BYTES),
        cost_estimate=pl.CostEstimate(
            flops=2 * experts * capacity * tokens * width, bytes_accessed=2 * experts * capacity * width, transcendentals=0
        ),
        name="token_sum",
    )(scal, meta, *rows)


def gradient_kernel(units, count, scal, *refs):
    ins, cots, grads = refs[: 2 * count], refs[2 * count : 4 * count], refs[4 * count : 6 * count]
    out = refs[6 * count]
    keep = scal[0] != scal[2]
    left = jnp.concatenate([ref[...] for ref in ins], axis=0)
    right = jnp.concatenate([ref[:, : 2 * units] for ref in grads], axis=0)
    out[0, :, : 2 * units] = jnp.where(keep, dot(left, right, (0, 0)), 0.0)
    left = jnp.concatenate([ref[...] for ref in cots], axis=0)
    right = jnp.concatenate([ref[:, 2 * units :] for ref in grads], axis=0)
    out[0, :, 2 * units :] = jnp.where(keep, dot(left, right, (0, 0)), 0.0)


def expert_gradient(units, scal, mine, packs, others):
    width, columns, count = mine[0].shape[1], 3 * units, len(mine)
    tile = 256
    tiles, skip = width // 2 // tile, columns // tile
    total = 2 * sum(part.shape[0] for part in mine)
    rows = mine + others

    def tiled(first):
        specs = [pl.BlockSpec((part.shape[0], tile), lambda i: (0, i + first)) for part in mine]
        return specs + [
            pl.BlockSpec((part.shape[0], tile), lambda i: (0, i + first + skip)) for part in others
        ]

    in_specs = [pl.BlockSpec(memory_space=pltpu.SMEM)] + tiled(0) + tiled(tiles)
    in_specs += [pl.BlockSpec((part.shape[0], columns), lambda i: (0, 0)) for part in packs + others]
    return pl.pallas_call(
        functools.partial(gradient_kernel, units, count),
        grid=(tiles,),
        out_shape=jax.ShapeDtypeStruct((1, width // 2, columns), F32),
        in_specs=in_specs,
        out_specs=pl.BlockSpec((1, tile, columns), lambda i: (0, i, 0)),
        compiler_params=pltpu.CompilerParams(vmem_limit_bytes=VMEM_BYTES),
        cost_estimate=pl.CostEstimate(
            flops=width * columns * total, bytes_accessed=3 * width * columns, transcendentals=0
        ),
        name="expert_gradient",
    )(scal, *rows, *rows, *packs, *others)


def message_kernel(fanout, tokens, cotangent, routes, route_weight, ratio, clip, message, meta):
    count, width = tokens.shape
    message[:, :width] = tokens[...]
    message[:, width : 2 * width] = cotangent[...]
    weight = route_weight[...] * ratio[...] * clip[...].astype(F32)
    first = weight.astype(BF16).astype(F32)
    rest = weight - first
    second = rest.astype(BF16).astype(F32)
    lines = -(-4 * fanout // 8) * 8
    row = lax.broadcasted_iota(jnp.int32, (lines, count), 0)
    table = jnp.zeros((lines, count), F32)
    for number, part in enumerate([routes[...].astype(F32), first, second, rest - second]):
        for k in range(fanout):
            table = jnp.where(row == number * fanout + k, part[k : k + 1], table)
    table = jnp.concatenate([table, jnp.zeros((128 - lines, count), F32)], axis=0)
    columns = table.T.astype(BF16)
    message[:, 2 * width :] = columns
    meta[...] = columns


def build_message(tokens, cotangent, routes, route_weight, ratio, clip):
    count, width = tokens.shape
    vmem = pl.BlockSpec(memory_space=pltpu.VMEM)
    return pl.pallas_call(
        functools.partial(message_kernel, routes.shape[1]),
        out_shape=[
            jax.ShapeDtypeStruct((count, 2 * width + 128), BF16),
            jax.ShapeDtypeStruct((count, 128), BF16),
        ],
        in_specs=[vmem] * 6,
        out_specs=[vmem] * 2,
        cost_estimate=pl.CostEstimate(flops=0, bytes_accessed=8 * count * width, transcendentals=0),
        name="ring_message",
    )(tokens, cotangent, routes.T, route_weight.T, ratio[None], clip[None])


def order_kernel(plan, experts, capacity, scal, *refs):
    parts, mine, theirs = refs[:-2], refs[-2], refs[-1]
    shift = to_ring(scal[0], experts) - to_ring(scal[2], experts)
    width = mine.shape[1]
    for steps, part in zip(plan, parts):
        for at, step in enumerate(steps):
            place = slot_place((shift + step + 2 * experts) % experts, experts)
            there = pl.ds(pl.multiple_of(place * capacity, capacity), capacity)
            mine[there, :] = part[at * capacity : (at + 1) * capacity, :width]
            theirs[there, :] = part[at * capacity : (at + 1) * capacity, width:]


def ordered(plan, experts, capacity, scal, parts):
    vmem = pl.BlockSpec(memory_space=pltpu.VMEM)
    rows, width = experts * capacity, parts[0].shape[1] // 2
    return pl.pallas_call(
        functools.partial(order_kernel, plan, experts, capacity),
        out_shape=[jax.ShapeDtypeStruct((rows, width), BF16)] * 2,
        in_specs=[pl.BlockSpec(memory_space=pltpu.SMEM)] + [vmem] * len(parts),
        out_specs=[vmem] * 2,
        compiler_params=pltpu.CompilerParams(vmem_limit_bytes=VMEM_BYTES),
        cost_estimate=pl.CostEstimate(flops=0, bytes_accessed=8 * rows * width, transcendentals=0),
        name="hot_rows_ordered",
    )(scal, *parts)


def shadow_kernel(experts, scal, mine, theirs, hot_mine, hot_theirs, out):
    own = scal[0]
    taken = mine.shape[0]
    width = out.shape[1]
    gates = taken * experts * 2 // 3
    column = own * taken + lax.broadcasted_iota(jnp.int32, (taken, 1), 0)

    def product(first):
        columns = pl.ds(first, width)
        return dot(mine[...], hot_mine[:, columns], (1, 0)) + dot(theirs[...], hot_theirs[:, columns], (1, 0))

    @pl.when((own + 1) * taken <= gates)
    def _():
        out[...] = product(0)

    @pl.when(own * taken >= gates)
    def _():
        out[...] = product(width)

    @pl.when((own * taken < gates) & ((own + 1) * taken > gates))
    def _():
        out[...] = jnp.where(column < gates, product(0), product(width))


def shadow_gradient(experts, scal, mine, theirs, hot_mine, hot_theirs):
    taken, rows = mine.shape
    width = hot_mine.shape[1] // 2
    vmem = pl.BlockSpec(memory_space=pltpu.VMEM)
    return pl.pallas_call(
        functools.partial(shadow_kernel, experts),
        out_shape=jax.ShapeDtypeStruct((taken, width), F32),
        in_specs=[pl.BlockSpec(memory_space=pltpu.SMEM)] + [vmem] * 4,
        out_specs=vmem,
        compiler_params=pltpu.CompilerParams(vmem_limit_bytes=24 * 1024 * 1024),
        cost_estimate=pl.CostEstimate(
            flops=4 * taken * rows * width, bytes_accessed=4 * rows * width, transcendentals=0
        ),
        name="shadow_gradient",
    )(scal, mine, theirs, hot_mine, hot_theirs)


def on_device(
    tokens, cotangent, routes, route_weight, ratio_advantage, clip_mask, shadow_plan, gate_up, down
):
    experts = lax.axis_size("expert")
    tok_rows, width = tokens.shape
    fanout = routes.shape[1]
    units = down.shape[1]
    capacity = 2 * tok_rows * fanout // experts
    gate_up, down = gate_up[0], down[0]
    order = ring_order(experts)
    half = experts // 2

    def shift(block, step):
        pairs = [(order[i], order[(i + step) % experts]) for i in range(experts)]
        return lax.ppermute(block, "expert", pairs)

    def swap(block):
        return lax.ppermute(block, "dp", [(0, 1), (1, 0)])

    own = lax.axis_index("expert")
    hottest = shadow_plan[0]
    scal = jnp.stack([own, lax.axis_index("dp"), hottest]).astype(jnp.int32)
    message, meta = build_message(
        tokens, cotangent, routes, route_weight, ratio_advantage, clip_mask
    )

    plan = distances(experts)
    mine, packs, hot, turned, late = [], [], [], [], []
    returned = {}
    up, below, held = message, message, [message]
    for number, steps in enumerate(plan):
        if number + 1 < half:
            following = [shift(up, 1), shift(below, -1)]
        elif number + 1 == half:
            following = [shift(up[:, :width], 1), shift(below[:, width:], -1)]
        if 0 < number < half - 1:
            held, late[number - 1] = lax.optimization_barrier((held, late[number - 1]))
        (rows, pack, hot_rows), back, turn = run_step(
            steps,
            fanout,
            capacity,
            scal,
            held,
            packs[0] if number == half else None,
            gate_up,
            down,
        )
        following, back = lax.optimization_barrier((following, back))
        steps = steps * (len(back) // len(steps))
        sent = [shift(part, step) if step else part for step, part in zip(steps, back)]
        late.append((sent, swap(pack)))
        mine.append(rows)
        packs.append(pack)
        hot.append(hot_rows)
        turned += turn
        held = following
        if number < half:
            up, below = following
    (back_behind, back_ahead), other = late[half - 1]
    turned[-1], late[half - 2] = lax.optimization_barrier((turned[-1], late[half - 2]))

    taken = 3 * units // experts
    ring_hot = to_ring(hottest, experts)
    is_hot = own == hottest

    def chunk(distance):
        owner = from_ring((ring_hot + distance + experts) % experts, experts)
        parts = [lax.dynamic_slice_in_dim(part, owner * taken, taken, axis=0) for part in turned]
        return jnp.concatenate(parts, axis=1)

    far = chunk(half)
    lanes = far.shape[1] // 2
    around = [far[:, :lanes], far[:, lanes:]]
    around, other = lax.optimization_barrier((around, other))
    around = [shift(around[0], 1), shift(around[1], -1)]
    others = [part for _, part in late[: half - 1]] + [other, late[half][1]]
    expert_grad = expert_gradient(units, scal, mine, packs, others)
    chunks = [chunk(distance) for distance in range(1 - half, half)]
    back_far = list(late[half][0])
    hot_mine, hot_theirs = ordered(plan, experts, capacity, scal, hot)
    for number in range(1, half):
        if number == 1:
            around, expert_grad, back_ahead, chunks = lax.optimization_barrier(
                (around, expert_grad, back_ahead, chunks)
            )
            around = [jnp.concatenate([part, part], axis=1) for part in around]
        if number == half - 2:
            around, back_behind = lax.optimization_barrier((around, back_behind))
        if number == half - 1:
            around, back_far[0], hot_mine, hot_theirs = lax.optimization_barrier(
                (around, back_far[0], hot_mine, hot_theirs)
            )
        ahead = jnp.where(is_hot, chunks[2 * half - 1 - number], around[0])
        behind = jnp.where(is_hot, chunks[number - 1], around[1])
        around = [shift(ahead, 1), shift(behind, -1)]
    around, back_far[1] = lax.optimization_barrier((around, back_far[1]))
    hot_theirs = swap(hot_theirs)
    away = (to_ring(own, experts) - ring_hot + experts) % experts
    lane = lax.broadcasted_iota(jnp.int32, far.shape, 1)
    reach = jnp.where(lane < lanes, half, half - 1)
    columns = jnp.where(
        away == 0, chunks[half - 1], jnp.where(away <= reach, around[0], around[1])
    )
    shadow_grad = shadow_gradient(
        experts, scal, columns, swap(columns), hot_mine, hot_theirs
    ).T
    sent = [rows for rows, _ in late[: half - 1]] + [[back_behind, back_ahead]]
    for steps, parts in zip(plan, sent):
        for step, part in zip(steps, parts):
            returned[step % experts] = [part]
    returned[half] = back_far
    rows = [part for distance in range(experts) for part in returned[distance]]
    token_grad = combine(experts, fanout, capacity, scal, meta, rows)
    return (token_grad, expert_grad, shadow_grad)


def solution(mesh):
    placed = (
        P(("group", "expert", "dp"), None),
        P(("group", "expert", "dp"), None),
        P(("group", "expert", "dp"), None),
        P(("group", "expert", "dp"), None),
        P(("group", "expert", "dp")),
        P(("group", "expert", "dp")),
        P("group"),
        P("expert", None, None),
        P("expert", None, None),
    )
    return jax.shard_map(
        on_device,
        mesh=mesh,
        in_specs=placed,
        out_specs=(
            P(("group", "expert", "dp"), None),
            P(("group", "expert"), "dp", None),
            P(("group", "dp"), "expert"),
        ),
        check_vma=False,
    )
```

```python
import functools

import jax
import jax.numpy as jnp
from jax import lax
from jax.experimental import pallas as pl
from jax.experimental.pallas import tpu as pltpu
from jax.sharding import PartitionSpec as P

BF16 = jnp.bfloat16
F32 = jnp.float32
VMEM_BYTES = 56 * 1024 * 1024


def snaked(experts):
    return experts <= 8


def to_ring(expert, experts):
    if not snaked(experts):
        return expert
    down = experts - 1 - (expert - 1) // 2
    return jnp.where(expert % 2 == 0, expert // 2, down)


def from_ring(place, experts):
    if not snaked(experts):
        return place
    return jnp.where(place < experts // 2, 2 * place, 2 * (experts - 1 - place) + 1)


def ring_order(experts):
    if not snaked(experts):
        return list(range(experts))
    return list(range(0, experts, 2)) + list(range(experts - 1, 0, -2))


def distances(experts):
    half = experts // 2
    return [[0]] + [[-step, step] for step in range(1, half)] + [[half]]


def slot_place(distance, experts):
    half = experts // 2
    near = jnp.where(distance < half, 2 * distance - 1, 2 * (experts - distance) - 2)
    near = jnp.where(distance == half, experts - 1, near)
    return jnp.where(distance == 0, experts - 2, near)


def dot(a, b, dims):
    return lax.dot_general(a, b, ((dims[:1], dims[1:]), ((), ())), preferred_element_type=F32)


def selection(table, expert, fanout, capacity):
    tokens = table.shape[1]
    hit = table[:fanout] == expert.astype(F32)
    named = jnp.sum(jnp.where(hit, 1.0, 0.0), axis=0, keepdims=True)
    parts = table[fanout : 4 * fanout]
    weights = parts[:fanout] + parts[fanout : 2 * fanout] + parts[2 * fanout :]
    weight = jnp.sum(jnp.where(hit, weights, 0.0), axis=0, keepdims=True)
    upto = lax.broadcasted_iota(jnp.int32, (tokens, tokens), 0) <= lax.broadcasted_iota(
        jnp.int32, (tokens, tokens), 1
    )
    upto = jnp.where(upto, 1.0, 0.0).astype(BF16)
    place = dot(jnp.broadcast_to(named, (8, tokens)).astype(BF16), upto, (1, 0))[:1]
    row = lax.broadcasted_iota(jnp.int32, (capacity, tokens), 0).astype(F32) + 1.0
    onehot = jnp.where((row == place) & (named > 0.5), 1.0, 0.0)
    return onehot, weight


def step_kernel(steps, pieces, fanout, capacity, joined, scal, *refs):
    count = len(steps)
    blocks, refs = refs[: max(count, 1 + joined)], refs[max(count, 1 + joined) :]
    if joined:
        first, refs = refs[0], refs[1:]
        blocks = [jnp.concatenate([block[...] for block in blocks], axis=1)]
    weights_gu, weights_down, mine, pack, hot = refs[:5]
    back, refs = refs[5 : 5 + count * pieces], refs[5 + count * pieces :]
    if len(refs) > 7:
        turned, refs = refs[0], refs[1:]
    else:
        turned = None
    rows_in, rows_cot, hot_in, hot_cot, gate_up, down, sems = refs
    own, half, hottest = scal[0], scal[1], scal[2]
    units, width = down.shape
    load_gu = pltpu.make_async_copy(weights_gu, gate_up, sems.at[0])
    load_down = pltpu.make_async_copy(weights_down, down, sems.at[1])
    load_gu.start()
    load_down.start()
    for at, block in enumerate(blocks):
        rows = slice(at * capacity, (at + 1) * capacity)
        table = block[:, 2 * width :].astype(F32).T
        own_hot, own_weight = selection(table, own, fanout, capacity)
        all_hot, all_weight = selection(table, hottest, fanout, capacity)
        scale = jnp.concatenate(
            [
                jnp.sum(own_hot * own_weight, axis=1, keepdims=True),
                jnp.sum(all_hot * all_weight, axis=1, keepdims=True),
            ],
            axis=0,
        )
        onehot = jnp.concatenate([own_hot, all_hot], axis=0).astype(BF16)
        picked = dot(onehot, block[:, :width], (1, 0)).astype(BF16)
        rows_in[rows, :] = picked[:capacity]
        hot_in[rows, :] = picked[capacity:]
        picked = (scale * dot(onehot, block[:, width : 2 * width], (1, 0))).astype(BF16)
        rows_cot[rows, :] = picked[:capacity]
        hot_cot[rows, :] = picked[capacity:]
    part = width // 2
    here = pl.ds(pl.multiple_of(half * part, part), part)
    there = pl.ds(pl.multiple_of((1 - half) * part, part), part)
    mine[:, :part] = rows_in[:, here]
    mine[:, part:] = rows_cot[:, here]
    pack[:, 3 * units : 3 * units + part] = rows_in[:, there]
    pack[:, 3 * units + part :] = rows_cot[:, there]
    hot[:, :part] = hot_in[:, here]
    hot[:, part:width] = hot_cot[:, here]
    hot[:, width : width + part] = hot_in[:, there]
    hot[:, width + part :] = hot_cot[:, there]
    load_gu.wait()
    projected = dot(rows_in[...], gate_up[...], (1, 0))
    gate_pre, up_pre = projected[:, :units], projected[:, units:]
    load_down.wait()
    hidden_grad = dot(rows_cot[...], down[...], (1, 1))
    sigmoid_gate = jax.nn.sigmoid(gate_pre)
    activation = gate_pre * sigmoid_gate
    gate_grad = hidden_grad * up_pre * sigmoid_gate * (1.0 + gate_pre * (1.0 - sigmoid_gate))
    pack[:, :units] = gate_grad.astype(BF16)
    pack[:, units : 2 * units] = (hidden_grad * activation).astype(BF16)
    pack[:, 2 * units : 3 * units] = (activation * up_pre).astype(BF16)
    input_rows = dot(pack[:, : 2 * units], gate_up[...], (1, 1)).astype(BF16)
    for at, part in enumerate(back):
        part[...] = input_rows[at * part.shape[0] : (at + 1) * part.shape[0]]
    if turned is not None:
        grads = pack[:, : 3 * units]
        if joined:
            grads = jnp.concatenate([first[:, : 3 * units], grads], axis=0)
        turned[...] = grads.T


def run_step(steps, fanout, capacity, scal, blocks, first, gate_up, down):
    count, rows = len(steps), len(steps) * capacity
    units, width = down.shape
    vmem = pl.BlockSpec(memory_space=pltpu.VMEM)
    far = pl.BlockSpec(memory_space=pl.ANY)
    shapes = [(rows, width), (rows, 3 * units + width), (rows, 2 * width)]
    joined = first is not None
    pieces = 2 if joined else 1
    shapes += [(capacity // pieces, width)] * (count * pieces)
    if joined or count > 1:
        shapes += [(3 * units, 2 * capacity)]
    firsts = [first] if joined else []
    out = pl.pallas_call(
        functools.partial(step_kernel, steps, pieces, fanout, capacity, joined),
        out_shape=[jax.ShapeDtypeStruct(shape, BF16) for shape in shapes],
        in_specs=[pl.BlockSpec(memory_space=pltpu.SMEM)] + [vmem] * (len(blocks) + len(firsts)) + [far] * 2,
        out_specs=[vmem] * len(shapes),
        scratch_shapes=[pltpu.VMEM((rows, width), BF16)] * 4
        + [
            pltpu.VMEM(gate_up.shape, BF16),
            pltpu.VMEM(down.shape, BF16),
            pltpu.SemaphoreType.DMA((2,)),
        ],
        compiler_params=pltpu.CompilerParams(vmem_limit_bytes=VMEM_BYTES),
        cost_estimate=pl.CostEstimate(
            flops=2 * 256 * 5 * width * units, bytes_accessed=3 * 2 * width * units, transcendentals=0
        ),
        name="expert_step",
    )(scal, *blocks, *firsts, gate_up, down)
    return out[:3], out[3 : 3 + count * pieces], out[3 + count * pieces :]


def combine_kernel(experts, fanout, capacity, scal, meta, *refs):
    rows, out = refs[:-1], refs[-1]
    place = to_ring(scal[0], experts)
    table = meta[...].astype(F32).T
    picks = []
    for step in range(experts):
        expert = from_ring((place - step + experts) % experts, experts)
        picks.append(selection(table, expert, fanout, capacity)[0])
    onehot = jnp.concatenate(picks, axis=0).astype(BF16)
    out[...] = dot(onehot, jnp.concatenate([part[...] for part in rows], axis=0), (0, 0)).astype(BF16)


def combine(experts, fanout, capacity, scal, meta, rows):
    vmem = pl.BlockSpec(memory_space=pltpu.VMEM)
    tokens, width = meta.shape[0], rows[0].shape[1]
    return pl.pallas_call(
        functools.partial(combine_kernel, experts, fanout, capacity),
        out_shape=jax.ShapeDtypeStruct((tokens, width), BF16),
        in_specs=[pl.BlockSpec(memory_space=pltpu.SMEM)] + [vmem] * (len(rows) + 1),
        out_specs=vmem,
        compiler_params=pltpu.CompilerParams(vmem_limit_bytes=VMEM_BYTES),
        cost_estimate=pl.CostEstimate(
            flops=2 * experts * capacity * tokens * width, bytes_accessed=2 * experts * capacity * width, transcendentals=0
        ),
        name="token_sum",
    )(scal, meta, *rows)


def gradient_kernel(units, count, scal, *refs):
    ins, cots, grads = refs[: 2 * count], refs[2 * count : 4 * count], refs[4 * count : 6 * count]
    out = refs[6 * count]
    keep = scal[0] != scal[2]
    left = jnp.concatenate([ref[...] for ref in ins], axis=0)
    right = jnp.concatenate([ref[:, : 2 * units] for ref in grads], axis=0)
    out[0, :, : 2 * units] = jnp.where(keep, dot(left, right, (0, 0)), 0.0)
    left = jnp.concatenate([ref[...] for ref in cots], axis=0)
    right = jnp.concatenate([ref[:, 2 * units :] for ref in grads], axis=0)
    out[0, :, 2 * units :] = jnp.where(keep, dot(left, right, (0, 0)), 0.0)


def expert_gradient(units, scal, mine, packs, others):
    width, columns, count = mine[0].shape[1], 3 * units, len(mine)
    tile = 256
    tiles, skip = width // 2 // tile, columns // tile
    total = 2 * sum(part.shape[0] for part in mine)
    rows = mine + others

    def tiled(first):
        specs = [pl.BlockSpec((part.shape[0], tile), lambda i: (0, i + first)) for part in mine]
        return specs + [
            pl.BlockSpec((part.shape[0], tile), lambda i: (0, i + first + skip)) for part in others
        ]

    in_specs = [pl.BlockSpec(memory_space=pltpu.SMEM)] + tiled(0) + tiled(tiles)
    in_specs += [pl.BlockSpec((part.shape[0], columns), lambda i: (0, 0)) for part in packs + others]
    return pl.pallas_call(
        functools.partial(gradient_kernel, units, count),
        grid=(tiles,),
        out_shape=jax.ShapeDtypeStruct((1, width // 2, columns), F32),
        in_specs=in_specs,
        out_specs=pl.BlockSpec((1, tile, columns), lambda i: (0, i, 0)),
        compiler_params=pltpu.CompilerParams(vmem_limit_bytes=VMEM_BYTES),
        cost_estimate=pl.CostEstimate(
            flops=width * columns * total, bytes_accessed=3 * width * columns, transcendentals=0
        ),
        name="expert_gradient",
    )(scal, *rows, *rows, *packs, *others)


def message_kernel(fanout, tokens, cotangent, routes, route_weight, ratio, clip, message, meta):
    count, width = tokens.shape
    message[:, :width] = tokens[...]
    message[:, width : 2 * width] = cotangent[...]
    weight = route_weight[...] * ratio[...] * clip[...].astype(F32)
    first = weight.astype(BF16).astype(F32)
    rest = weight - first
    second = rest.astype(BF16).astype(F32)
    lines = -(-4 * fanout // 8) * 8
    row = lax.broadcasted_iota(jnp.int32, (lines, count), 0)
    table = jnp.zeros((lines, count), F32)
    for number, part in enumerate([routes[...].astype(F32), first, second, rest - second]):
        for k in range(fanout):
            table = jnp.where(row == number * fanout + k, part[k : k + 1], table)
    table = jnp.concatenate([table, jnp.zeros((128 - lines, count), F32)], axis=0)
    columns = table.T.astype(BF16)
    message[:, 2 * width :] = columns
    meta[...] = columns


def build_message(tokens, cotangent, routes, route_weight, ratio, clip):
    count, width = tokens.shape
    vmem = pl.BlockSpec(memory_space=pltpu.VMEM)
    return pl.pallas_call(
        functools.partial(message_kernel, routes.shape[1]),
        out_shape=[
            jax.ShapeDtypeStruct((count, 2 * width + 128), BF16),
            jax.ShapeDtypeStruct((count, 128), BF16),
        ],
        in_specs=[vmem] * 6,
        out_specs=[vmem] * 2,
        cost_estimate=pl.CostEstimate(flops=0, bytes_accessed=8 * count * width, transcendentals=0),
        name="ring_message",
    )(tokens, cotangent, routes.T, route_weight.T, ratio[None], clip[None])


def order_kernel(plan, experts, capacity, scal, *refs):
    parts, mine, theirs = refs[:-2], refs[-2], refs[-1]
    shift = to_ring(scal[0], experts) - to_ring(scal[2], experts)
    width = mine.shape[1]
    for steps, part in zip(plan, parts):
        for at, step in enumerate(steps):
            place = slot_place((shift + step + 2 * experts) % experts, experts)
            there = pl.ds(pl.multiple_of(place * capacity, capacity), capacity)
            mine[there, :] = part[at * capacity : (at + 1) * capacity, :width]
            theirs[there, :] = part[at * capacity : (at + 1) * capacity, width:]


def ordered(plan, experts, capacity, scal, parts):
    vmem = pl.BlockSpec(memory_space=pltpu.VMEM)
    rows, width = experts * capacity, parts[0].shape[1] // 2
    return pl.pallas_call(
        functools.partial(order_kernel, plan, experts, capacity),
        out_shape=[jax.ShapeDtypeStruct((rows, width), BF16)] * 2,
        in_specs=[pl.BlockSpec(memory_space=pltpu.SMEM)] + [vmem] * len(parts),
        out_specs=[vmem] * 2,
        compiler_params=pltpu.CompilerParams(vmem_limit_bytes=VMEM_BYTES),
        cost_estimate=pl.CostEstimate(flops=0, bytes_accessed=8 * rows * width, transcendentals=0),
        name="hot_rows_ordered",
    )(scal, *parts)


def shadow_kernel(experts, scal, mine, theirs, hot_mine, hot_theirs, out):
    own = scal[0]
    taken = mine.shape[0]
    width = out.shape[1]
    gates = taken * experts * 2 // 3
    column = own * taken + lax.broadcasted_iota(jnp.int32, (taken, 1), 0)

    def product(first):
        columns = pl.ds(first, width)
        return dot(mine[...], hot_mine[:, columns], (1, 0)) + dot(theirs[...], hot_theirs[:, columns], (1, 0))

    @pl.when((own + 1) * taken <= gates)
    def _():
        out[...] = product(0)

    @pl.when(own * taken >= gates)
    def _():
        out[...] = product(width)

    @pl.when((own * taken < gates) & ((own + 1) * taken > gates))
    def _():
        out[...] = jnp.where(column < gates, product(0), product(width))


def shadow_gradient(experts, scal, mine, theirs, hot_mine, hot_theirs):
    taken, rows = mine.shape
    width = hot_mine.shape[1] // 2
    vmem = pl.BlockSpec(memory_space=pltpu.VMEM)
    return pl.pallas_call(
        functools.partial(shadow_kernel, experts),
        out_shape=jax.ShapeDtypeStruct((taken, width), F32),
        in_specs=[pl.BlockSpec(memory_space=pltpu.SMEM)] + [vmem] * 4,
        out_specs=vmem,
        compiler_params=pltpu.CompilerParams(vmem_limit_bytes=24 * 1024 * 1024),
        cost_estimate=pl.CostEstimate(
            flops=4 * taken * rows * width, bytes_accessed=4 * rows * width, transcendentals=0
        ),
        name="shadow_gradient",
    )(scal, mine, theirs, hot_mine, hot_theirs)


def on_device(
    tokens, cotangent, routes, route_weight, ratio_advantage, clip_mask, shadow_plan, gate_up, down
):
    experts = lax.axis_size("expert")
    tok_rows, width = tokens.shape
    fanout = routes.shape[1]
    units = down.shape[1]
    capacity = 2 * tok_rows * fanout // experts
    gate_up, down = gate_up[0], down[0]
    order = ring_order(experts)
    half = experts // 2

    def shift(block, step):
        pairs = [(order[i], order[(i + step) % experts]) for i in range(experts)]
        return lax.ppermute(block, "expert", pairs)

    def swap(block):
        return lax.ppermute(block, "dp", [(0, 1), (1, 0)])

    own = lax.axis_index("expert")
    hottest = shadow_plan[0]
    scal = jnp.stack([own, lax.axis_index("dp"), hottest]).astype(jnp.int32)
    message, meta = build_message(
        tokens, cotangent, routes, route_weight, ratio_advantage, clip_mask
    )

    plan = distances(experts)
    mine, packs, hot, turned, late = [], [], [], [], []
    returned = {}
    up, below, held = message, message, [message]
    for number, steps in enumerate(plan):
        if number + 1 < half:
            following = [shift(up, 1), shift(below, -1)]
        elif number + 1 == half:
            following = [shift(up[:, :width], 1), shift(below[:, width:], -1)]
        if number > 1:
            sent, other = late[number - 2]
            held, other = lax.optimization_barrier((held, other))
            late[number - 2] = (sent, other)
        if number == half - 1:
            held, late[: half - 2] = lax.optimization_barrier((held, late[: half - 2]))
        (rows, pack, hot_rows), back, turn = run_step(
            steps,
            fanout,
            capacity,
            scal,
            held,
            packs[0] if number == half else None,
            gate_up,
            down,
        )
        following, back = lax.optimization_barrier((following, back))
        steps = steps * (len(back) // len(steps))
        sent = [shift(part, step) if step else part for step, part in zip(steps, back)]
        late.append((sent, swap(pack)))
        mine.append(rows)
        packs.append(pack)
        hot.append(hot_rows)
        turned += turn
        held = following
        if number < half:
            up, below = following
    (back_behind, back_ahead), other = late[half - 1]
    turned[-1], late[half - 2] = lax.optimization_barrier((turned[-1], late[half - 2]))

    taken = 3 * units // experts
    ring_hot = to_ring(hottest, experts)
    is_hot = own == hottest

    def chunk(distance):
        owner = from_ring((ring_hot + distance + experts) % experts, experts)
        parts = [lax.dynamic_slice_in_dim(part, owner * taken, taken, axis=0) for part in turned]
        return jnp.concatenate(parts, axis=1)

    far = chunk(half)
    lanes = far.shape[1] // 2
    around = [far[:, :lanes], far[:, lanes:]]
    around, other = lax.optimization_barrier((around, other))
    around = [shift(around[0], 1), shift(around[1], -1)]
    others = [part for _, part in late[: half - 1]] + [other, late[half][1]]
    expert_grad = expert_gradient(units, scal, mine, packs, others)
    chunks = [chunk(distance) for distance in range(1 - half, half)]
    back_far = list(late[half][0])
    hot_mine, hot_theirs = ordered(plan, experts, capacity, scal, hot)
    for number in range(1, half):
        if number == 1:
            around, expert_grad, back_ahead, back_behind, chunks = lax.optimization_barrier(
                (around, expert_grad, back_ahead, back_behind, chunks)
            )
            around = [jnp.concatenate([part, part], axis=1) for part in around]
        if number == half - 2:
            around, back_far[0] = lax.optimization_barrier((around, back_far[0]))
        if number == half - 1:
            around, back_far[1], hot_mine, hot_theirs = lax.optimization_barrier(
                (around, back_far[1], hot_mine, hot_theirs)
            )
        ahead = jnp.where(is_hot, chunks[2 * half - 1 - number], around[0])
        behind = jnp.where(is_hot, chunks[number - 1], around[1])
        around = [shift(ahead, 1), shift(behind, -1)]
    hot_theirs = swap(hot_theirs)
    away = (to_ring(own, experts) - ring_hot + experts) % experts
    lane = lax.broadcasted_iota(jnp.int32, far.shape, 1)
    reach = jnp.where(lane < lanes, half, half - 1)
    columns = jnp.where(
        away == 0, chunks[half - 1], jnp.where(away <= reach, around[0], around[1])
    )
    shadow_grad = shadow_gradient(
        experts, scal, columns, swap(columns), hot_mine, hot_theirs
    ).T
    sent = [rows for rows, _ in late[: half - 1]] + [[back_behind, back_ahead]]
    for steps, parts in zip(plan, sent):
        for step, part in zip(steps, parts):
            returned[step % experts] = [part]
    returned[half] = back_far
    rows = [part for distance in range(experts) for part in returned[distance]]
    token_grad = combine(experts, fanout, capacity, scal, meta, rows)
    return (token_grad, expert_grad, shadow_grad)


def solution(mesh):
    placed = (
        P(("group", "expert", "dp"), None),
        P(("group", "expert", "dp"), None),
        P(("group", "expert", "dp"), None),
        P(("group", "expert", "dp"), None),
        P(("group", "expert", "dp")),
        P(("group", "expert", "dp")),
        P("group"),
        P("expert", None, None),
        P("expert", None, None),
    )
    return jax.shard_map(
        on_device,
        mesh=mesh,
        in_specs=placed,
        out_specs=(
            P(("group", "expert", "dp"), None),
            P(("group", "expert"), "dp", None),
            P(("group", "dp"), "expert"),
        ),
        check_vma=False,
    )
```

```python
import functools

import jax
import jax.numpy as jnp
from jax import lax
from jax.experimental import pallas as pl
from jax.experimental.pallas import tpu as pltpu
from jax.sharding import PartitionSpec as P

BF16 = jnp.bfloat16
F32 = jnp.float32
VMEM_BYTES = 56 * 1024 * 1024


def snaked(experts):
    return experts <= 8


def to_ring(expert, experts):
    if not snaked(experts):
        return expert
    down = experts - 1 - (expert - 1) // 2
    return jnp.where(expert % 2 == 0, expert // 2, down)


def from_ring(place, experts):
    if not snaked(experts):
        return place
    return jnp.where(place < experts // 2, 2 * place, 2 * (experts - 1 - place) + 1)


def ring_order(experts):
    if not snaked(experts):
        return list(range(experts))
    return list(range(0, experts, 2)) + list(range(experts - 1, 0, -2))


def distances(experts):
    half = experts // 2
    return [[0]] + [[-step, step] for step in range(1, half)] + [[half]]


def slot_place(distance, experts):
    half = experts // 2
    near = jnp.where(distance < half, 2 * distance - 1, 2 * (experts - distance) - 2)
    near = jnp.where(distance == half, experts - 1, near)
    return jnp.where(distance == 0, experts - 2, near)


def dot(a, b, dims):
    return lax.dot_general(a, b, ((dims[:1], dims[1:]), ((), ())), preferred_element_type=F32)


def selection(table, expert, fanout, capacity):
    tokens = table.shape[1]
    hit = table[:fanout] == expert.astype(F32)
    named = jnp.sum(jnp.where(hit, 1.0, 0.0), axis=0, keepdims=True)
    parts = table[fanout : 4 * fanout]
    weights = parts[:fanout] + parts[fanout : 2 * fanout] + parts[2 * fanout :]
    weight = jnp.sum(jnp.where(hit, weights, 0.0), axis=0, keepdims=True)
    upto = lax.broadcasted_iota(jnp.int32, (tokens, tokens), 0) <= lax.broadcasted_iota(
        jnp.int32, (tokens, tokens), 1
    )
    upto = jnp.where(upto, 1.0, 0.0).astype(BF16)
    place = dot(jnp.broadcast_to(named, (8, tokens)).astype(BF16), upto, (1, 0))[:1]
    row = lax.broadcasted_iota(jnp.int32, (capacity, tokens), 0).astype(F32) + 1.0
    onehot = jnp.where((row == place) & (named > 0.5), 1.0, 0.0)
    return onehot, weight


def step_kernel(steps, fanout, capacity, joined, scal, *refs):
    count = len(steps)
    messages, cotangents, refs = refs[:count], refs[count : 2 * count], refs[2 * count :]
    if joined:
        first, refs = refs[0], refs[1:]
    weights_gu, weights_down, mine, pack, hot = refs[:5]
    back, refs = refs[5 : 5 + count], refs[5 + count :]
    if len(refs) > 7:
        turned, refs = refs[0], refs[1:]
    else:
        turned = None
    rows_in, rows_cot, hot_in, hot_cot, gate_up, down, sems = refs
    own, half, hottest = scal[0], scal[1], scal[2]
    units, width = down.shape
    load_gu = pltpu.make_async_copy(weights_gu, gate_up, sems.at[0])
    load_down = pltpu.make_async_copy(weights_down, down, sems.at[1])
    load_gu.start()
    load_down.start()
    for at, (message, cotangent) in enumerate(zip(messages, cotangents)):
        rows = slice(at * capacity, (at + 1) * capacity)
        table = message[:, width:].astype(F32).T
        own_hot, own_weight = selection(table, own, fanout, capacity)
        all_hot, all_weight = selection(table, hottest, fanout, capacity)
        scale = jnp.concatenate(
            [
                jnp.sum(own_hot * own_weight, axis=1, keepdims=True),
                jnp.sum(all_hot * all_weight, axis=1, keepdims=True),
            ],
            axis=0,
        )
        onehot = jnp.concatenate([own_hot, all_hot], axis=0).astype(BF16)
        picked = dot(onehot, message[:, :width], (1, 0)).astype(BF16)
        rows_in[rows, :] = picked[:capacity]
        hot_in[rows, :] = picked[capacity:]
        picked = (scale * dot(onehot, cotangent[...], (1, 0))).astype(BF16)
        rows_cot[rows, :] = picked[:capacity]
        hot_cot[rows, :] = picked[capacity:]
    part = width // 2
    here = pl.ds(pl.multiple_of(half * part, part), part)
    there = pl.ds(pl.multiple_of((1 - half) * part, part), part)
    mine[:, :part] = rows_in[:, here]
    mine[:, part:] = rows_cot[:, here]
    pack[:, 3 * units : 3 * units + part] = rows_in[:, there]
    pack[:, 3 * units + part :] = rows_cot[:, there]
    hot[:, :part] = hot_in[:, here]
    hot[:, part:width] = hot_cot[:, here]
    hot[:, width : width + part] = hot_in[:, there]
    hot[:, width + part :] = hot_cot[:, there]
    load_gu.wait()
    projected = dot(rows_in[...], gate_up[...], (1, 0))
    gate_pre, up_pre = projected[:, :units], projected[:, units:]
    load_down.wait()
    hidden_grad = dot(rows_cot[...], down[...], (1, 1))
    sigmoid_gate = jax.nn.sigmoid(gate_pre)
    activation = gate_pre * sigmoid_gate
    gate_grad = hidden_grad * up_pre * sigmoid_gate * (1.0 + gate_pre * (1.0 - sigmoid_gate))
    pack[:, :units] = gate_grad.astype(BF16)
    pack[:, units : 2 * units] = (hidden_grad * activation).astype(BF16)
    pack[:, 2 * units : 3 * units] = (activation * up_pre).astype(BF16)
    input_rows = dot(pack[:, : 2 * units], gate_up[...], (1, 1)).astype(BF16)
    for at, part in enumerate(back):
        part[...] = input_rows[at * part.shape[0] : (at + 1) * part.shape[0]]
    if turned is not None:
        grads = pack[:, : 3 * units]
        if joined:
            grads = jnp.concatenate([first[:, : 3 * units], grads], axis=0)
        turned[...] = grads.T


def run_step(steps, fanout, capacity, scal, messages, cotangents, first, gate_up, down):
    count, rows = len(steps), len(steps) * capacity
    units, width = down.shape
    vmem = pl.BlockSpec(memory_space=pltpu.VMEM)
    far = pl.BlockSpec(memory_space=pl.ANY)
    shapes = [(rows, width), (rows, 3 * units + width), (rows, 2 * width)]
    joined = first is not None
    shapes += [(capacity, width)] * count
    if joined or count > 1:
        shapes += [(3 * units, 2 * capacity)]
    firsts = [first] if joined else []
    out = pl.pallas_call(
        functools.partial(step_kernel, steps, fanout, capacity, joined),
        out_shape=[jax.ShapeDtypeStruct(shape, BF16) for shape in shapes],
        in_specs=[pl.BlockSpec(memory_space=pltpu.SMEM)] + [vmem] * (2 * count + len(firsts)) + [far] * 2,
        out_specs=[vmem] * len(shapes),
        scratch_shapes=[pltpu.VMEM((rows, width), BF16)] * 4
        + [
            pltpu.VMEM(gate_up.shape, BF16),
            pltpu.VMEM(down.shape, BF16),
            pltpu.SemaphoreType.DMA((2,)),
        ],
        compiler_params=pltpu.CompilerParams(vmem_limit_bytes=VMEM_BYTES),
        cost_estimate=pl.CostEstimate(
            flops=2 * 256 * 5 * width * units, bytes_accessed=3 * 2 * width * units, transcendentals=0
        ),
        name="expert_step",
    )(scal, *messages, *cotangents, *firsts, gate_up, down)
    return out[:3], out[3 : 3 + count], out[3 + count :]


def combine_kernel(experts, fanout, capacity, scal, meta, *refs):
    rows, out = refs[:-1], refs[-1]
    place = to_ring(scal[0], experts)
    table = meta[...].astype(F32).T
    picks = []
    for step in range(experts):
        expert = from_ring((place - step + experts) % experts, experts)
        picks.append(selection(table, expert, fanout, capacity)[0])
    onehot = jnp.concatenate(picks, axis=0).astype(BF16)
    out[...] = dot(onehot, jnp.concatenate([part[...] for part in rows], axis=0), (0, 0)).astype(BF16)


def combine(experts, fanout, capacity, scal, meta, rows):
    vmem = pl.BlockSpec(memory_space=pltpu.VMEM)
    tokens, width = meta.shape[0], rows[0].shape[1]
    return pl.pallas_call(
        functools.partial(combine_kernel, experts, fanout, capacity),
        out_shape=jax.ShapeDtypeStruct((tokens, width), BF16),
        in_specs=[pl.BlockSpec(memory_space=pltpu.SMEM)] + [vmem] * (len(rows) + 1),
        out_specs=vmem,
        compiler_params=pltpu.CompilerParams(vmem_limit_bytes=VMEM_BYTES),
        cost_estimate=pl.CostEstimate(
            flops=2 * experts * capacity * tokens * width, bytes_accessed=2 * experts * capacity * width, transcendentals=0
        ),
        name="token_sum",
    )(scal, meta, *rows)


def gradient_kernel(units, count, scal, *refs):
    ins, cots, grads = refs[: 2 * count], refs[2 * count : 4 * count], refs[4 * count : 6 * count]
    out = refs[6 * count]
    keep = scal[0] != scal[2]
    left = jnp.concatenate([ref[...] for ref in ins], axis=0)
    right = jnp.concatenate([ref[:, : 2 * units] for ref in grads], axis=0)
    out[0, :, : 2 * units] = jnp.where(keep, dot(left, right, (0, 0)), 0.0)
    left = jnp.concatenate([ref[...] for ref in cots], axis=0)
    right = jnp.concatenate([ref[:, 2 * units :] for ref in grads], axis=0)
    out[0, :, 2 * units :] = jnp.where(keep, dot(left, right, (0, 0)), 0.0)


def expert_gradient(units, scal, mine, packs, others):
    width, columns, count = mine[0].shape[1], 3 * units, len(mine)
    tile = 256
    tiles, skip = width // 2 // tile, columns // tile
    total = 2 * sum(part.shape[0] for part in mine)
    rows = mine + others

    def tiled(first):
        specs = [pl.BlockSpec((part.shape[0], tile), lambda i: (0, i + first)) for part in mine]
        return specs + [
            pl.BlockSpec((part.shape[0], tile), lambda i: (0, i + first + skip)) for part in others
        ]

    in_specs = [pl.BlockSpec(memory_space=pltpu.SMEM)] + tiled(0) + tiled(tiles)
    in_specs += [pl.BlockSpec((part.shape[0], columns), lambda i: (0, 0)) for part in packs + others]
    return pl.pallas_call(
        functools.partial(gradient_kernel, units, count),
        grid=(tiles,),
        out_shape=jax.ShapeDtypeStruct((1, width // 2, columns), F32),
        in_specs=in_specs,
        out_specs=pl.BlockSpec((1, tile, columns), lambda i: (0, i, 0)),
        compiler_params=pltpu.CompilerParams(vmem_limit_bytes=VMEM_BYTES),
        cost_estimate=pl.CostEstimate(
            flops=width * columns * total, bytes_accessed=3 * width * columns, transcendentals=0
        ),
        name="expert_gradient",
    )(scal, *rows, *rows, *packs, *others)


def message_kernel(fanout, tokens, routes, route_weight, ratio, clip, message, meta):
    count, width = tokens.shape
    message[:, :width] = tokens[...]
    weight = route_weight[...] * ratio[...] * clip[...].astype(F32)
    first = weight.astype(BF16).astype(F32)
    rest = weight - first
    second = rest.astype(BF16).astype(F32)
    lines = -(-4 * fanout // 8) * 8
    row = lax.broadcasted_iota(jnp.int32, (lines, count), 0)
    table = jnp.zeros((lines, count), F32)
    for number, part in enumerate([routes[...].astype(F32), first, second, rest - second]):
        for k in range(fanout):
            table = jnp.where(row == number * fanout + k, part[k : k + 1], table)
    table = jnp.concatenate([table, jnp.zeros((128 - lines, count), F32)], axis=0)
    columns = table.T.astype(BF16)
    message[:, width:] = columns
    meta[...] = columns


def build_message(tokens, routes, route_weight, ratio, clip):
    count, width = tokens.shape
    vmem = pl.BlockSpec(memory_space=pltpu.VMEM)
    return pl.pallas_call(
        functools.partial(message_kernel, routes.shape[1]),
        out_shape=[
            jax.ShapeDtypeStruct((count, width + 128), BF16),
            jax.ShapeDtypeStruct((count, 128), BF16),
        ],
        in_specs=[vmem] * 5,
        out_specs=[vmem] * 2,
        cost_estimate=pl.CostEstimate(flops=0, bytes_accessed=4 * count * width, transcendentals=0),
        name="ring_message",
    )(tokens, routes.T, route_weight.T, ratio[None], clip[None])


def order_kernel(plan, experts, capacity, scal, *refs):
    parts, mine, theirs = refs[:-2], refs[-2], refs[-1]
    shift = to_ring(scal[0], experts) - to_ring(scal[2], experts)
    width = mine.shape[1]
    for steps, part in zip(plan, parts):
        for at, step in enumerate(steps):
            place = slot_place((shift + step + 2 * experts) % experts, experts)
            there = pl.ds(pl.multiple_of(place * capacity, capacity), capacity)
            mine[there, :] = part[at * capacity : (at + 1) * capacity, :width]
            theirs[there, :] = part[at * capacity : (at + 1) * capacity, width:]


def ordered(plan, experts, capacity, scal, parts):
    vmem = pl.BlockSpec(memory_space=pltpu.VMEM)
    rows, width = experts * capacity, parts[0].shape[1] // 2
    return pl.pallas_call(
        functools.partial(order_kernel, plan, experts, capacity),
        out_shape=[jax.ShapeDtypeStruct((rows, width), BF16)] * 2,
        in_specs=[pl.BlockSpec(memory_space=pltpu.SMEM)] + [vmem] * len(parts),
        out_specs=[vmem] * 2,
        compiler_params=pltpu.CompilerParams(vmem_limit_bytes=VMEM_BYTES),
        cost_estimate=pl.CostEstimate(flops=0, bytes_accessed=8 * rows * width, transcendentals=0),
        name="hot_rows_ordered",
    )(scal, *parts)


def shadow_kernel(experts, scal, mine, theirs, hot_mine, hot_theirs, out):
    own = scal[0]
    taken = mine.shape[0]
    width = out.shape[1]
    gates = taken * experts * 2 // 3
    column = own * taken + lax.broadcasted_iota(jnp.int32, (taken, 1), 0)

    def product(first):
        columns = pl.ds(first, width)
        return dot(mine[...], hot_mine[:, columns], (1, 0)) + dot(theirs[...], hot_theirs[:, columns], (1, 0))

    @pl.when((own + 1) * taken <= gates)
    def _():
        out[...] = product(0)

    @pl.when(own * taken >= gates)
    def _():
        out[...] = product(width)

    @pl.when((own * taken < gates) & ((own + 1) * taken > gates))
    def _():
        out[...] = jnp.where(column < gates, product(0), product(width))


def shadow_gradient(experts, scal, mine, theirs, hot_mine, hot_theirs):
    taken, rows = mine.shape
    width = hot_mine.shape[1] // 2
    vmem = pl.BlockSpec(memory_space=pltpu.VMEM)
    return pl.pallas_call(
        functools.partial(shadow_kernel, experts),
        out_shape=jax.ShapeDtypeStruct((taken, width), F32),
        in_specs=[pl.BlockSpec(memory_space=pltpu.SMEM)] + [vmem] * 4,
        out_specs=vmem,
        compiler_params=pltpu.CompilerParams(vmem_limit_bytes=24 * 1024 * 1024),
        cost_estimate=pl.CostEstimate(
            flops=4 * taken * rows * width, bytes_accessed=4 * rows * width, transcendentals=0
        ),
        name="shadow_gradient",
    )(scal, mine, theirs, hot_mine, hot_theirs)


def on_device(
    tokens, cotangent, routes, route_weight, ratio_advantage, clip_mask, shadow_plan, gate_up, down
):
    experts = lax.axis_size("expert")
    tok_rows, width = tokens.shape
    fanout = routes.shape[1]
    units = down.shape[1]
    capacity = 2 * tok_rows * fanout // experts
    gate_up, down = gate_up[0], down[0]
    order = ring_order(experts)
    half = experts // 2

    def shift(block, step):
        pairs = [(order[i], order[(i + step) % experts]) for i in range(experts)]
        return lax.ppermute(block, "expert", pairs)

    def swap(block):
        return lax.ppermute(block, "dp", [(0, 1), (1, 0)])

    own = lax.axis_index("expert")
    hottest = shadow_plan[0]
    scal = jnp.stack([own, lax.axis_index("dp"), hottest]).astype(jnp.int32)
    message, meta = build_message(tokens, routes, route_weight, ratio_advantage, clip_mask)

    plan = distances(experts)
    mine, packs, hot, turned, late = [], [], [], [], []
    returned = {}
    up, below, held = [message, cotangent], [message, cotangent], [[message], [cotangent]]
    for number, steps in enumerate(plan):
        if number + 1 < half:
            up, below = [shift(part, 1) for part in up], [shift(part, -1) for part in below]
            following = [[up[0], below[0]], [up[1], below[1]]]
        elif number + 1 == half:
            following = [[shift(up[0], 1)], [shift(below[1], -1)]]
        if number > 1:
            sent, other = late[number - 2]
            held, other = lax.optimization_barrier((held, other))
            late[number - 2] = (sent, other)
        if number == half - 1:
            held, late[: half - 2] = lax.optimization_barrier((held, late[: half - 2]))
        (rows, pack, hot_rows), back, turn = run_step(
            steps,
            fanout,
            capacity,
            scal,
            *held,
            packs[0] if number == half else None,
            gate_up,
            down,
        )
        following[1], back = lax.optimization_barrier((following[1], back))
        if number + 1 < half:
            up, below = [[part[k] for part in following] for k in range(2)]
        sent = [shift(part, step) if step else part for step, part in zip(steps, back)]
        late.append((sent, swap(pack)))
        mine.append(rows)
        packs.append(pack)
        hot.append(hot_rows)
        turned += turn
        held = following
    (back_behind, back_ahead), other = late[half - 1]
    turned[-1], late[half - 2] = lax.optimization_barrier((turned[-1], late[half - 2]))

    taken = 3 * units // experts
    ring_hot = to_ring(hottest, experts)
    is_hot = own == hottest

    def chunk(distance):
        owner = from_ring((ring_hot + distance + experts) % experts, experts)
        parts = [lax.dynamic_slice_in_dim(part, owner * taken, taken, axis=0) for part in turned]
        return jnp.concatenate(parts, axis=1)

    far = chunk(half)
    lanes = far.shape[1] // 2
    around = [far[:, :lanes], far[:, lanes:]]
    around, other = lax.optimization_barrier((around, other))
    around = [shift(around[0], 1), shift(around[1], -1)]
    others = [part for _, part in late[: half - 1]] + [other, late[half][1]]
    expert_grad = expert_gradient(units, scal, mine, packs, others)
    chunks = [chunk(distance) for distance in range(1 - half, half)]
    (back_far,) = late[half][0]
    hot_mine, hot_theirs = ordered(plan, experts, capacity, scal, hot)
    for number in range(1, half):
        if number == 1:
            around, expert_grad, back_ahead, back_behind, back_far, chunks = (
                lax.optimization_barrier(
                    (around, expert_grad, back_ahead, back_behind, back_far, chunks)
                )
            )
            around = [jnp.concatenate([part, part], axis=1) for part in around]
        if number == half - 1:
            around, hot_mine, hot_theirs = lax.optimization_barrier((around, hot_mine, hot_theirs))
        ahead = jnp.where(is_hot, chunks[2 * half - 1 - number], around[0])
        behind = jnp.where(is_hot, chunks[number - 1], around[1])
        around = [shift(ahead, 1), shift(behind, -1)]
    hot_theirs = swap(hot_theirs)
    sent = [rows for rows, _ in late[: half - 1]] + [[back_behind, back_ahead], [back_far]]
    for steps, parts in zip(plan, sent):
        for step, part in zip(steps, parts):
            returned[step % experts] = part
    token_grad = combine(experts, fanout, capacity, scal, meta, [returned[d] for d in range(experts)])
    around, token_grad = lax.optimization_barrier((around, token_grad))
    away = (to_ring(own, experts) - ring_hot + experts) % experts
    lane = lax.broadcasted_iota(jnp.int32, far.shape, 1)
    reach = jnp.where(lane < lanes, half, half - 1)
    columns = jnp.where(
        away == 0, chunks[half - 1], jnp.where(away <= reach, around[0], around[1])
    )
    shadow_grad = shadow_gradient(
        experts, scal, columns, swap(columns), hot_mine, hot_theirs
    ).T
    return (token_grad, expert_grad, shadow_grad)


def solution(mesh):
    placed = (
        P(("group", "expert", "dp"), None),
        P(("group", "expert", "dp"), None),
        P(("group", "expert", "dp"), None),
        P(("group", "expert", "dp"), None),
        P(("group", "expert", "dp")),
        P(("group", "expert", "dp")),
        P("group"),
        P("expert", None, None),
        P("expert", None, None),
    )
    return jax.shard_map(
        on_device,
        mesh=mesh,
        in_specs=placed,
        out_specs=(
            P(("group", "expert", "dp"), None),
            P(("group", "expert"), "dp", None),
            P(("group", "dp"), "expert"),
        ),
        check_vma=False,
    )
```

```python
import functools

import jax
import jax.numpy as jnp
from jax import lax
from jax.experimental import pallas as pl
from jax.experimental.pallas import tpu as pltpu
from jax.sharding import PartitionSpec as P

BF16 = jnp.bfloat16
F32 = jnp.float32
VMEM_BYTES = 56 * 1024 * 1024


def snaked(experts):
    return experts <= 8


def to_ring(expert, experts):
    if not snaked(experts):
        return expert
    down = experts - 1 - (expert - 1) // 2
    return jnp.where(expert % 2 == 0, expert // 2, down)


def from_ring(place, experts):
    if not snaked(experts):
        return place
    return jnp.where(place < experts // 2, 2 * place, 2 * (experts - 1 - place) + 1)


def ring_order(experts):
    if not snaked(experts):
        return list(range(experts))
    return list(range(0, experts, 2)) + list(range(experts - 1, 0, -2))


def distances(experts):
    half = experts // 2
    return [[0]] + [[-step, step] for step in range(1, half)] + [[half]]


def slot_place(distance, experts):
    half = experts // 2
    near = jnp.where(distance < half, 2 * distance - 1, 2 * (experts - distance) - 2)
    near = jnp.where(distance == half, experts - 1, near)
    return jnp.where(distance == 0, experts - 2, near)


def dot(a, b, dims):
    return lax.dot_general(a, b, ((dims[:1], dims[1:]), ((), ())), preferred_element_type=F32)


def selection(table, expert, fanout, capacity):
    tokens = table.shape[1]
    hit = table[:fanout] == expert.astype(F32)
    named = jnp.sum(jnp.where(hit, 1.0, 0.0), axis=0, keepdims=True)
    parts = table[fanout : 4 * fanout]
    weights = parts[:fanout] + parts[fanout : 2 * fanout] + parts[2 * fanout :]
    weight = jnp.sum(jnp.where(hit, weights, 0.0), axis=0, keepdims=True)
    upto = lax.broadcasted_iota(jnp.int32, (tokens, tokens), 0) <= lax.broadcasted_iota(
        jnp.int32, (tokens, tokens), 1
    )
    upto = jnp.where(upto, 1.0, 0.0).astype(BF16)
    place = dot(jnp.broadcast_to(named, (8, tokens)).astype(BF16), upto, (1, 0))[:1]
    row = lax.broadcasted_iota(jnp.int32, (capacity, tokens), 0).astype(F32) + 1.0
    onehot = jnp.where((row == place) & (named > 0.5), 1.0, 0.0)
    return onehot, weight


def back_sections(capacity):
    return [capacity // 2] * 2


def step_kernel(steps, fanout, capacity, joined, scal, *refs):
    count = len(steps)
    messages, cotangents, refs = refs[:count], refs[count : 2 * count], refs[2 * count :]
    if joined:
        first, refs = refs[0], refs[1:]
    weights_gu, weights_down, mine, pack, hot = refs[:5]
    sections = len(back_sections(capacity)) if joined else count
    back, refs = refs[5 : 5 + sections], refs[5 + sections :]
    if len(refs) > 7:
        turned, refs = refs[0], refs[1:]
    else:
        turned = None
    rows_in, rows_cot, hot_in, hot_cot, gate_up, down, sems = refs
    own, half, hottest = scal[0], scal[1], scal[2]
    units, width = down.shape
    load_gu = pltpu.make_async_copy(weights_gu, gate_up, sems.at[0])
    load_down = pltpu.make_async_copy(weights_down, down, sems.at[1])
    load_gu.start()
    load_down.start()
    for at, (message, cotangent) in enumerate(zip(messages, cotangents)):
        rows = slice(at * capacity, (at + 1) * capacity)
        table = message[:, width:].astype(F32).T
        own_hot, own_weight = selection(table, own, fanout, capacity)
        all_hot, all_weight = selection(table, hottest, fanout, capacity)
        scale = jnp.concatenate(
            [
                jnp.sum(own_hot * own_weight, axis=1, keepdims=True),
                jnp.sum(all_hot * all_weight, axis=1, keepdims=True),
            ],
            axis=0,
        )
        onehot = jnp.concatenate([own_hot, all_hot], axis=0).astype(BF16)
        picked = dot(onehot, message[:, :width], (1, 0)).astype(BF16)
        rows_in[rows, :] = picked[:capacity]
        hot_in[rows, :] = picked[capacity:]
        picked = (scale * dot(onehot, cotangent[...], (1, 0))).astype(BF16)
        rows_cot[rows, :] = picked[:capacity]
        hot_cot[rows, :] = picked[capacity:]
    part = width // 2
    here = pl.ds(pl.multiple_of(half * part, part), part)
    there = pl.ds(pl.multiple_of((1 - half) * part, part), part)
    mine[:, :part] = rows_in[:, here]
    mine[:, part:] = rows_cot[:, here]
    pack[:, 3 * units : 3 * units + part] = rows_in[:, there]
    pack[:, 3 * units + part :] = rows_cot[:, there]
    hot[:, :part] = hot_in[:, here]
    hot[:, part:width] = hot_cot[:, here]
    hot[:, width : width + part] = hot_in[:, there]
    hot[:, width + part :] = hot_cot[:, there]
    load_gu.wait()
    projected = dot(rows_in[...], gate_up[...], (1, 0))
    gate_pre, up_pre = projected[:, :units], projected[:, units:]
    load_down.wait()
    hidden_grad = dot(rows_cot[...], down[...], (1, 1))
    sigmoid_gate = jax.nn.sigmoid(gate_pre)
    activation = gate_pre * sigmoid_gate
    gate_grad = hidden_grad * up_pre * sigmoid_gate * (1.0 + gate_pre * (1.0 - sigmoid_gate))
    pack[:, :units] = gate_grad.astype(BF16)
    pack[:, units : 2 * units] = (hidden_grad * activation).astype(BF16)
    pack[:, 2 * units : 3 * units] = (activation * up_pre).astype(BF16)
    input_rows = dot(pack[:, : 2 * units], gate_up[...], (1, 1)).astype(BF16)
    at = 0
    for part in back:
        part[...] = input_rows[at : at + part.shape[0]]
        at += part.shape[0]
    if turned is not None:
        grads = pack[:, : 3 * units]
        if joined:
            grads = jnp.concatenate([first[:, : 3 * units], grads], axis=0)
        turned[...] = grads.T


def run_step(steps, fanout, capacity, scal, messages, cotangents, first, gate_up, down):
    count, rows = len(steps), len(steps) * capacity
    units, width = down.shape
    vmem = pl.BlockSpec(memory_space=pltpu.VMEM)
    far = pl.BlockSpec(memory_space=pl.ANY)
    shapes = [(rows, width), (rows, 3 * units + width), (rows, 2 * width)]
    joined = first is not None
    sections = back_sections(capacity) if first is not None else [capacity] * count
    shapes += [(size, width) for size in sections]
    if joined or count > 1:
        shapes += [(3 * units, 2 * capacity)]
    firsts = [first] if joined else []
    out = pl.pallas_call(
        functools.partial(step_kernel, steps, fanout, capacity, joined),
        out_shape=[jax.ShapeDtypeStruct(shape, BF16) for shape in shapes],
        in_specs=[pl.BlockSpec(memory_space=pltpu.SMEM)] + [vmem] * (2 * count + len(firsts)) + [far] * 2,
        out_specs=[vmem] * len(shapes),
        scratch_shapes=[pltpu.VMEM((rows, width), BF16)] * 4
        + [
            pltpu.VMEM(gate_up.shape, BF16),
            pltpu.VMEM(down.shape, BF16),
            pltpu.SemaphoreType.DMA((2,)),
        ],
        compiler_params=pltpu.CompilerParams(vmem_limit_bytes=VMEM_BYTES),
        cost_estimate=pl.CostEstimate(
            flops=2 * 256 * 5 * width * units, bytes_accessed=3 * 2 * width * units, transcendentals=0
        ),
        name="expert_step",
    )(scal, *messages, *cotangents, *firsts, gate_up, down)
    return out[:3], out[3 : 3 + len(sections)], out[3 + len(sections) :]


def combine_kernel(experts, fanout, capacity, scal, meta, *refs):
    rows, out = refs[:-1], refs[-1]
    place = to_ring(scal[0], experts)
    table = meta[...].astype(F32).T
    picks = []
    for step in range(experts):
        expert = from_ring((place - step + experts) % experts, experts)
        picks.append(selection(table, expert, fanout, capacity)[0])
    onehot = jnp.concatenate(picks, axis=0).astype(BF16)
    out[...] = dot(onehot, jnp.concatenate([part[...] for part in rows], axis=0), (0, 0)).astype(BF16)


def combine(experts, fanout, capacity, scal, meta, rows):
    vmem = pl.BlockSpec(memory_space=pltpu.VMEM)
    tokens, width = meta.shape[0], rows[0].shape[1]
    return pl.pallas_call(
        functools.partial(combine_kernel, experts, fanout, capacity),
        out_shape=jax.ShapeDtypeStruct((tokens, width), BF16),
        in_specs=[pl.BlockSpec(memory_space=pltpu.SMEM)] + [vmem] * (len(rows) + 1),
        out_specs=vmem,
        compiler_params=pltpu.CompilerParams(vmem_limit_bytes=VMEM_BYTES),
        cost_estimate=pl.CostEstimate(
            flops=2 * experts * capacity * tokens * width, bytes_accessed=2 * experts * capacity * width, transcendentals=0
        ),
        name="token_sum",
    )(scal, meta, *rows)


def gradient_kernel(units, count, scal, *refs):
    ins, cots, grads = refs[: 2 * count], refs[2 * count : 4 * count], refs[4 * count : 6 * count]
    out = refs[6 * count]
    keep = scal[0] != scal[2]
    left = jnp.concatenate([ref[...] for ref in ins], axis=0)
    right = jnp.concatenate([ref[:, : 2 * units] for ref in grads], axis=0)
    out[0, :, : 2 * units] = jnp.where(keep, dot(left, right, (0, 0)), 0.0)
    left = jnp.concatenate([ref[...] for ref in cots], axis=0)
    right = jnp.concatenate([ref[:, 2 * units :] for ref in grads], axis=0)
    out[0, :, 2 * units :] = jnp.where(keep, dot(left, right, (0, 0)), 0.0)


def expert_gradient(units, scal, mine, packs, others):
    width, columns, count = mine[0].shape[1], 3 * units, len(mine)
    tile = 256
    tiles, skip = width // 2 // tile, columns // tile
    total = 2 * sum(part.shape[0] for part in mine)
    rows = mine + others

    def tiled(first):
        specs = [pl.BlockSpec((part.shape[0], tile), lambda i: (0, i + first)) for part in mine]
        return specs + [
            pl.BlockSpec((part.shape[0], tile), lambda i: (0, i + first + skip)) for part in others
        ]

    in_specs = [pl.BlockSpec(memory_space=pltpu.SMEM)] + tiled(0) + tiled(tiles)
    in_specs += [pl.BlockSpec((part.shape[0], columns), lambda i: (0, 0)) for part in packs + others]
    return pl.pallas_call(
        functools.partial(gradient_kernel, units, count),
        grid=(tiles,),
        out_shape=jax.ShapeDtypeStruct((1, width // 2, columns), F32),
        in_specs=in_specs,
        out_specs=pl.BlockSpec((1, tile, columns), lambda i: (0, i, 0)),
        compiler_params=pltpu.CompilerParams(vmem_limit_bytes=VMEM_BYTES),
        cost_estimate=pl.CostEstimate(
            flops=width * columns * total, bytes_accessed=3 * width * columns, transcendentals=0
        ),
        name="expert_gradient",
    )(scal, *rows, *rows, *packs, *others)


def message_kernel(fanout, tokens, routes, route_weight, ratio, clip, message, meta):
    count, width = tokens.shape
    message[:, :width] = tokens[...]
    weight = route_weight[...] * ratio[...] * clip[...].astype(F32)
    first = weight.astype(BF16).astype(F32)
    rest = weight - first
    second = rest.astype(BF16).astype(F32)
    lines = -(-4 * fanout // 8) * 8
    row = lax.broadcasted_iota(jnp.int32, (lines, count), 0)
    table = jnp.zeros((lines, count), F32)
    for number, part in enumerate([routes[...].astype(F32), first, second, rest - second]):
        for k in range(fanout):
            table = jnp.where(row == number * fanout + k, part[k : k + 1], table)
    table = jnp.concatenate([table, jnp.zeros((128 - lines, count), F32)], axis=0)
    columns = table.T.astype(BF16)
    message[:, width:] = columns
    meta[...] = columns


def build_message(tokens, routes, route_weight, ratio, clip):
    count, width = tokens.shape
    vmem = pl.BlockSpec(memory_space=pltpu.VMEM)
    return pl.pallas_call(
        functools.partial(message_kernel, routes.shape[1]),
        out_shape=[
            jax.ShapeDtypeStruct((count, width + 128), BF16),
            jax.ShapeDtypeStruct((count, 128), BF16),
        ],
        in_specs=[vmem] * 5,
        out_specs=[vmem] * 2,
        cost_estimate=pl.CostEstimate(flops=0, bytes_accessed=4 * count * width, transcendentals=0),
        name="ring_message",
    )(tokens, routes.T, route_weight.T, ratio[None], clip[None])


def order_kernel(plan, experts, capacity, scal, *refs):
    parts, mine, theirs = refs[:-2], refs[-2], refs[-1]
    shift = to_ring(scal[0], experts) - to_ring(scal[2], experts)
    width = mine.shape[1]
    for steps, part in zip(plan, parts):
        for at, step in enumerate(steps):
            place = slot_place((shift + step + 2 * experts) % experts, experts)
            there = pl.ds(pl.multiple_of(place * capacity, capacity), capacity)
            mine[there, :] = part[at * capacity : (at + 1) * capacity, :width]
            theirs[there, :] = part[at * capacity : (at + 1) * capacity, width:]


def ordered(plan, experts, capacity, scal, parts):
    vmem = pl.BlockSpec(memory_space=pltpu.VMEM)
    rows, width = experts * capacity, parts[0].shape[1] // 2
    return pl.pallas_call(
        functools.partial(order_kernel, plan, experts, capacity),
        out_shape=[jax.ShapeDtypeStruct((rows, width), BF16)] * 2,
        in_specs=[pl.BlockSpec(memory_space=pltpu.SMEM)] + [vmem] * len(parts),
        out_specs=[vmem] * 2,
        compiler_params=pltpu.CompilerParams(vmem_limit_bytes=VMEM_BYTES),
        cost_estimate=pl.CostEstimate(flops=0, bytes_accessed=8 * rows * width, transcendentals=0),
        name="hot_rows_ordered",
    )(scal, *parts)


def shadow_kernel(experts, scal, mine, theirs, hot_mine, hot_theirs, out):
    own = scal[0]
    taken = mine.shape[0]
    width = out.shape[1]
    gates = taken * experts * 2 // 3
    column = own * taken + lax.broadcasted_iota(jnp.int32, (taken, 1), 0)

    def product(first):
        columns = pl.ds(first, width)
        return dot(mine[...], hot_mine[:, columns], (1, 0)) + dot(theirs[...], hot_theirs[:, columns], (1, 0))

    @pl.when((own + 1) * taken <= gates)
    def _():
        out[...] = product(0)

    @pl.when(own * taken >= gates)
    def _():
        out[...] = product(width)

    @pl.when((own * taken < gates) & ((own + 1) * taken > gates))
    def _():
        out[...] = jnp.where(column < gates, product(0), product(width))


def shadow_gradient(experts, scal, mine, theirs, hot_mine, hot_theirs):
    taken, rows = mine.shape
    width = hot_mine.shape[1] // 2
    vmem = pl.BlockSpec(memory_space=pltpu.VMEM)
    return pl.pallas_call(
        functools.partial(shadow_kernel, experts),
        out_shape=jax.ShapeDtypeStruct((taken, width), F32),
        in_specs=[pl.BlockSpec(memory_space=pltpu.SMEM)] + [vmem] * 4,
        out_specs=vmem,
        compiler_params=pltpu.CompilerParams(vmem_limit_bytes=24 * 1024 * 1024),
        cost_estimate=pl.CostEstimate(
            flops=4 * taken * rows * width, bytes_accessed=4 * rows * width, transcendentals=0
        ),
        name="shadow_gradient",
    )(scal, mine, theirs, hot_mine, hot_theirs)


def on_device(
    tokens, cotangent, routes, route_weight, ratio_advantage, clip_mask, shadow_plan, gate_up, down
):
    experts = lax.axis_size("expert")
    tok_rows, width = tokens.shape
    fanout = routes.shape[1]
    units = down.shape[1]
    capacity = 2 * tok_rows * fanout // experts
    gate_up, down = gate_up[0], down[0]
    order = ring_order(experts)
    half = experts // 2

    def shift(block, step):
        pairs = [(order[i], order[(i + step) % experts]) for i in range(experts)]
        return lax.ppermute(block, "expert", pairs)

    def swap(block):
        return lax.ppermute(block, "dp", [(0, 1), (1, 0)])

    own = lax.axis_index("expert")
    hottest = shadow_plan[0]
    scal = jnp.stack([own, lax.axis_index("dp"), hottest]).astype(jnp.int32)
    message, meta = build_message(tokens, routes, route_weight, ratio_advantage, clip_mask)

    plan = distances(experts)
    mine, packs, hot, turned, late = [], [], [], [], []
    returned = {}
    up, below, held = [message, cotangent], [message, cotangent], [[message], [cotangent]]
    for number, steps in enumerate(plan):
        if number + 1 < half:
            up, below = [shift(part, 1) for part in up], [shift(part, -1) for part in below]
            following = [[up[0], below[0]], [up[1], below[1]]]
        elif number + 1 == half:
            following = [[shift(up[0], 1)], [shift(below[1], -1)]]
        if number > 2:
            sent, other = late[number - 3]
            held, other = lax.optimization_barrier((held, other))
            late[number - 3] = (sent, other)
        (rows, pack, hot_rows), back, turn = run_step(
            steps,
            fanout,
            capacity,
            scal,
            *held,
            packs[0] if number == half else None,
            gate_up,
            down,
        )
        following[1], back = lax.optimization_barrier((following[1], back))
        if number + 1 < half:
            up, below = [[part[k] for part in following] for k in range(2)]
        steps = steps if number < half else steps * len(back)
        sent = [shift(part, step) if step else part for step, part in zip(steps, back)]
        late.append((sent, swap(pack)))
        mine.append(rows)
        packs.append(pack)
        hot.append(hot_rows)
        turned += turn
        held = following
    (back_behind, back_ahead), other = late[half - 1]
    turned[-1], late[: half - 1] = lax.optimization_barrier((turned[-1], late[: half - 1]))

    taken = 3 * units // experts
    ring_hot = to_ring(hottest, experts)
    is_hot = own == hottest

    def chunk(distance):
        owner = from_ring((ring_hot + distance + experts) % experts, experts)
        parts = [lax.dynamic_slice_in_dim(part, owner * taken, taken, axis=0) for part in turned]
        return jnp.concatenate(parts, axis=1)

    far = chunk(half)
    lanes = far.shape[1] // 2
    around = [far[:, :lanes], far[:, lanes:]]
    around, other = lax.optimization_barrier((around, other))
    around = [shift(around[0], 1), shift(around[1], -1)]
    others = [part for _, part in late[: half - 1]] + [other, late[half][1]]
    expert_grad = expert_gradient(units, scal, mine, packs, others)
    chunks = [chunk(distance) for distance in range(1 - half, half)]
    back_far = list(late[half][0])
    hot_mine, hot_theirs = ordered(plan, experts, capacity, scal, hot)
    for number in range(1, half):
        if number == 1:
            around, expert_grad, back_ahead, back_behind, chunks = lax.optimization_barrier(
                (around, expert_grad, back_ahead, back_behind, chunks)
            )
            around = [jnp.concatenate([part, part], axis=1) for part in around]
        if number == 2:
            around, back_far[0] = lax.optimization_barrier((around, back_far[0]))
        if number == half - 1:
            around, back_far[1], hot_mine, hot_theirs = lax.optimization_barrier(
                (around, back_far[1], hot_mine, hot_theirs)
            )
        ahead = jnp.where(is_hot, chunks[2 * half - 1 - number], around[0])
        behind = jnp.where(is_hot, chunks[number - 1], around[1])
        around = [shift(ahead, 1), shift(behind, -1)]
    hot_theirs = swap(hot_theirs)
    sent = [rows for rows, _ in late[: half - 1]] + [[back_behind, back_ahead]]
    for steps, parts in zip(plan, sent):
        for step, part in zip(steps, parts):
            returned[step % experts] = [part]
    returned[half] = back_far
    rows = [part for distance in range(experts) for part in returned[distance]]
    token_grad = combine(experts, fanout, capacity, scal, meta, rows)
    away = (to_ring(own, experts) - ring_hot + experts) % experts
    lane = lax.broadcasted_iota(jnp.int32, far.shape, 1)
    reach = jnp.where(lane < lanes, half, half - 1)
    columns = jnp.where(
        away == 0, chunks[half - 1], jnp.where(away <= reach, around[0], around[1])
    )
    shadow_grad = shadow_gradient(
        experts, scal, columns, swap(columns), hot_mine, hot_theirs
    ).T
    return (token_grad, expert_grad, shadow_grad)


def solution(mesh):
    placed = (
        P(("group", "expert", "dp"), None),
        P(("group", "expert", "dp"), None),
        P(("group", "expert", "dp"), None),
        P(("group", "expert", "dp"), None),
        P(("group", "expert", "dp")),
        P(("group", "expert", "dp")),
        P("group"),
        P("expert", None, None),
        P("expert", None, None),
    )
    return jax.shard_map(
        on_device,
        mesh=mesh,
        in_specs=placed,
        out_specs=(
            P(("group", "expert", "dp"), None),
            P(("group", "expert"), "dp", None),
            P(("group", "dp"), "expert"),
        ),
        check_vma=False,
    )
```

```python
import functools

import jax
import jax.numpy as jnp
from jax import lax
from jax.experimental import pallas as pl
from jax.experimental.pallas import tpu as pltpu
from jax.sharding import PartitionSpec as P

BF16 = jnp.bfloat16
F32 = jnp.float32
VMEM_BYTES = 56 * 1024 * 1024


def snaked(experts):
    return experts <= 8


def to_ring(expert, experts):
    if not snaked(experts):
        return expert
    down = experts - 1 - (expert - 1) // 2
    return jnp.where(expert % 2 == 0, expert // 2, down)


def from_ring(place, experts):
    if not snaked(experts):
        return place
    return jnp.where(place < experts // 2, 2 * place, 2 * (experts - 1 - place) + 1)


def ring_order(experts):
    if not snaked(experts):
        return list(range(experts))
    return list(range(0, experts, 2)) + list(range(experts - 1, 0, -2))


def distances(experts):
    half = experts // 2
    return [[0]] + [[-step, step] for step in range(1, half)] + [[half]]


def slot_place(distance, experts):
    half = experts // 2
    near = jnp.where(distance < half, 2 * distance - 1, 2 * (experts - distance) - 2)
    near = jnp.where(distance == half, experts - 1, near)
    return jnp.where(distance == 0, experts - 2, near)


def dot(a, b, dims):
    return lax.dot_general(a, b, ((dims[:1], dims[1:]), ((), ())), preferred_element_type=F32)


def selection(table, expert, fanout, capacity):
    tokens = table.shape[1]
    hit = table[:fanout] == expert.astype(F32)
    named = jnp.sum(jnp.where(hit, 1.0, 0.0), axis=0, keepdims=True)
    parts = table[fanout : 4 * fanout]
    weights = parts[:fanout] + parts[fanout : 2 * fanout] + parts[2 * fanout :]
    weight = jnp.sum(jnp.where(hit, weights, 0.0), axis=0, keepdims=True)
    upto = lax.broadcasted_iota(jnp.int32, (tokens, tokens), 0) <= lax.broadcasted_iota(
        jnp.int32, (tokens, tokens), 1
    )
    upto = jnp.where(upto, 1.0, 0.0).astype(BF16)
    place = dot(jnp.broadcast_to(named, (8, tokens)).astype(BF16), upto, (1, 0))[:1]
    row = lax.broadcasted_iota(jnp.int32, (capacity, tokens), 0).astype(F32) + 1.0
    onehot = jnp.where((row == place) & (named > 0.5), 1.0, 0.0)
    return onehot, weight


def step_kernel(steps, fanout, capacity, joined, scal, *refs):
    count = len(steps)
    messages, cotangents, refs = refs[:count], refs[count : 2 * count], refs[2 * count :]
    if joined:
        first, refs = refs[0], refs[1:]
    weights_gu, weights_down, mine, pack, hot = refs[:5]
    back, refs = refs[5 : 5 + count], refs[5 + count :]
    if len(refs) > 7:
        turned, refs = refs[0], refs[1:]
    else:
        turned = None
    rows_in, rows_cot, hot_in, hot_cot, gate_up, down, sems = refs
    own, half, hottest = scal[0], scal[1], scal[2]
    units, width = down.shape
    load_gu = pltpu.make_async_copy(weights_gu, gate_up, sems.at[0])
    load_down = pltpu.make_async_copy(weights_down, down, sems.at[1])
    load_gu.start()
    load_down.start()
    for at, (message, cotangent) in enumerate(zip(messages, cotangents)):
        rows = slice(at * capacity, (at + 1) * capacity)
        table = message[:, width:].astype(F32).T
        own_hot, own_weight = selection(table, own, fanout, capacity)
        all_hot, all_weight = selection(table, hottest, fanout, capacity)
        scale = jnp.concatenate(
            [
                jnp.sum(own_hot * own_weight, axis=1, keepdims=True),
                jnp.sum(all_hot * all_weight, axis=1, keepdims=True),
            ],
            axis=0,
        )
        onehot = jnp.concatenate([own_hot, all_hot], axis=0).astype(BF16)
        picked = dot(onehot, message[:, :width], (1, 0)).astype(BF16)
        rows_in[rows, :] = picked[:capacity]
        hot_in[rows, :] = picked[capacity:]
        picked = (scale * dot(onehot, cotangent[...], (1, 0))).astype(BF16)
        rows_cot[rows, :] = picked[:capacity]
        hot_cot[rows, :] = picked[capacity:]
    part = width // 2
    here = pl.ds(pl.multiple_of(half * part, part), part)
    there = pl.ds(pl.multiple_of((1 - half) * part, part), part)
    mine[:, :part] = rows_in[:, here]
    mine[:, part:] = rows_cot[:, here]
    pack[:, 3 * units : 3 * units + part] = rows_in[:, there]
    pack[:, 3 * units + part :] = rows_cot[:, there]
    hot[:, :part] = hot_in[:, here]
    hot[:, part:width] = hot_cot[:, here]
    hot[:, width : width + part] = hot_in[:, there]
    hot[:, width + part :] = hot_cot[:, there]
    load_gu.wait()
    projected = dot(rows_in[...], gate_up[...], (1, 0))
    gate_pre, up_pre = projected[:, :units], projected[:, units:]
    load_down.wait()
    hidden_grad = dot(rows_cot[...], down[...], (1, 1))
    sigmoid_gate = jax.nn.sigmoid(gate_pre)
    activation = gate_pre * sigmoid_gate
    gate_grad = hidden_grad * up_pre * sigmoid_gate * (1.0 + gate_pre * (1.0 - sigmoid_gate))
    pack[:, :units] = gate_grad.astype(BF16)
    pack[:, units : 2 * units] = (hidden_grad * activation).astype(BF16)
    pack[:, 2 * units : 3 * units] = (activation * up_pre).astype(BF16)
    input_rows = dot(pack[:, : 2 * units], gate_up[...], (1, 1)).astype(BF16)
    for at, part in enumerate(back):
        part[...] = input_rows[at * part.shape[0] : (at + 1) * part.shape[0]]
    if turned is not None:
        grads = pack[:, : 3 * units]
        if joined:
            grads = jnp.concatenate([first[:, : 3 * units], grads], axis=0)
        turned[...] = grads.T


def run_step(steps, fanout, capacity, scal, messages, cotangents, first, gate_up, down):
    count, rows = len(steps), len(steps) * capacity
    units, width = down.shape
    vmem = pl.BlockSpec(memory_space=pltpu.VMEM)
    far = pl.BlockSpec(memory_space=pl.ANY)
    shapes = [(rows, width), (rows, 3 * units + width), (rows, 2 * width)]
    joined = first is not None
    shapes += [(capacity, width)] * count
    if joined or count > 1:
        shapes += [(3 * units, 2 * capacity)]
    firsts = [first] if joined else []
    out = pl.pallas_call(
        functools.partial(step_kernel, steps, fanout, capacity, joined),
        out_shape=[jax.ShapeDtypeStruct(shape, BF16) for shape in shapes],
        in_specs=[pl.BlockSpec(memory_space=pltpu.SMEM)] + [vmem] * (2 * count + len(firsts)) + [far] * 2,
        out_specs=[vmem] * len(shapes),
        scratch_shapes=[pltpu.VMEM((rows, width), BF16)] * 4
        + [
            pltpu.VMEM(gate_up.shape, BF16),
            pltpu.VMEM(down.shape, BF16),
            pltpu.SemaphoreType.DMA((2,)),
        ],
        compiler_params=pltpu.CompilerParams(vmem_limit_bytes=VMEM_BYTES),
        cost_estimate=pl.CostEstimate(
            flops=2 * 256 * 5 * width * units, bytes_accessed=3 * 2 * width * units, transcendentals=0
        ),
        name="expert_step",
    )(scal, *messages, *cotangents, *firsts, gate_up, down)
    return out[:3], out[3 : 3 + count], out[3 + count :]


def combine_kernel(experts, fanout, capacity, scal, meta, *refs):
    rows, out = refs[:-1], refs[-1]
    place = to_ring(scal[0], experts)
    table = meta[...].astype(F32).T
    picks = []
    for step in range(experts):
        expert = from_ring((place - step + experts) % experts, experts)
        picks.append(selection(table, expert, fanout, capacity)[0])
    onehot = jnp.concatenate(picks, axis=0).astype(BF16)
    out[...] = dot(onehot, jnp.concatenate([part[...] for part in rows], axis=0), (0, 0)).astype(BF16)


def combine(experts, fanout, capacity, scal, meta, rows):
    vmem = pl.BlockSpec(memory_space=pltpu.VMEM)
    tokens, width = meta.shape[0], rows[0].shape[1]
    return pl.pallas_call(
        functools.partial(combine_kernel, experts, fanout, capacity),
        out_shape=jax.ShapeDtypeStruct((tokens, width), BF16),
        in_specs=[pl.BlockSpec(memory_space=pltpu.SMEM)] + [vmem] * (len(rows) + 1),
        out_specs=vmem,
        compiler_params=pltpu.CompilerParams(vmem_limit_bytes=VMEM_BYTES),
        cost_estimate=pl.CostEstimate(
            flops=2 * experts * capacity * tokens * width, bytes_accessed=2 * experts * capacity * width, transcendentals=0
        ),
        name="token_sum",
    )(scal, meta, *rows)


def gradient_kernel(units, count, scal, *refs):
    ins, cots, grads = refs[: 2 * count], refs[2 * count : 4 * count], refs[4 * count : 6 * count]
    out = refs[6 * count]
    keep = scal[0] != scal[2]
    left = jnp.concatenate([ref[...] for ref in ins], axis=0)
    right = jnp.concatenate([ref[:, : 2 * units] for ref in grads], axis=0)
    out[0, :, : 2 * units] = jnp.where(keep, dot(left, right, (0, 0)), 0.0)
    left = jnp.concatenate([ref[...] for ref in cots], axis=0)
    right = jnp.concatenate([ref[:, 2 * units :] for ref in grads], axis=0)
    out[0, :, 2 * units :] = jnp.where(keep, dot(left, right, (0, 0)), 0.0)


def expert_gradient(units, scal, mine, packs, others):
    width, columns, count = mine[0].shape[1], 3 * units, len(mine)
    tile = 256
    tiles, skip = width // 2 // tile, columns // tile
    total = 2 * sum(part.shape[0] for part in mine)
    rows = mine + others

    def tiled(first):
        specs = [pl.BlockSpec((part.shape[0], tile), lambda i: (0, i + first)) for part in mine]
        return specs + [
            pl.BlockSpec((part.shape[0], tile), lambda i: (0, i + first + skip)) for part in others
        ]

    in_specs = [pl.BlockSpec(memory_space=pltpu.SMEM)] + tiled(0) + tiled(tiles)
    in_specs += [pl.BlockSpec((part.shape[0], columns), lambda i: (0, 0)) for part in packs + others]
    return pl.pallas_call(
        functools.partial(gradient_kernel, units, count),
        grid=(tiles,),
        out_shape=jax.ShapeDtypeStruct((1, width // 2, columns), F32),
        in_specs=in_specs,
        out_specs=pl.BlockSpec((1, tile, columns), lambda i: (0, i, 0)),
        compiler_params=pltpu.CompilerParams(vmem_limit_bytes=VMEM_BYTES),
        cost_estimate=pl.CostEstimate(
            flops=width * columns * total, bytes_accessed=3 * width * columns, transcendentals=0
        ),
        name="expert_gradient",
    )(scal, *rows, *rows, *packs, *others)


def message_kernel(fanout, tokens, routes, route_weight, ratio, clip, message, meta):
    count, width = tokens.shape
    message[:, :width] = tokens[...]
    weight = route_weight[...] * ratio[...] * clip[...].astype(F32)
    first = weight.astype(BF16).astype(F32)
    rest = weight - first
    second = rest.astype(BF16).astype(F32)
    lines = -(-4 * fanout // 8) * 8
    row = lax.broadcasted_iota(jnp.int32, (lines, count), 0)
    table = jnp.zeros((lines, count), F32)
    for number, part in enumerate([routes[...].astype(F32), first, second, rest - second]):
        for k in range(fanout):
            table = jnp.where(row == number * fanout + k, part[k : k + 1], table)
    table = jnp.concatenate([table, jnp.zeros((128 - lines, count), F32)], axis=0)
    columns = table.T.astype(BF16)
    message[:, width:] = columns
    meta[...] = columns


def build_message(tokens, routes, route_weight, ratio, clip):
    count, width = tokens.shape
    vmem = pl.BlockSpec(memory_space=pltpu.VMEM)
    return pl.pallas_call(
        functools.partial(message_kernel, routes.shape[1]),
        out_shape=[
            jax.ShapeDtypeStruct((count, width + 128), BF16),
            jax.ShapeDtypeStruct((count, 128), BF16),
        ],
        in_specs=[vmem] * 5,
        out_specs=[vmem] * 2,
        cost_estimate=pl.CostEstimate(flops=0, bytes_accessed=4 * count * width, transcendentals=0),
        name="ring_message",
    )(tokens, routes.T, route_weight.T, ratio[None], clip[None])


def order_kernel(plan, experts, capacity, scal, *refs):
    parts, mine, theirs = refs[:-2], refs[-2], refs[-1]
    shift = to_ring(scal[0], experts) - to_ring(scal[2], experts)
    width = mine.shape[1]
    for steps, part in zip(plan, parts):
        for at, step in enumerate(steps):
            place = slot_place((shift + step + 2 * experts) % experts, experts)
            there = pl.ds(pl.multiple_of(place * capacity, capacity), capacity)
            mine[there, :] = part[at * capacity : (at + 1) * capacity, :width]
            theirs[there, :] = part[at * capacity : (at + 1) * capacity, width:]


def ordered(plan, experts, capacity, scal, parts):
    vmem = pl.BlockSpec(memory_space=pltpu.VMEM)
    rows, width = experts * capacity, parts[0].shape[1] // 2
    return pl.pallas_call(
        functools.partial(order_kernel, plan, experts, capacity),
        out_shape=[jax.ShapeDtypeStruct((rows, width), BF16)] * 2,
        in_specs=[pl.BlockSpec(memory_space=pltpu.SMEM)] + [vmem] * len(parts),
        out_specs=[vmem] * 2,
        compiler_params=pltpu.CompilerParams(vmem_limit_bytes=VMEM_BYTES),
        cost_estimate=pl.CostEstimate(flops=0, bytes_accessed=8 * rows * width, transcendentals=0),
        name="hot_rows_ordered",
    )(scal, *parts)


def shadow_kernel(experts, scal, mine, theirs, hot_mine, hot_theirs, out):
    own = scal[0]
    taken = mine.shape[0]
    width = out.shape[1]
    gates = taken * experts * 2 // 3
    column = own * taken + lax.broadcasted_iota(jnp.int32, (taken, 1), 0)

    def product(first):
        columns = pl.ds(first, width)
        return dot(mine[...], hot_mine[:, columns], (1, 0)) + dot(theirs[...], hot_theirs[:, columns], (1, 0))

    @pl.when((own + 1) * taken <= gates)
    def _():
        out[...] = product(0)

    @pl.when(own * taken >= gates)
    def _():
        out[...] = product(width)

    @pl.when((own * taken < gates) & ((own + 1) * taken > gates))
    def _():
        out[...] = jnp.where(column < gates, product(0), product(width))


def shadow_gradient(experts, scal, mine, theirs, hot_mine, hot_theirs):
    taken, rows = mine.shape
    width = hot_mine.shape[1] // 2
    vmem = pl.BlockSpec(memory_space=pltpu.VMEM)
    return pl.pallas_call(
        functools.partial(shadow_kernel, experts),
        out_shape=jax.ShapeDtypeStruct((taken, width), F32),
        in_specs=[pl.BlockSpec(memory_space=pltpu.SMEM)] + [vmem] * 4,
        out_specs=vmem,
        compiler_params=pltpu.CompilerParams(vmem_limit_bytes=24 * 1024 * 1024),
        cost_estimate=pl.CostEstimate(
            flops=4 * taken * rows * width, bytes_accessed=4 * rows * width, transcendentals=0
        ),
        name="shadow_gradient",
    )(scal, mine, theirs, hot_mine, hot_theirs)


def on_device(
    tokens, cotangent, routes, route_weight, ratio_advantage, clip_mask, shadow_plan, gate_up, down
):
    experts = lax.axis_size("expert")
    tok_rows, width = tokens.shape
    fanout = routes.shape[1]
    units = down.shape[1]
    capacity = 2 * tok_rows * fanout // experts
    gate_up, down = gate_up[0], down[0]
    order = ring_order(experts)
    half = experts // 2

    def shift(block, step):
        pairs = [(order[i], order[(i + step) % experts]) for i in range(experts)]
        return lax.ppermute(block, "expert", pairs)

    def swap(block):
        return lax.ppermute(block, "dp", [(0, 1), (1, 0)])

    own = lax.axis_index("expert")
    hottest = shadow_plan[0]
    scal = jnp.stack([own, lax.axis_index("dp"), hottest]).astype(jnp.int32)
    message, meta = build_message(tokens, routes, route_weight, ratio_advantage, clip_mask)

    plan = distances(experts)
    mine, packs, hot, turned, late = [], [], [], [], []
    returned = {}
    up, below, held = [message, cotangent], [message, cotangent], [[message], [cotangent]]
    for number, steps in enumerate(plan):
        if number + 1 < half:
            up, below = [shift(part, 1) for part in up], [shift(part, -1) for part in below]
            following = [[up[0], below[0]], [up[1], below[1]]]
        elif number + 1 == half:
            following = [[shift(up[0], 1)], [shift(below[1], -1)]]
        if number > 1:
            sent, other = late[number - 2]
            held, other = lax.optimization_barrier((held, other))
            late[number - 2] = (sent, other)
        if number == half - 1:
            held, late[: half - 2] = lax.optimization_barrier((held, late[: half - 2]))
        (rows, pack, hot_rows), back, turn = run_step(
            steps,
            fanout,
            capacity,
            scal,
            *held,
            packs[0] if number == half else None,
            gate_up,
            down,
        )
        following[1], back = lax.optimization_barrier((following[1], back))
        if number + 1 < half:
            up, below = [[part[k] for part in following] for k in range(2)]
        sent = [shift(part, step) if step else part for step, part in zip(steps, back)]
        late.append((sent, swap(pack)))
        mine.append(rows)
        packs.append(pack)
        hot.append(hot_rows)
        turned += turn
        held = following
    (back_behind, back_ahead), other = late[half - 1]
    turned[-1], late[half - 2] = lax.optimization_barrier((turned[-1], late[half - 2]))

    taken = 3 * units // experts
    ring_hot = to_ring(hottest, experts)
    is_hot = own == hottest

    def chunk(distance):
        owner = from_ring((ring_hot + distance + experts) % experts, experts)
        parts = [lax.dynamic_slice_in_dim(part, owner * taken, taken, axis=0) for part in turned]
        return jnp.concatenate(parts, axis=1)

    lanes = experts * capacity // 2

    def halves(distance):
        columns = chunk(distance)
        return [columns[:, :lanes], columns[:, lanes:]]

    hot_mine, hot_theirs = ordered(plan, experts, capacity, scal, hot)
    far = halves(half)
    far, other, hot_mine, hot_theirs = lax.optimization_barrier((far, other, hot_mine, hot_theirs))
    hot_theirs = swap(hot_theirs)
    far = [shift(far[0], 1), shift(far[1], -1)]
    others = [part for _, part in late[: half - 1]] + [other, late[half][1]]
    expert_grad = expert_gradient(units, scal, mine, packs, others)
    chunks = {distance: halves(distance) for distance in range(1 - half, half)}
    (back_far,) = late[half][0]
    far, expert_grad, back_ahead, back_behind, back_far, chunks = lax.optimization_barrier(
        (far, expert_grad, back_ahead, back_behind, back_far, chunks)
    )
    ahead, behind = [far[0], None], [None, far[1]]

    def onward(kept, received, step):
        return shift(kept if received is None else jnp.where(is_hot, kept, received), step)

    for number in range(1, half):
        for k in range(2):
            ahead[k] = onward(chunks[half - number][k], ahead[k], 1)
            behind[k] = onward(chunks[number - half][k], behind[k], -1)
    sent = [rows for rows, _ in late[: half - 1]] + [[back_behind, back_ahead], [back_far]]
    for steps, parts in zip(plan, sent):
        for step, part in zip(steps, parts):
            returned[step % experts] = part
    token_grad = combine(experts, fanout, capacity, scal, meta, [returned[d] for d in range(experts)])
    ahead, behind, token_grad = lax.optimization_barrier((ahead, behind, token_grad))
    away = (to_ring(own, experts) - ring_hot + experts) % experts
    columns = [
        jnp.where(away == 0, chunks[0][k], jnp.where(away <= half - k, ahead[k], behind[k]))
        for k in range(2)
    ]
    columns = jnp.concatenate(columns, axis=1)
    shadow_grad = shadow_gradient(
        experts, scal, columns, swap(columns), hot_mine, hot_theirs
    ).T
    return (token_grad, expert_grad, shadow_grad)


def solution(mesh):
    placed = (
        P(("group", "expert", "dp"), None),
        P(("group", "expert", "dp"), None),
        P(("group", "expert", "dp"), None),
        P(("group", "expert", "dp"), None),
        P(("group", "expert", "dp")),
        P(("group", "expert", "dp")),
        P("group"),
        P("expert", None, None),
        P("expert", None, None),
    )
    return jax.shard_map(
        on_device,
        mesh=mesh,
        in_specs=placed,
        out_specs=(
            P(("group", "expert", "dp"), None),
            P(("group", "expert"), "dp", None),
            P(("group", "dp"), "expert"),
        ),
        check_vma=False,
    )
```

```python
import functools

import jax
import jax.numpy as jnp
from jax import lax
from jax.experimental import pallas as pl
from jax.experimental.pallas import tpu as pltpu
from jax.sharding import PartitionSpec as P

BF16 = jnp.bfloat16
F32 = jnp.float32
VMEM_BYTES = 56 * 1024 * 1024


def snaked(experts):
    return experts <= 8


def to_ring(expert, experts):
    if not snaked(experts):
        return expert
    down = experts - 1 - (expert - 1) // 2
    return jnp.where(expert % 2 == 0, expert // 2, down)


def from_ring(place, experts):
    if not snaked(experts):
        return place
    return jnp.where(place < experts // 2, 2 * place, 2 * (experts - 1 - place) + 1)


def ring_order(experts):
    if not snaked(experts):
        return list(range(experts))
    return list(range(0, experts, 2)) + list(range(experts - 1, 0, -2))


def distances(experts):
    half = experts // 2
    return [[0]] + [[-step, step] for step in range(1, half)] + [[half]]


def slot_place(distance, experts):
    half = experts // 2
    near = jnp.where(distance < half, 2 * distance - 1, 2 * (experts - distance) - 2)
    near = jnp.where(distance == half, experts - 1, near)
    return jnp.where(distance == 0, experts - 2, near)


def dot(a, b, dims):
    return lax.dot_general(a, b, ((dims[:1], dims[1:]), ((), ())), preferred_element_type=F32)


def selection(table, expert, fanout, capacity):
    tokens = table.shape[1]
    hit = table[:fanout] == expert.astype(F32)
    named = jnp.sum(jnp.where(hit, 1.0, 0.0), axis=0, keepdims=True)
    parts = table[fanout : 4 * fanout]
    weights = parts[:fanout] + parts[fanout : 2 * fanout] + parts[2 * fanout :]
    weight = jnp.sum(jnp.where(hit, weights, 0.0), axis=0, keepdims=True)
    upto = lax.broadcasted_iota(jnp.int32, (tokens, tokens), 0) <= lax.broadcasted_iota(
        jnp.int32, (tokens, tokens), 1
    )
    upto = jnp.where(upto, 1.0, 0.0).astype(BF16)
    place = dot(jnp.broadcast_to(named, (8, tokens)).astype(BF16), upto, (1, 0))[:1]
    row = lax.broadcasted_iota(jnp.int32, (capacity, tokens), 0).astype(F32) + 1.0
    onehot = jnp.where((row == place) & (named > 0.5), 1.0, 0.0)
    return onehot, weight


def step_kernel(steps, fanout, capacity, joined, scal, *refs):
    count = len(steps)
    messages, cotangents, refs = refs[:count], refs[count : 2 * count], refs[2 * count :]
    if joined:
        first, refs = refs[0], refs[1:]
    weights_gu, weights_down, mine, pack, hot = refs[:5]
    back, refs = refs[5 : 5 + count], refs[5 + count :]
    if len(refs) > 7:
        turned, refs = refs[0], refs[1:]
    else:
        turned = None
    rows_in, rows_cot, hot_in, hot_cot, gate_up, down, sems = refs
    own, half, hottest = scal[0], scal[1], scal[2]
    units, width = down.shape
    load_gu = pltpu.make_async_copy(weights_gu, gate_up, sems.at[0])
    load_down = pltpu.make_async_copy(weights_down, down, sems.at[1])
    load_gu.start()
    load_down.start()
    for at, (message, cotangent) in enumerate(zip(messages, cotangents)):
        rows = slice(at * capacity, (at + 1) * capacity)
        table = message[:, width:].astype(F32).T
        own_hot, own_weight = selection(table, own, fanout, capacity)
        all_hot, all_weight = selection(table, hottest, fanout, capacity)
        scale = jnp.concatenate(
            [
                jnp.sum(own_hot * own_weight, axis=1, keepdims=True),
                jnp.sum(all_hot * all_weight, axis=1, keepdims=True),
            ],
            axis=0,
        )
        onehot = jnp.concatenate([own_hot, all_hot], axis=0).astype(BF16)
        picked = dot(onehot, message[:, :width], (1, 0)).astype(BF16)
        rows_in[rows, :] = picked[:capacity]
        hot_in[rows, :] = picked[capacity:]
        picked = (scale * dot(onehot, cotangent[...], (1, 0))).astype(BF16)
        rows_cot[rows, :] = picked[:capacity]
        hot_cot[rows, :] = picked[capacity:]
    part = width // 2
    here = pl.ds(pl.multiple_of(half * part, part), part)
    there = pl.ds(pl.multiple_of((1 - half) * part, part), part)
    mine[:, :part] = rows_in[:, here]
    mine[:, part:] = rows_cot[:, here]
    pack[:, 3 * units : 3 * units + part] = rows_in[:, there]
    pack[:, 3 * units + part :] = rows_cot[:, there]
    hot[:, :part] = hot_in[:, here]
    hot[:, part:width] = hot_cot[:, here]
    hot[:, width : width + part] = hot_in[:, there]
    hot[:, width + part :] = hot_cot[:, there]
    load_gu.wait()
    projected = dot(rows_in[...], gate_up[...], (1, 0))
    gate_pre, up_pre = projected[:, :units], projected[:, units:]
    load_down.wait()
    hidden_grad = dot(rows_cot[...], down[...], (1, 1))
    sigmoid_gate = jax.nn.sigmoid(gate_pre)
    activation = gate_pre * sigmoid_gate
    gate_grad = hidden_grad * up_pre * sigmoid_gate * (1.0 + gate_pre * (1.0 - sigmoid_gate))
    pack[:, :units] = gate_grad.astype(BF16)
    pack[:, units : 2 * units] = (hidden_grad * activation).astype(BF16)
    pack[:, 2 * units : 3 * units] = (activation * up_pre).astype(BF16)
    input_rows = dot(pack[:, : 2 * units], gate_up[...], (1, 1)).astype(BF16)
    for at, part in enumerate(back):
        part[...] = input_rows[at * part.shape[0] : (at + 1) * part.shape[0]]
    if turned is not None:
        grads = pack[:, : 3 * units]
        if joined:
            grads = jnp.concatenate([first[:, : 3 * units], grads], axis=0)
        turned[...] = grads.T


def run_step(steps, fanout, capacity, scal, messages, cotangents, first, gate_up, down):
    count, rows = len(steps), len(steps) * capacity
    units, width = down.shape
    vmem = pl.BlockSpec(memory_space=pltpu.VMEM)
    far = pl.BlockSpec(memory_space=pl.ANY)
    shapes = [(rows, width), (rows, 3 * units + width), (rows, 2 * width)]
    joined = first is not None
    shapes += [(capacity, width)] * count
    if joined or count > 1:
        shapes += [(3 * units, 2 * capacity)]
    firsts = [first] if joined else []
    out = pl.pallas_call(
        functools.partial(step_kernel, steps, fanout, capacity, joined),
        out_shape=[jax.ShapeDtypeStruct(shape, BF16) for shape in shapes],
        in_specs=[pl.BlockSpec(memory_space=pltpu.SMEM)] + [vmem] * (2 * count + len(firsts)) + [far] * 2,
        out_specs=[vmem] * len(shapes),
        scratch_shapes=[pltpu.VMEM((rows, width), BF16)] * 4
        + [
            pltpu.VMEM(gate_up.shape, BF16),
            pltpu.VMEM(down.shape, BF16),
            pltpu.SemaphoreType.DMA((2,)),
        ],
        compiler_params=pltpu.CompilerParams(vmem_limit_bytes=VMEM_BYTES),
        cost_estimate=pl.CostEstimate(
            flops=2 * 256 * 5 * width * units, bytes_accessed=3 * 2 * width * units, transcendentals=0
        ),
        name="expert_step",
    )(scal, *messages, *cotangents, *firsts, gate_up, down)
    return out[:3], out[3 : 3 + count], out[3 + count :]


def combine_kernel(experts, fanout, capacity, scal, meta, *refs):
    rows, out = refs[:-1], refs[-1]
    place = to_ring(scal[0], experts)
    table = meta[...].astype(F32).T
    picks = []
    for step in range(experts):
        expert = from_ring((place - step + experts) % experts, experts)
        picks.append(selection(table, expert, fanout, capacity)[0])
    onehot = jnp.concatenate(picks, axis=0).astype(BF16)
    out[...] = dot(onehot, jnp.concatenate([part[...] for part in rows], axis=0), (0, 0)).astype(BF16)


def combine(experts, fanout, capacity, scal, meta, rows):
    vmem = pl.BlockSpec(memory_space=pltpu.VMEM)
    tokens, width = meta.shape[0], rows[0].shape[1]
    return pl.pallas_call(
        functools.partial(combine_kernel, experts, fanout, capacity),
        out_shape=jax.ShapeDtypeStruct((tokens, width), BF16),
        in_specs=[pl.BlockSpec(memory_space=pltpu.SMEM)] + [vmem] * (len(rows) + 1),
        out_specs=vmem,
        compiler_params=pltpu.CompilerParams(vmem_limit_bytes=VMEM_BYTES),
        cost_estimate=pl.CostEstimate(
            flops=2 * experts * capacity * tokens * width, bytes_accessed=2 * experts * capacity * width, transcendentals=0
        ),
        name="token_sum",
    )(scal, meta, *rows)


def gradient_kernel(units, count, scal, *refs):
    ins, cots, grads = refs[: 2 * count], refs[2 * count : 4 * count], refs[4 * count : 6 * count]
    out = refs[6 * count]
    keep = scal[0] != scal[2]
    left = jnp.concatenate([ref[...] for ref in ins], axis=0)
    right = jnp.concatenate([ref[:, : 2 * units] for ref in grads], axis=0)
    out[0, :, : 2 * units] = jnp.where(keep, dot(left, right, (0, 0)), 0.0)
    left = jnp.concatenate([ref[...] for ref in cots], axis=0)
    right = jnp.concatenate([ref[:, 2 * units :] for ref in grads], axis=0)
    out[0, :, 2 * units :] = jnp.where(keep, dot(left, right, (0, 0)), 0.0)


def expert_gradient(units, scal, mine, packs, others):
    width, columns, count = mine[0].shape[1], 3 * units, len(mine)
    tile = 256
    tiles, skip = width // 2 // tile, columns // tile
    total = 2 * sum(part.shape[0] for part in mine)
    rows = mine + others

    def tiled(first):
        specs = [pl.BlockSpec((part.shape[0], tile), lambda i: (0, i + first)) for part in mine]
        return specs + [
            pl.BlockSpec((part.shape[0], tile), lambda i: (0, i + first + skip)) for part in others
        ]

    in_specs = [pl.BlockSpec(memory_space=pltpu.SMEM)] + tiled(0) + tiled(tiles)
    in_specs += [pl.BlockSpec((part.shape[0], columns), lambda i: (0, 0)) for part in packs + others]
    return pl.pallas_call(
        functools.partial(gradient_kernel, units, count),
        grid=(tiles,),
        out_shape=jax.ShapeDtypeStruct((1, width // 2, columns), F32),
        in_specs=in_specs,
        out_specs=pl.BlockSpec((1, tile, columns), lambda i: (0, i, 0)),
        compiler_params=pltpu.CompilerParams(vmem_limit_bytes=VMEM_BYTES),
        cost_estimate=pl.CostEstimate(
            flops=width * columns * total, bytes_accessed=3 * width * columns, transcendentals=0
        ),
        name="expert_gradient",
    )(scal, *rows, *rows, *packs, *others)


def message_kernel(fanout, tokens, routes, route_weight, ratio, clip, message, meta):
    count, width = tokens.shape
    message[:, :width] = tokens[...]
    weight = route_weight[...] * ratio[...] * clip[...].astype(F32)
    first = weight.astype(BF16).astype(F32)
    rest = weight - first
    second = rest.astype(BF16).astype(F32)
    lines = -(-4 * fanout // 8) * 8
    row = lax.broadcasted_iota(jnp.int32, (lines, count), 0)
    table = jnp.zeros((lines, count), F32)
    for number, part in enumerate([routes[...].astype(F32), first, second, rest - second]):
        for k in range(fanout):
            table = jnp.where(row == number * fanout + k, part[k : k + 1], table)
    table = jnp.concatenate([table, jnp.zeros((128 - lines, count), F32)], axis=0)
    columns = table.T.astype(BF16)
    message[:, width:] = columns
    meta[...] = columns


def build_message(tokens, routes, route_weight, ratio, clip):
    count, width = tokens.shape
    vmem = pl.BlockSpec(memory_space=pltpu.VMEM)
    return pl.pallas_call(
        functools.partial(message_kernel, routes.shape[1]),
        out_shape=[
            jax.ShapeDtypeStruct((count, width + 128), BF16),
            jax.ShapeDtypeStruct((count, 128), BF16),
        ],
        in_specs=[vmem] * 5,
        out_specs=[vmem] * 2,
        cost_estimate=pl.CostEstimate(flops=0, bytes_accessed=4 * count * width, transcendentals=0),
        name="ring_message",
    )(tokens, routes.T, route_weight.T, ratio[None], clip[None])


def order_kernel(plan, experts, capacity, scal, *refs):
    parts, mine, theirs = refs[:-2], refs[-2], refs[-1]
    shift = to_ring(scal[0], experts) - to_ring(scal[2], experts)
    width = mine.shape[1]
    for steps, part in zip(plan, parts):
        for at, step in enumerate(steps):
            place = slot_place((shift + step + 2 * experts) % experts, experts)
            there = pl.ds(pl.multiple_of(place * capacity, capacity), capacity)
            mine[there, :] = part[at * capacity : (at + 1) * capacity, :width]
            theirs[there, :] = part[at * capacity : (at + 1) * capacity, width:]


def ordered(plan, experts, capacity, scal, parts):
    vmem = pl.BlockSpec(memory_space=pltpu.VMEM)
    rows, width = experts * capacity, parts[0].shape[1] // 2
    return pl.pallas_call(
        functools.partial(order_kernel, plan, experts, capacity),
        out_shape=[jax.ShapeDtypeStruct((rows, width), BF16)] * 2,
        in_specs=[pl.BlockSpec(memory_space=pltpu.SMEM)] + [vmem] * len(parts),
        out_specs=[vmem] * 2,
        compiler_params=pltpu.CompilerParams(vmem_limit_bytes=VMEM_BYTES),
        cost_estimate=pl.CostEstimate(flops=0, bytes_accessed=8 * rows * width, transcendentals=0),
        name="hot_rows_ordered",
    )(scal, *parts)


def shadow_kernel(experts, scal, mine, theirs, hot_mine, hot_theirs, out):
    own = scal[0]
    taken = mine.shape[0]
    width = out.shape[1]
    gates = taken * experts * 2 // 3
    column = own * taken + lax.broadcasted_iota(jnp.int32, (taken, 1), 0)

    def product(first):
        columns = pl.ds(first, width)
        return dot(mine[...], hot_mine[:, columns], (1, 0)) + dot(theirs[...], hot_theirs[:, columns], (1, 0))

    @pl.when((own + 1) * taken <= gates)
    def _():
        out[...] = product(0)

    @pl.when(own * taken >= gates)
    def _():
        out[...] = product(width)

    @pl.when((own * taken < gates) & ((own + 1) * taken > gates))
    def _():
        out[...] = jnp.where(column < gates, product(0), product(width))


def shadow_gradient(experts, scal, mine, theirs, hot_mine, hot_theirs):
    taken, rows = mine.shape
    width = hot_mine.shape[1] // 2
    vmem = pl.BlockSpec(memory_space=pltpu.VMEM)
    return pl.pallas_call(
        functools.partial(shadow_kernel, experts),
        out_shape=jax.ShapeDtypeStruct((taken, width), F32),
        in_specs=[pl.BlockSpec(memory_space=pltpu.SMEM)] + [vmem] * 4,
        out_specs=vmem,
        compiler_params=pltpu.CompilerParams(vmem_limit_bytes=24 * 1024 * 1024),
        cost_estimate=pl.CostEstimate(
            flops=4 * taken * rows * width, bytes_accessed=4 * rows * width, transcendentals=0
        ),
        name="shadow_gradient",
    )(scal, mine, theirs, hot_mine, hot_theirs)


def on_device(
    tokens, cotangent, routes, route_weight, ratio_advantage, clip_mask, shadow_plan, gate_up, down
):
    experts = lax.axis_size("expert")
    tok_rows, width = tokens.shape
    fanout = routes.shape[1]
    units = down.shape[1]
    capacity = 2 * tok_rows * fanout // experts
    gate_up, down = gate_up[0], down[0]
    order = ring_order(experts)
    half = experts // 2

    def shift(block, step):
        pairs = [(order[i], order[(i + step) % experts]) for i in range(experts)]
        return lax.ppermute(block, "expert", pairs)

    def swap(block):
        return lax.ppermute(block, "dp", [(0, 1), (1, 0)])

    own = lax.axis_index("expert")
    hottest = shadow_plan[0]
    scal = jnp.stack([own, lax.axis_index("dp"), hottest]).astype(jnp.int32)
    message, meta = build_message(tokens, routes, route_weight, ratio_advantage, clip_mask)

    plan = distances(experts)
    mine, packs, hot, turned, late = [], [], [], [], []
    returned = {}
    up, below, held = [message, cotangent], [message, cotangent], [[message], [cotangent]]
    for number, steps in enumerate(plan):
        if number + 1 < half:
            up, below = [shift(part, 1) for part in up], [shift(part, -1) for part in below]
            following = [[up[0], below[0]], [up[1], below[1]]]
        elif number + 1 == half:
            following = [[shift(up[0], 1)], [shift(below[1], -1)]]
        if number > 1:
            sent, other = late[number - 2]
            held, other = lax.optimization_barrier((held, other))
            late[number - 2] = (sent, other)
        if number == half - 1:
            held, late[: half - 2] = lax.optimization_barrier((held, late[: half - 2]))
        (rows, pack, hot_rows), back, turn = run_step(
            steps,
            fanout,
            capacity,
            scal,
            *held,
            packs[0] if number == half else None,
            gate_up,
            down,
        )
        following[1], back = lax.optimization_barrier((following[1], back))
        if number + 1 < half:
            up, below = [[part[k] for part in following] for k in range(2)]
        sent = [shift(part, step) if step else part for step, part in zip(steps, back)]
        late.append((sent, swap(pack)))
        mine.append(rows)
        packs.append(pack)
        hot.append(hot_rows)
        turned += turn
        held = following
    (back_behind, back_ahead), other = late[half - 1]

    taken = 3 * units // experts
    ring_hot = to_ring(hottest, experts)
    is_hot = own == hottest

    def chunk(distance):
        owner = from_ring((ring_hot + distance + experts) % experts, experts)
        parts = [lax.dynamic_slice_in_dim(part, owner * taken, taken, axis=0) for part in turned]
        return jnp.concatenate(parts, axis=1)

    lanes = experts * capacity // 2

    def halves(distance):
        columns = chunk(distance)
        return [columns[:, :lanes], columns[:, lanes:]]

    hot_mine, hot_theirs = ordered(plan, experts, capacity, scal, hot)
    far = halves(half)
    far, other, hot_mine, hot_theirs = lax.optimization_barrier((far, other, hot_mine, hot_theirs))
    hot_theirs = swap(hot_theirs)
    far = [shift(far[0], 1), shift(far[1], -1)]
    others = [part for _, part in late[: half - 1]] + [other, late[half][1]]
    expert_grad = expert_gradient(units, scal, mine, packs, others)
    chunks = {distance: halves(distance) for distance in range(1 - half, half)}
    (back_far,) = late[half][0]
    far, expert_grad, back_ahead, back_behind, chunks, late[half - 2] = (
        lax.optimization_barrier(
            (far, expert_grad, back_ahead, back_behind, chunks, late[half - 2])
        )
    )
    ahead, behind = [far[0], None], [None, far[1]]

    def onward(kept, received, step):
        return shift(kept if received is None else jnp.where(is_hot, kept, received), step)

    for number in range(1, half):
        for k in range(2):
            ahead[k] = onward(chunks[half - number][k], ahead[k], 1)
            behind[k] = onward(chunks[number - half][k], behind[k], -1)
    sent = [rows for rows, _ in late[: half - 1]] + [[back_behind, back_ahead], [back_far]]
    for steps, parts in zip(plan, sent):
        for step, part in zip(steps, parts):
            returned[step % experts] = part
    token_grad = combine(experts, fanout, capacity, scal, meta, [returned[d] for d in range(experts)])
    ahead, behind, token_grad = lax.optimization_barrier((ahead, behind, token_grad))
    away = (to_ring(own, experts) - ring_hot + experts) % experts
    columns = [
        jnp.where(away == 0, chunks[0][k], jnp.where(away <= half - k, ahead[k], behind[k]))
        for k in range(2)
    ]
    columns = jnp.concatenate(columns, axis=1)
    shadow_grad = shadow_gradient(
        experts, scal, columns, swap(columns), hot_mine, hot_theirs
    ).T
    return (token_grad, expert_grad, shadow_grad)


def solution(mesh):
    placed = (
        P(("group", "expert", "dp"), None),
        P(("group", "expert", "dp"), None),
        P(("group", "expert", "dp"), None),
        P(("group", "expert", "dp"), None),
        P(("group", "expert", "dp")),
        P(("group", "expert", "dp")),
        P("group"),
        P("expert", None, None),
        P("expert", None, None),
    )
    return jax.shard_map(
        on_device,
        mesh=mesh,
        in_specs=placed,
        out_specs=(
            P(("group", "expert", "dp"), None),
            P(("group", "expert"), "dp", None),
            P(("group", "dp"), "expert"),
        ),
        check_vma=False,
    )
```

```python
import functools

import jax
import jax.numpy as jnp
from jax import lax
from jax.experimental import pallas as pl
from jax.experimental.pallas import tpu as pltpu
from jax.sharding import PartitionSpec as P

BF16 = jnp.bfloat16
F32 = jnp.float32
VMEM_BYTES = 56 * 1024 * 1024


def snaked(experts):
    return experts <= 8


def to_ring(expert, experts):
    if not snaked(experts):
        return expert
    down = experts - 1 - (expert - 1) // 2
    return jnp.where(expert % 2 == 0, expert // 2, down)


def from_ring(place, experts):
    if not snaked(experts):
        return place
    return jnp.where(place < experts // 2, 2 * place, 2 * (experts - 1 - place) + 1)


def ring_order(experts):
    if not snaked(experts):
        return list(range(experts))
    return list(range(0, experts, 2)) + list(range(experts - 1, 0, -2))


def distances(experts):
    half = experts // 2
    return [[0]] + [[-step, step] for step in range(1, half)] + [[half]]


def slot_place(distance, experts):
    half = experts // 2
    near = jnp.where(distance < half, 2 * distance - 1, 2 * (experts - distance) - 2)
    near = jnp.where(distance == half, experts - 1, near)
    return jnp.where(distance == 0, experts - 2, near)


def dot(a, b, dims):
    return lax.dot_general(a, b, ((dims[:1], dims[1:]), ((), ())), preferred_element_type=F32)


def selection(table, expert, fanout, capacity):
    tokens = table.shape[1]
    hit = table[:fanout] == expert.astype(F32)
    named = jnp.sum(jnp.where(hit, 1.0, 0.0), axis=0, keepdims=True)
    parts = table[fanout : 4 * fanout]
    weights = parts[:fanout] + parts[fanout : 2 * fanout] + parts[2 * fanout :]
    weight = jnp.sum(jnp.where(hit, weights, 0.0), axis=0, keepdims=True)
    upto = lax.broadcasted_iota(jnp.int32, (tokens, tokens), 0) <= lax.broadcasted_iota(
        jnp.int32, (tokens, tokens), 1
    )
    upto = jnp.where(upto, 1.0, 0.0).astype(BF16)
    place = dot(jnp.broadcast_to(named, (8, tokens)).astype(BF16), upto, (1, 0))[:1]
    row = lax.broadcasted_iota(jnp.int32, (capacity, tokens), 0).astype(F32) + 1.0
    onehot = jnp.where((row == place) & (named > 0.5), 1.0, 0.0)
    return onehot, weight


def step_kernel(steps, fanout, capacity, joined, scal, *refs):
    count = len(steps)
    messages, cotangents, refs = refs[:count], refs[count : 2 * count], refs[2 * count :]
    if joined:
        first, refs = refs[0], refs[1:]
    weights_gu, weights_down, mine, pack, hot = refs[:5]
    back, refs = refs[5 : 5 + count], refs[5 + count :]
    if len(refs) > 7:
        turned, refs = refs[0], refs[1:]
    else:
        turned = None
    rows_in, rows_cot, hot_in, hot_cot, gate_up, down, sems = refs
    own, half, hottest = scal[0], scal[1], scal[2]
    units, width = down.shape
    load_gu = pltpu.make_async_copy(weights_gu, gate_up, sems.at[0])
    load_down = pltpu.make_async_copy(weights_down, down, sems.at[1])
    load_gu.start()
    load_down.start()
    for at, (message, cotangent) in enumerate(zip(messages, cotangents)):
        rows = slice(at * capacity, (at + 1) * capacity)
        table = message[:, width:].astype(F32).T
        own_hot, own_weight = selection(table, own, fanout, capacity)
        all_hot, all_weight = selection(table, hottest, fanout, capacity)
        scale = jnp.concatenate(
            [
                jnp.sum(own_hot * own_weight, axis=1, keepdims=True),
                jnp.sum(all_hot * all_weight, axis=1, keepdims=True),
            ],
            axis=0,
        )
        onehot = jnp.concatenate([own_hot, all_hot], axis=0).astype(BF16)
        picked = dot(onehot, message[:, :width], (1, 0)).astype(BF16)
        rows_in[rows, :] = picked[:capacity]
        hot_in[rows, :] = picked[capacity:]
        picked = (scale * dot(onehot, cotangent[...], (1, 0))).astype(BF16)
        rows_cot[rows, :] = picked[:capacity]
        hot_cot[rows, :] = picked[capacity:]
    part = width // 2
    here = pl.ds(pl.multiple_of(half * part, part), part)
    there = pl.ds(pl.multiple_of((1 - half) * part, part), part)
    mine[:, :part] = rows_in[:, here]
    mine[:, part:] = rows_cot[:, here]
    pack[:, 3 * units : 3 * units + part] = rows_in[:, there]
    pack[:, 3 * units + part :] = rows_cot[:, there]
    hot[:, :part] = hot_in[:, here]
    hot[:, part:width] = hot_cot[:, here]
    hot[:, width : width + part] = hot_in[:, there]
    hot[:, width + part :] = hot_cot[:, there]
    load_gu.wait()
    projected = dot(rows_in[...], gate_up[...], (1, 0))
    gate_pre, up_pre = projected[:, :units], projected[:, units:]
    load_down.wait()
    hidden_grad = dot(rows_cot[...], down[...], (1, 1))
    sigmoid_gate = jax.nn.sigmoid(gate_pre)
    activation = gate_pre * sigmoid_gate
    gate_grad = hidden_grad * up_pre * sigmoid_gate * (1.0 + gate_pre * (1.0 - sigmoid_gate))
    pack[:, :units] = gate_grad.astype(BF16)
    pack[:, units : 2 * units] = (hidden_grad * activation).astype(BF16)
    pack[:, 2 * units : 3 * units] = (activation * up_pre).astype(BF16)
    input_rows = dot(pack[:, : 2 * units], gate_up[...], (1, 1)).astype(BF16)
    for at, part in enumerate(back):
        part[...] = input_rows[at * part.shape[0] : (at + 1) * part.shape[0]]
    if turned is not None:
        grads = pack[:, : 3 * units]
        if joined:
            grads = jnp.concatenate([first[:, : 3 * units], grads], axis=0)
        turned[...] = grads.T


def run_step(steps, fanout, capacity, scal, messages, cotangents, first, gate_up, down):
    count, rows = len(steps), len(steps) * capacity
    units, width = down.shape
    vmem = pl.BlockSpec(memory_space=pltpu.VMEM)
    far = pl.BlockSpec(memory_space=pl.ANY)
    shapes = [(rows, width), (rows, 3 * units + width), (rows, 2 * width)]
    joined = first is not None
    shapes += [(capacity, width)] * count
    if joined or count > 1:
        shapes += [(3 * units, 2 * capacity)]
    firsts = [first] if joined else []
    out = pl.pallas_call(
        functools.partial(step_kernel, steps, fanout, capacity, joined),
        out_shape=[jax.ShapeDtypeStruct(shape, BF16) for shape in shapes],
        in_specs=[pl.BlockSpec(memory_space=pltpu.SMEM)] + [vmem] * (2 * count + len(firsts)) + [far] * 2,
        out_specs=[vmem] * len(shapes),
        scratch_shapes=[pltpu.VMEM((rows, width), BF16)] * 4
        + [
            pltpu.VMEM(gate_up.shape, BF16),
            pltpu.VMEM(down.shape, BF16),
            pltpu.SemaphoreType.DMA((2,)),
        ],
        compiler_params=pltpu.CompilerParams(vmem_limit_bytes=VMEM_BYTES),
        cost_estimate=pl.CostEstimate(
            flops=2 * 256 * 5 * width * units, bytes_accessed=3 * 2 * width * units, transcendentals=0
        ),
        name="expert_step",
    )(scal, *messages, *cotangents, *firsts, gate_up, down)
    return out[:3], out[3 : 3 + count], out[3 + count :]


def combine_kernel(experts, fanout, capacity, scal, meta, *refs):
    rows, out = refs[:-1], refs[-1]
    place = to_ring(scal[0], experts)
    table = meta[...].astype(F32).T
    picks = []
    for step in range(experts):
        expert = from_ring((place - step + experts) % experts, experts)
        picks.append(selection(table, expert, fanout, capacity)[0])
    onehot = jnp.concatenate(picks, axis=0).astype(BF16)
    out[...] = dot(onehot, jnp.concatenate([part[...] for part in rows], axis=0), (0, 0)).astype(BF16)


def combine(experts, fanout, capacity, scal, meta, rows):
    vmem = pl.BlockSpec(memory_space=pltpu.VMEM)
    tokens, width = meta.shape[0], rows[0].shape[1]
    return pl.pallas_call(
        functools.partial(combine_kernel, experts, fanout, capacity),
        out_shape=jax.ShapeDtypeStruct((tokens, width), BF16),
        in_specs=[pl.BlockSpec(memory_space=pltpu.SMEM)] + [vmem] * (len(rows) + 1),
        out_specs=vmem,
        compiler_params=pltpu.CompilerParams(vmem_limit_bytes=VMEM_BYTES),
        cost_estimate=pl.CostEstimate(
            flops=2 * experts * capacity * tokens * width, bytes_accessed=2 * experts * capacity * width, transcendentals=0
        ),
        name="token_sum",
    )(scal, meta, *rows)


def gradient_kernel(units, count, scal, *refs):
    ins, cots, grads = refs[: 2 * count], refs[2 * count : 4 * count], refs[4 * count : 6 * count]
    out = refs[6 * count]
    keep = scal[0] != scal[2]
    left = jnp.concatenate([ref[...] for ref in ins], axis=0)
    right = jnp.concatenate([ref[:, : 2 * units] for ref in grads], axis=0)
    out[0, :, : 2 * units] = jnp.where(keep, dot(left, right, (0, 0)), 0.0)
    left = jnp.concatenate([ref[...] for ref in cots], axis=0)
    right = jnp.concatenate([ref[:, 2 * units :] for ref in grads], axis=0)
    out[0, :, 2 * units :] = jnp.where(keep, dot(left, right, (0, 0)), 0.0)


def expert_gradient(units, scal, mine, packs, others):
    width, columns, count = mine[0].shape[1], 3 * units, len(mine)
    tile = 256
    tiles, skip = width // 2 // tile, columns // tile
    total = 2 * sum(part.shape[0] for part in mine)
    rows = mine + others

    def tiled(first):
        specs = [pl.BlockSpec((part.shape[0], tile), lambda i: (0, i + first)) for part in mine]
        return specs + [
            pl.BlockSpec((part.shape[0], tile), lambda i: (0, i + first + skip)) for part in others
        ]

    in_specs = [pl.BlockSpec(memory_space=pltpu.SMEM)] + tiled(0) + tiled(tiles)
    in_specs += [pl.BlockSpec((part.shape[0], columns), lambda i: (0, 0)) for part in packs + others]
    return pl.pallas_call(
        functools.partial(gradient_kernel, units, count),
        grid=(tiles,),
        out_shape=jax.ShapeDtypeStruct((1, width // 2, columns), F32),
        in_specs=in_specs,
        out_specs=pl.BlockSpec((1, tile, columns), lambda i: (0, i, 0)),
        compiler_params=pltpu.CompilerParams(vmem_limit_bytes=VMEM_BYTES),
        cost_estimate=pl.CostEstimate(
            flops=width * columns * total, bytes_accessed=3 * width * columns, transcendentals=0
        ),
        name="expert_gradient",
    )(scal, *rows, *rows, *packs, *others)


def message_kernel(fanout, tokens, routes, route_weight, ratio, clip, message, meta):
    count, width = tokens.shape
    message[:, :width] = tokens[...]
    weight = route_weight[...] * ratio[...] * clip[...].astype(F32)
    first = weight.astype(BF16).astype(F32)
    rest = weight - first
    second = rest.astype(BF16).astype(F32)
    lines = -(-4 * fanout // 8) * 8
    row = lax.broadcasted_iota(jnp.int32, (lines, count), 0)
    table = jnp.zeros((lines, count), F32)
    for number, part in enumerate([routes[...].astype(F32), first, second, rest - second]):
        for k in range(fanout):
            table = jnp.where(row == number * fanout + k, part[k : k + 1], table)
    table = jnp.concatenate([table, jnp.zeros((128 - lines, count), F32)], axis=0)
    columns = table.T.astype(BF16)
    message[:, width:] = columns
    meta[...] = columns


def build_message(tokens, routes, route_weight, ratio, clip):
    count, width = tokens.shape
    vmem = pl.BlockSpec(memory_space=pltpu.VMEM)
    return pl.pallas_call(
        functools.partial(message_kernel, routes.shape[1]),
        out_shape=[
            jax.ShapeDtypeStruct((count, width + 128), BF16),
            jax.ShapeDtypeStruct((count, 128), BF16),
        ],
        in_specs=[vmem] * 5,
        out_specs=[vmem] * 2,
        cost_estimate=pl.CostEstimate(flops=0, bytes_accessed=4 * count * width, transcendentals=0),
        name="ring_message",
    )(tokens, routes.T, route_weight.T, ratio[None], clip[None])


def order_kernel(plan, experts, capacity, scal, *refs):
    parts, mine, theirs = refs[:-2], refs[-2], refs[-1]
    shift = to_ring(scal[0], experts) - to_ring(scal[2], experts)
    width = mine.shape[1]
    for steps, part in zip(plan, parts):
        for at, step in enumerate(steps):
            place = slot_place((shift + step + 2 * experts) % experts, experts)
            there = pl.ds(pl.multiple_of(place * capacity, capacity), capacity)
            mine[there, :] = part[at * capacity : (at + 1) * capacity, :width]
            theirs[there, :] = part[at * capacity : (at + 1) * capacity, width:]


def ordered(plan, experts, capacity, scal, parts):
    vmem = pl.BlockSpec(memory_space=pltpu.VMEM)
    rows, width = experts * capacity, parts[0].shape[1] // 2
    return pl.pallas_call(
        functools.partial(order_kernel, plan, experts, capacity),
        out_shape=[jax.ShapeDtypeStruct((rows, width), BF16)] * 2,
        in_specs=[pl.BlockSpec(memory_space=pltpu.SMEM)] + [vmem] * len(parts),
        out_specs=[vmem] * 2,
        compiler_params=pltpu.CompilerParams(vmem_limit_bytes=VMEM_BYTES),
        cost_estimate=pl.CostEstimate(flops=0, bytes_accessed=8 * rows * width, transcendentals=0),
        name="hot_rows_ordered",
    )(scal, *parts)


def shadow_kernel(experts, scal, mine, theirs, hot_mine, hot_theirs, out):
    own = scal[0]
    taken = mine.shape[0]
    width = out.shape[1]
    gates = taken * experts * 2 // 3
    column = own * taken + lax.broadcasted_iota(jnp.int32, (taken, 1), 0)

    def product(first):
        columns = pl.ds(first, width)
        return dot(mine[...], hot_mine[:, columns], (1, 0)) + dot(theirs[...], hot_theirs[:, columns], (1, 0))

    @pl.when((own + 1) * taken <= gates)
    def _():
        out[...] = product(0)

    @pl.when(own * taken >= gates)
    def _():
        out[...] = product(width)

    @pl.when((own * taken < gates) & ((own + 1) * taken > gates))
    def _():
        out[...] = jnp.where(column < gates, product(0), product(width))


def shadow_gradient(experts, scal, mine, theirs, hot_mine, hot_theirs):
    taken, rows = mine.shape
    width = hot_mine.shape[1] // 2
    vmem = pl.BlockSpec(memory_space=pltpu.VMEM)
    return pl.pallas_call(
        functools.partial(shadow_kernel, experts),
        out_shape=jax.ShapeDtypeStruct((taken, width), F32),
        in_specs=[pl.BlockSpec(memory_space=pltpu.SMEM)] + [vmem] * 4,
        out_specs=vmem,
        compiler_params=pltpu.CompilerParams(vmem_limit_bytes=24 * 1024 * 1024),
        cost_estimate=pl.CostEstimate(
            flops=4 * taken * rows * width, bytes_accessed=4 * rows * width, transcendentals=0
        ),
        name="shadow_gradient",
    )(scal, mine, theirs, hot_mine, hot_theirs)


def on_device(
    tokens, cotangent, routes, route_weight, ratio_advantage, clip_mask, shadow_plan, gate_up, down
):
    experts = lax.axis_size("expert")
    tok_rows, width = tokens.shape
    fanout = routes.shape[1]
    units = down.shape[1]
    capacity = 2 * tok_rows * fanout // experts
    gate_up, down = gate_up[0], down[0]
    order = ring_order(experts)
    half = experts // 2

    def shift(block, step):
        pairs = [(order[i], order[(i + step) % experts]) for i in range(experts)]
        return lax.ppermute(block, "expert", pairs)

    def swap(block):
        return lax.ppermute(block, "dp", [(0, 1), (1, 0)])

    own = lax.axis_index("expert")
    hottest = shadow_plan[0]
    scal = jnp.stack([own, lax.axis_index("dp"), hottest]).astype(jnp.int32)
    message, meta = build_message(tokens, routes, route_weight, ratio_advantage, clip_mask)

    plan = distances(experts)
    mine, packs, hot, turned, late = [], [], [], [], []
    returned = {}
    up, below, held = [message, cotangent], [message, cotangent], [[message], [cotangent]]
    for number, steps in enumerate(plan):
        if number + 1 < half:
            up, below = [shift(part, 1) for part in up], [shift(part, -1) for part in below]
            following = [[up[0], below[0]], [up[1], below[1]]]
        elif number + 1 == half:
            following = [[shift(up[0], 1)], [shift(below[1], -1)]]
        if number > 1:
            sent, other = late[number - 2]
            held, other = lax.optimization_barrier((held, other))
            late[number - 2] = (sent, other)
        if number == half - 1:
            held, late[: half - 2] = lax.optimization_barrier((held, late[: half - 2]))
        (rows, pack, hot_rows), back, turn = run_step(
            steps,
            fanout,
            capacity,
            scal,
            *held,
            packs[0] if number == half else None,
            gate_up,
            down,
        )
        following[1], back = lax.optimization_barrier((following[1], back))
        if number + 1 < half:
            up, below = [[part[k] for part in following] for k in range(2)]
        sent = [shift(part, step) if step else part for step, part in zip(steps, back)]
        late.append((sent, swap(pack)))
        mine.append(rows)
        packs.append(pack)
        hot.append(hot_rows)
        turned += turn
        held = following
    (back_behind, back_ahead), other = late[half - 1]
    hot_mine, hot_theirs = ordered(plan, experts, capacity, scal, hot)
    turned[-1], late[half - 2], hot_mine, hot_theirs = lax.optimization_barrier(
        (turned[-1], late[half - 2], hot_mine, hot_theirs)
    )

    taken = 3 * units // experts
    ring_hot = to_ring(hottest, experts)
    is_hot = own == hottest

    def chunk(distance):
        owner = from_ring((ring_hot + distance + experts) % experts, experts)
        parts = [lax.dynamic_slice_in_dim(part, owner * taken, taken, axis=0) for part in turned]
        return jnp.concatenate(parts, axis=1)

    lanes = experts * capacity // 2

    def halves(distance):
        columns = chunk(distance)
        return [columns[:, :lanes], columns[:, lanes:]]

    far = halves(half)
    far, other = lax.optimization_barrier((far, other))
    hot_theirs = swap(hot_theirs)
    far = [shift(far[0], 1), shift(far[1], -1)]
    others = [part for _, part in late[: half - 1]] + [other, late[half][1]]
    expert_grad = expert_gradient(units, scal, mine, packs, others)
    chunks = {distance: halves(distance) for distance in range(1 - half, half)}
    (back_far,) = late[half][0]
    far, expert_grad, back_ahead, back_behind, back_far, chunks = lax.optimization_barrier(
        (far, expert_grad, back_ahead, back_behind, back_far, chunks)
    )
    ahead, behind = [far[0], None], [None, far[1]]

    def onward(kept, received, step):
        return shift(kept if received is None else jnp.where(is_hot, kept, received), step)

    for number in range(1, half):
        for k in range(2):
            ahead[k] = onward(chunks[half - number][k], ahead[k], 1)
            behind[k] = onward(chunks[number - half][k], behind[k], -1)
    sent = [rows for rows, _ in late[: half - 1]] + [[back_behind, back_ahead], [back_far]]
    for steps, parts in zip(plan, sent):
        for step, part in zip(steps, parts):
            returned[step % experts] = part
    token_grad = combine(experts, fanout, capacity, scal, meta, [returned[d] for d in range(experts)])
    ahead, behind, token_grad = lax.optimization_barrier((ahead, behind, token_grad))
    away = (to_ring(own, experts) - ring_hot + experts) % experts
    columns = [
        jnp.where(away == 0, chunks[0][k], jnp.where(away <= half - k, ahead[k], behind[k]))
        for k in range(2)
    ]
    columns = jnp.concatenate(columns, axis=1)
    shadow_grad = shadow_gradient(
        experts, scal, columns, swap(columns), hot_mine, hot_theirs
    ).T
    return (token_grad, expert_grad, shadow_grad)


def solution(mesh):
    placed = (
        P(("group", "expert", "dp"), None),
        P(("group", "expert", "dp"), None),
        P(("group", "expert", "dp"), None),
        P(("group", "expert", "dp"), None),
        P(("group", "expert", "dp")),
        P(("group", "expert", "dp")),
        P("group"),
        P("expert", None, None),
        P("expert", None, None),
    )
    return jax.shard_map(
        on_device,
        mesh=mesh,
        in_specs=placed,
        out_specs=(
            P(("group", "expert", "dp"), None),
            P(("group", "expert"), "dp", None),
            P(("group", "dp"), "expert"),
        ),
        check_vma=False,
    )
```

```python
import functools

import jax
import jax.numpy as jnp
from jax import lax
from jax.experimental import pallas as pl
from jax.experimental.pallas import tpu as pltpu
from jax.sharding import PartitionSpec as P

BF16 = jnp.bfloat16
F32 = jnp.float32
VMEM_BYTES = 56 * 1024 * 1024


def snaked(experts):
    return experts <= 8


def to_ring(expert, experts):
    if not snaked(experts):
        return expert
    down = experts - 1 - (expert - 1) // 2
    return jnp.where(expert % 2 == 0, expert // 2, down)


def from_ring(place, experts):
    if not snaked(experts):
        return place
    return jnp.where(place < experts // 2, 2 * place, 2 * (experts - 1 - place) + 1)


def ring_order(experts):
    if not snaked(experts):
        return list(range(experts))
    return list(range(0, experts, 2)) + list(range(experts - 1, 0, -2))


def distances(experts):
    half = experts // 2
    return [[0]] + [[-step, step] for step in range(1, half)] + [[half]]


def slot_place(distance, experts):
    half = experts // 2
    near = jnp.where(distance < half, 2 * distance - 1, 2 * (experts - distance) - 2)
    near = jnp.where(distance == half, experts - 1, near)
    return jnp.where(distance == 0, experts - 2, near)


def dot(a, b, dims):
    return lax.dot_general(a, b, ((dims[:1], dims[1:]), ((), ())), preferred_element_type=F32)


def selection(table, expert, fanout, capacity):
    tokens = table.shape[1]
    hit = table[:fanout] == expert.astype(F32)
    named = jnp.sum(jnp.where(hit, 1.0, 0.0), axis=0, keepdims=True)
    parts = table[fanout : 4 * fanout]
    weights = parts[:fanout] + parts[fanout : 2 * fanout] + parts[2 * fanout :]
    weight = jnp.sum(jnp.where(hit, weights, 0.0), axis=0, keepdims=True)
    upto = lax.broadcasted_iota(jnp.int32, (tokens, tokens), 0) <= lax.broadcasted_iota(
        jnp.int32, (tokens, tokens), 1
    )
    upto = jnp.where(upto, 1.0, 0.0).astype(BF16)
    place = dot(jnp.broadcast_to(named, (8, tokens)).astype(BF16), upto, (1, 0))[:1]
    row = lax.broadcasted_iota(jnp.int32, (capacity, tokens), 0).astype(F32) + 1.0
    onehot = jnp.where((row == place) & (named > 0.5), 1.0, 0.0)
    return onehot, weight


def step_kernel(steps, fanout, capacity, joined, scal, *refs):
    count = len(steps)
    messages, cotangents, refs = refs[:count], refs[count : 2 * count], refs[2 * count :]
    if joined:
        first, refs = refs[0], refs[1:]
    weights_gu, weights_down, mine, pack, hot = refs[:5]
    back, refs = refs[5 : 5 + count], refs[5 + count :]
    if len(refs) > 7:
        turned, refs = refs[0], refs[1:]
    else:
        turned = None
    rows_in, rows_cot, hot_in, hot_cot, gate_up, down, sems = refs
    own, half, hottest = scal[0], scal[1], scal[2]
    units, width = down.shape
    load_gu = pltpu.make_async_copy(weights_gu, gate_up, sems.at[0])
    load_down = pltpu.make_async_copy(weights_down, down, sems.at[1])
    load_gu.start()
    load_down.start()
    for at, (message, cotangent) in enumerate(zip(messages, cotangents)):
        rows = slice(at * capacity, (at + 1) * capacity)
        table = message[:, width:].astype(F32).T
        own_hot, own_weight = selection(table, own, fanout, capacity)
        all_hot, all_weight = selection(table, hottest, fanout, capacity)
        scale = jnp.concatenate(
            [
                jnp.sum(own_hot * own_weight, axis=1, keepdims=True),
                jnp.sum(all_hot * all_weight, axis=1, keepdims=True),
            ],
            axis=0,
        )
        onehot = jnp.concatenate([own_hot, all_hot], axis=0).astype(BF16)
        picked = dot(onehot, message[:, :width], (1, 0)).astype(BF16)
        rows_in[rows, :] = picked[:capacity]
        hot_in[rows, :] = picked[capacity:]
        picked = (scale * dot(onehot, cotangent[...], (1, 0))).astype(BF16)
        rows_cot[rows, :] = picked[:capacity]
        hot_cot[rows, :] = picked[capacity:]
    part = width // 2
    here = pl.ds(pl.multiple_of(half * part, part), part)
    there = pl.ds(pl.multiple_of((1 - half) * part, part), part)
    mine[:, :part] = rows_in[:, here]
    mine[:, part:] = rows_cot[:, here]
    pack[:, 3 * units : 3 * units + part] = rows_in[:, there]
    pack[:, 3 * units + part :] = rows_cot[:, there]
    hot[:, :part] = hot_in[:, here]
    hot[:, part:width] = hot_cot[:, here]
    hot[:, width : width + part] = hot_in[:, there]
    hot[:, width + part :] = hot_cot[:, there]
    load_gu.wait()
    projected = dot(rows_in[...], gate_up[...], (1, 0))
    gate_pre, up_pre = projected[:, :units], projected[:, units:]
    load_down.wait()
    hidden_grad = dot(rows_cot[...], down[...], (1, 1))
    sigmoid_gate = jax.nn.sigmoid(gate_pre)
    activation = gate_pre * sigmoid_gate
    gate_grad = hidden_grad * up_pre * sigmoid_gate * (1.0 + gate_pre * (1.0 - sigmoid_gate))
    pack[:, :units] = gate_grad.astype(BF16)
    pack[:, units : 2 * units] = (hidden_grad * activation).astype(BF16)
    pack[:, 2 * units : 3 * units] = (activation * up_pre).astype(BF16)
    input_rows = dot(pack[:, : 2 * units], gate_up[...], (1, 1)).astype(BF16)
    for at, part in enumerate(back):
        part[...] = input_rows[at * part.shape[0] : (at + 1) * part.shape[0]]
    if turned is not None:
        grads = pack[:, : 3 * units]
        if joined:
            grads = jnp.concatenate([first[:, : 3 * units], grads], axis=0)
        turned[...] = grads.T


def run_step(steps, fanout, capacity, scal, messages, cotangents, first, gate_up, down):
    count, rows = len(steps), len(steps) * capacity
    units, width = down.shape
    vmem = pl.BlockSpec(memory_space=pltpu.VMEM)
    far = pl.BlockSpec(memory_space=pl.ANY)
    shapes = [(rows, width), (rows, 3 * units + width), (rows, 2 * width)]
    joined = first is not None
    shapes += [(capacity, width)] * count
    if joined or count > 1:
        shapes += [(3 * units, 2 * capacity)]
    firsts = [first] if joined else []
    out = pl.pallas_call(
        functools.partial(step_kernel, steps, fanout, capacity, joined),
        out_shape=[jax.ShapeDtypeStruct(shape, BF16) for shape in shapes],
        in_specs=[pl.BlockSpec(memory_space=pltpu.SMEM)] + [vmem] * (2 * count + len(firsts)) + [far] * 2,
        out_specs=[vmem] * len(shapes),
        scratch_shapes=[pltpu.VMEM((rows, width), BF16)] * 4
        + [
            pltpu.VMEM(gate_up.shape, BF16),
            pltpu.VMEM(down.shape, BF16),
            pltpu.SemaphoreType.DMA((2,)),
        ],
        compiler_params=pltpu.CompilerParams(vmem_limit_bytes=VMEM_BYTES),
        cost_estimate=pl.CostEstimate(
            flops=2 * 256 * 5 * width * units, bytes_accessed=3 * 2 * width * units, transcendentals=0
        ),
        name="expert_step",
    )(scal, *messages, *cotangents, *firsts, gate_up, down)
    return out[:3], out[3 : 3 + count], out[3 + count :]


def combine_kernel(experts, fanout, capacity, scal, meta, *refs):
    rows, out = refs[:-1], refs[-1]
    place = to_ring(scal[0], experts)
    table = meta[...].astype(F32).T
    picks = []
    for step in range(experts):
        expert = from_ring((place - step + experts) % experts, experts)
        picks.append(selection(table, expert, fanout, capacity)[0])
    onehot = jnp.concatenate(picks, axis=0).astype(BF16)
    out[...] = dot(onehot, jnp.concatenate([part[...] for part in rows], axis=0), (0, 0)).astype(BF16)


def combine(experts, fanout, capacity, scal, meta, rows):
    vmem = pl.BlockSpec(memory_space=pltpu.VMEM)
    tokens, width = meta.shape[0], rows[0].shape[1]
    return pl.pallas_call(
        functools.partial(combine_kernel, experts, fanout, capacity),
        out_shape=jax.ShapeDtypeStruct((tokens, width), BF16),
        in_specs=[pl.BlockSpec(memory_space=pltpu.SMEM)] + [vmem] * (len(rows) + 1),
        out_specs=vmem,
        compiler_params=pltpu.CompilerParams(vmem_limit_bytes=VMEM_BYTES),
        cost_estimate=pl.CostEstimate(
            flops=2 * experts * capacity * tokens * width, bytes_accessed=2 * experts * capacity * width, transcendentals=0
        ),
        name="token_sum",
    )(scal, meta, *rows)


def gradient_kernel(units, count, scal, *refs):
    ins, cots, grads = refs[: 2 * count], refs[2 * count : 4 * count], refs[4 * count : 6 * count]
    out, joined = refs[6 * count :]
    keep = scal[0] != scal[2]

    @pl.when(pl.program_id(0) == 0)
    def _():
        at = 0
        for ref in grads:
            joined[at : at + ref.shape[0], :] = ref[...]
            at += ref.shape[0]

    left = jnp.concatenate([ref[...] for ref in ins], axis=0)
    out[0, :, : 2 * units] = jnp.where(keep, dot(left, joined[:, : 2 * units], (0, 0)), 0.0)
    left = jnp.concatenate([ref[...] for ref in cots], axis=0)
    out[0, :, 2 * units :] = jnp.where(keep, dot(left, joined[:, 2 * units :], (0, 0)), 0.0)


def expert_gradient(units, scal, mine, packs, others):
    width, columns, count = mine[0].shape[1], 3 * units, len(mine)
    tile = 256
    tiles, skip = width // 2 // tile, columns // tile
    total = 2 * sum(part.shape[0] for part in mine)
    rows = mine + others

    def tiled(first):
        specs = [pl.BlockSpec((part.shape[0], tile), lambda i: (0, i + first)) for part in mine]
        return specs + [
            pl.BlockSpec((part.shape[0], tile), lambda i: (0, i + first + skip)) for part in others
        ]

    in_specs = [pl.BlockSpec(memory_space=pltpu.SMEM)] + tiled(0) + tiled(tiles)
    in_specs += [pl.BlockSpec((part.shape[0], columns), lambda i: (0, 0)) for part in packs + others]
    return pl.pallas_call(
        functools.partial(gradient_kernel, units, count),
        grid=(tiles,),
        out_shape=jax.ShapeDtypeStruct((1, width // 2, columns), F32),
        in_specs=in_specs,
        out_specs=pl.BlockSpec((1, tile, columns), lambda i: (0, i, 0)),
        scratch_shapes=[pltpu.VMEM((total, columns), BF16)],
        compiler_params=pltpu.CompilerParams(vmem_limit_bytes=VMEM_BYTES),
        cost_estimate=pl.CostEstimate(
            flops=width * columns * total, bytes_accessed=3 * width * columns, transcendentals=0
        ),
        name="expert_gradient",
    )(scal, *rows, *rows, *packs, *others)


def message_kernel(fanout, tokens, routes, route_weight, ratio, clip, message, meta):
    count, width = tokens.shape
    message[:, :width] = tokens[...]
    weight = route_weight[...] * ratio[...] * clip[...].astype(F32)
    first = weight.astype(BF16).astype(F32)
    rest = weight - first
    second = rest.astype(BF16).astype(F32)
    lines = -(-4 * fanout // 8) * 8
    row = lax.broadcasted_iota(jnp.int32, (lines, count), 0)
    table = jnp.zeros((lines, count), F32)
    for number, part in enumerate([routes[...].astype(F32), first, second, rest - second]):
        for k in range(fanout):
            table = jnp.where(row == number * fanout + k, part[k : k + 1], table)
    table = jnp.concatenate([table, jnp.zeros((128 - lines, count), F32)], axis=0)
    columns = table.T.astype(BF16)
    message[:, width:] = columns
    meta[...] = columns


def build_message(tokens, routes, route_weight, ratio, clip):
    count, width = tokens.shape
    vmem = pl.BlockSpec(memory_space=pltpu.VMEM)
    return pl.pallas_call(
        functools.partial(message_kernel, routes.shape[1]),
        out_shape=[
            jax.ShapeDtypeStruct((count, width + 128), BF16),
            jax.ShapeDtypeStruct((count, 128), BF16),
        ],
        in_specs=[vmem] * 5,
        out_specs=[vmem] * 2,
        cost_estimate=pl.CostEstimate(flops=0, bytes_accessed=4 * count * width, transcendentals=0),
        name="ring_message",
    )(tokens, routes.T, route_weight.T, ratio[None], clip[None])


def order_kernel(plan, experts, capacity, scal, *refs):
    parts, mine, theirs = refs[:-2], refs[-2], refs[-1]
    shift = to_ring(scal[0], experts) - to_ring(scal[2], experts)
    width = mine.shape[1]
    for steps, part in zip(plan, parts):
        for at, step in enumerate(steps):
            place = slot_place((shift + step + 2 * experts) % experts, experts)
            there = pl.ds(pl.multiple_of(place * capacity, capacity), capacity)
            mine[there, :] = part[at * capacity : (at + 1) * capacity, :width]
            theirs[there, :] = part[at * capacity : (at + 1) * capacity, width:]


def ordered(plan, experts, capacity, scal, parts):
    vmem = pl.BlockSpec(memory_space=pltpu.VMEM)
    rows, width = experts * capacity, parts[0].shape[1] // 2
    return pl.pallas_call(
        functools.partial(order_kernel, plan, experts, capacity),
        out_shape=[jax.ShapeDtypeStruct((rows, width), BF16)] * 2,
        in_specs=[pl.BlockSpec(memory_space=pltpu.SMEM)] + [vmem] * len(parts),
        out_specs=[vmem] * 2,
        compiler_params=pltpu.CompilerParams(vmem_limit_bytes=VMEM_BYTES),
        cost_estimate=pl.CostEstimate(flops=0, bytes_accessed=8 * rows * width, transcendentals=0),
        name="hot_rows_ordered",
    )(scal, *parts)


def shadow_kernel(experts, scal, mine, theirs, hot_mine, hot_theirs, out):
    own = scal[0]
    taken = mine.shape[0]
    width = out.shape[1]
    gates = taken * experts * 2 // 3
    column = own * taken + lax.broadcasted_iota(jnp.int32, (taken, 1), 0)

    def product(first):
        columns = pl.ds(first, width)
        return dot(mine[...], hot_mine[:, columns], (1, 0)) + dot(theirs[...], hot_theirs[:, columns], (1, 0))

    @pl.when((own + 1) * taken <= gates)
    def _():
        out[...] = product(0)

    @pl.when(own * taken >= gates)
    def _():
        out[...] = product(width)

    @pl.when((own * taken < gates) & ((own + 1) * taken > gates))
    def _():
        out[...] = jnp.where(column < gates, product(0), product(width))


def shadow_gradient(experts, scal, mine, theirs, hot_mine, hot_theirs):
    taken, rows = mine.shape
    width = hot_mine.shape[1] // 2
    vmem = pl.BlockSpec(memory_space=pltpu.VMEM)
    return pl.pallas_call(
        functools.partial(shadow_kernel, experts),
        out_shape=jax.ShapeDtypeStruct((taken, width), F32),
        in_specs=[pl.BlockSpec(memory_space=pltpu.SMEM)] + [vmem] * 4,
        out_specs=vmem,
        compiler_params=pltpu.CompilerParams(vmem_limit_bytes=24 * 1024 * 1024),
        cost_estimate=pl.CostEstimate(
            flops=4 * taken * rows * width, bytes_accessed=4 * rows * width, transcendentals=0
        ),
        name="shadow_gradient",
    )(scal, mine, theirs, hot_mine, hot_theirs)


def on_device(
    tokens, cotangent, routes, route_weight, ratio_advantage, clip_mask, shadow_plan, gate_up, down
):
    experts = lax.axis_size("expert")
    tok_rows, width = tokens.shape
    fanout = routes.shape[1]
    units = down.shape[1]
    capacity = 2 * tok_rows * fanout // experts
    gate_up, down = gate_up[0], down[0]
    order = ring_order(experts)
    half = experts // 2

    def shift(block, step):
        pairs = [(order[i], order[(i + step) % experts]) for i in range(experts)]
        return lax.ppermute(block, "expert", pairs)

    def swap(block):
        return lax.ppermute(block, "dp", [(0, 1), (1, 0)])

    own = lax.axis_index("expert")
    hottest = shadow_plan[0]
    scal = jnp.stack([own, lax.axis_index("dp"), hottest]).astype(jnp.int32)
    message, meta = build_message(tokens, routes, route_weight, ratio_advantage, clip_mask)

    plan = distances(experts)
    mine, packs, hot, turned, late = [], [], [], [], []
    returned = {}
    up, below, held = [message, cotangent], [message, cotangent], [[message], [cotangent]]
    for number, steps in enumerate(plan):
        if number + 1 < half:
            up, below = [shift(part, 1) for part in up], [shift(part, -1) for part in below]
            following = [[up[0], below[0]], [up[1], below[1]]]
        elif number + 1 == half:
            following = [[shift(up[0], 1)], [shift(below[1], -1)]]
        if number > 1:
            sent, other = late[number - 2]
            held, other = lax.optimization_barrier((held, other))
            late[number - 2] = (sent, other)
        if number == half - 1:
            held, late[: half - 2] = lax.optimization_barrier((held, late[: half - 2]))
        (rows, pack, hot_rows), back, turn = run_step(
            steps,
            fanout,
            capacity,
            scal,
            *held,
            packs[0] if number == half else None,
            gate_up,
            down,
        )
        following[1], back = lax.optimization_barrier((following[1], back))
        if number + 1 < half:
            up, below = [[part[k] for part in following] for k in range(2)]
        sent = [shift(part, step) if step else part for step, part in zip(steps, back)]
        late.append((sent, swap(pack)))
        mine.append(rows)
        packs.append(pack)
        hot.append(hot_rows)
        turned += turn
        held = following
    (back_behind, back_ahead), other = late[half - 1]
    hot_mine, hot_theirs = ordered(plan, experts, capacity, scal, hot)
    turned[-1], late[half - 2], hot_mine, hot_theirs = lax.optimization_barrier(
        (turned[-1], late[half - 2], hot_mine, hot_theirs)
    )

    taken = 3 * units // experts
    ring_hot = to_ring(hottest, experts)
    is_hot = own == hottest

    def chunk(distance):
        owner = from_ring((ring_hot + distance + experts) % experts, experts)
        parts = [lax.dynamic_slice_in_dim(part, owner * taken, taken, axis=0) for part in turned]
        return jnp.concatenate(parts, axis=1)

    lanes = experts * capacity // 2

    def halves(distance):
        columns = chunk(distance)
        return [columns[:, :lanes], columns[:, lanes:]]

    far = halves(half)
    far, other = lax.optimization_barrier((far, other))
    hot_theirs = swap(hot_theirs)
    far = [shift(far[0], 1), shift(far[1], -1)]
    others = [part for _, part in late[: half - 1]] + [other, late[half][1]]
    expert_grad = expert_gradient(units, scal, mine, packs, others)
    chunks = {distance: halves(distance) for distance in range(1 - half, half)}
    (back_far,) = late[half][0]
    far, expert_grad, back_ahead, back_behind, back_far, chunks = lax.optimization_barrier(
        (far, expert_grad, back_ahead, back_behind, back_far, chunks)
    )
    ahead, behind = [far[0], None], [None, far[1]]

    def onward(kept, received, step):
        return shift(kept if received is None else jnp.where(is_hot, kept, received), step)

    for number in range(1, half):
        for k in range(2):
            ahead[k] = onward(chunks[half - number][k], ahead[k], 1)
            behind[k] = onward(chunks[number - half][k], behind[k], -1)
    sent = [rows for rows, _ in late[: half - 1]] + [[back_behind, back_ahead], [back_far]]
    for steps, parts in zip(plan, sent):
        for step, part in zip(steps, parts):
            returned[step % experts] = part
    token_grad = combine(experts, fanout, capacity, scal, meta, [returned[d] for d in range(experts)])
    ahead, behind, token_grad = lax.optimization_barrier((ahead, behind, token_grad))
    away = (to_ring(own, experts) - ring_hot + experts) % experts
    columns = [
        jnp.where(away == 0, chunks[0][k], jnp.where(away <= half - k, ahead[k], behind[k]))
        for k in range(2)
    ]
    columns = jnp.concatenate(columns, axis=1)
    shadow_grad = shadow_gradient(
        experts, scal, columns, swap(columns), hot_mine, hot_theirs
    ).T
    return (token_grad, expert_grad, shadow_grad)


def solution(mesh):
    placed = (
        P(("group", "expert", "dp"), None),
        P(("group", "expert", "dp"), None),
        P(("group", "expert", "dp"), None),
        P(("group", "expert", "dp"), None),
        P(("group", "expert", "dp")),
        P(("group", "expert", "dp")),
        P("group"),
        P("expert", None, None),
        P("expert", None, None),
    )
    return jax.shard_map(
        on_device,
        mesh=mesh,
        in_specs=placed,
        out_specs=(
            P(("group", "expert", "dp"), None),
            P(("group", "expert"), "dp", None),
            P(("group", "dp"), "expert"),
        ),
        check_vma=False,
    )
```

```python
import functools

import jax
import jax.numpy as jnp
from jax import lax
from jax.experimental import pallas as pl
from jax.experimental.pallas import tpu as pltpu
from jax.sharding import PartitionSpec as P

BF16 = jnp.bfloat16
F32 = jnp.float32
VMEM_BYTES = 56 * 1024 * 1024


def snaked(experts):
    return experts <= 8


def to_ring(expert, experts):
    if not snaked(experts):
        return expert
    down = experts - 1 - (expert - 1) // 2
    return jnp.where(expert % 2 == 0, expert // 2, down)


def from_ring(place, experts):
    if not snaked(experts):
        return place
    return jnp.where(place < experts // 2, 2 * place, 2 * (experts - 1 - place) + 1)


def ring_order(experts):
    if not snaked(experts):
        return list(range(experts))
    return list(range(0, experts, 2)) + list(range(experts - 1, 0, -2))


def distances(experts):
    half = experts // 2
    return [[0]] + [[-step, step] for step in range(1, half)] + [[half]]


def slot_place(distance, experts):
    half = experts // 2
    near = jnp.where(distance < half, 2 * distance - 1, 2 * (experts - distance) - 2)
    near = jnp.where(distance == half, experts - 1, near)
    return jnp.where(distance == 0, experts - 2, near)


def dot(a, b, dims):
    return lax.dot_general(a, b, ((dims[:1], dims[1:]), ((), ())), preferred_element_type=F32)


def selection(table, expert, fanout, capacity):
    tokens = table.shape[1]
    hit = table[:fanout] == expert.astype(F32)
    named = jnp.sum(jnp.where(hit, 1.0, 0.0), axis=0, keepdims=True)
    parts = table[fanout : 4 * fanout]
    weights = parts[:fanout] + parts[fanout : 2 * fanout] + parts[2 * fanout :]
    weight = jnp.sum(jnp.where(hit, weights, 0.0), axis=0, keepdims=True)
    upto = lax.broadcasted_iota(jnp.int32, (tokens, tokens), 0) <= lax.broadcasted_iota(
        jnp.int32, (tokens, tokens), 1
    )
    upto = jnp.where(upto, 1.0, 0.0).astype(BF16)
    place = dot(jnp.broadcast_to(named, (8, tokens)).astype(BF16), upto, (1, 0))[:1]
    row = lax.broadcasted_iota(jnp.int32, (capacity, tokens), 0).astype(F32) + 1.0
    onehot = jnp.where((row == place) & (named > 0.5), 1.0, 0.0)
    return onehot, weight


def step_kernel(steps, fanout, capacity, joined, scal, *refs):
    count = len(steps)
    messages, cotangents, refs = refs[:count], refs[count : 2 * count], refs[2 * count :]
    if joined:
        first, refs = refs[0], refs[1:]
    weights_gu, weights_down, mine, pack, hot = refs[:5]
    back, refs = refs[5 : 5 + count], refs[5 + count :]
    if len(refs) > 7:
        turned, refs = refs[0], refs[1:]
    else:
        turned = None
    rows_in, rows_cot, hot_in, hot_cot, gate_up, down, sems = refs
    own, half, hottest = scal[0], scal[1], scal[2]
    units, width = down.shape
    load_gu = pltpu.make_async_copy(weights_gu, gate_up, sems.at[0])
    load_down = pltpu.make_async_copy(weights_down, down, sems.at[1])
    load_gu.start()
    load_down.start()
    for at, (message, cotangent) in enumerate(zip(messages, cotangents)):
        rows = slice(at * capacity, (at + 1) * capacity)
        table = message[:, width:].astype(F32).T
        own_hot, own_weight = selection(table, own, fanout, capacity)
        all_hot, all_weight = selection(table, hottest, fanout, capacity)
        scale = jnp.concatenate(
            [
                jnp.sum(own_hot * own_weight, axis=1, keepdims=True),
                jnp.sum(all_hot * all_weight, axis=1, keepdims=True),
            ],
            axis=0,
        )
        onehot = jnp.concatenate([own_hot, all_hot], axis=0).astype(BF16)
        picked = dot(onehot, message[:, :width], (1, 0)).astype(BF16)
        rows_in[rows, :] = picked[:capacity]
        hot_in[rows, :] = picked[capacity:]
        picked = (scale * dot(onehot, cotangent[...], (1, 0))).astype(BF16)
        rows_cot[rows, :] = picked[:capacity]
        hot_cot[rows, :] = picked[capacity:]
    part = width // 2
    here = pl.ds(pl.multiple_of(half * part, part), part)
    there = pl.ds(pl.multiple_of((1 - half) * part, part), part)
    mine[:, :part] = rows_in[:, here]
    mine[:, part:] = rows_cot[:, here]
    pack[:, 3 * units : 3 * units + part] = rows_in[:, there]
    pack[:, 3 * units + part :] = rows_cot[:, there]
    hot[:, :part] = hot_in[:, here]
    hot[:, part:width] = hot_cot[:, here]
    hot[:, width : width + part] = hot_in[:, there]
    hot[:, width + part :] = hot_cot[:, there]
    load_gu.wait()
    projected = dot(rows_in[...], gate_up[...], (1, 0))
    gate_pre, up_pre = projected[:, :units], projected[:, units:]
    load_down.wait()
    hidden_grad = dot(rows_cot[...], down[...], (1, 1))
    sigmoid_gate = jax.nn.sigmoid(gate_pre)
    activation = gate_pre * sigmoid_gate
    gate_grad = hidden_grad * up_pre * sigmoid_gate * (1.0 + gate_pre * (1.0 - sigmoid_gate))
    pack[:, :units] = gate_grad.astype(BF16)
    pack[:, units : 2 * units] = (hidden_grad * activation).astype(BF16)
    pack[:, 2 * units : 3 * units] = (activation * up_pre).astype(BF16)
    input_rows = dot(pack[:, : 2 * units], gate_up[...], (1, 1)).astype(BF16)
    for at, part in enumerate(back):
        part[...] = input_rows[at * part.shape[0] : (at + 1) * part.shape[0]]
    if turned is not None:
        grads = pack[:, : 3 * units]
        if joined:
            grads = jnp.concatenate([first[:, : 3 * units], grads], axis=0)
        turned[...] = grads.T


def run_step(steps, fanout, capacity, scal, messages, cotangents, first, gate_up, down):
    count, rows = len(steps), len(steps) * capacity
    units, width = down.shape
    vmem = pl.BlockSpec(memory_space=pltpu.VMEM)
    far = pl.BlockSpec(memory_space=pl.ANY)
    shapes = [(rows, width), (rows, 3 * units + width), (rows, 2 * width)]
    joined = first is not None
    shapes += [(capacity, width)] * count
    if joined or count > 1:
        shapes += [(3 * units, 2 * capacity)]
    firsts = [first] if joined else []
    out = pl.pallas_call(
        functools.partial(step_kernel, steps, fanout, capacity, joined),
        out_shape=[jax.ShapeDtypeStruct(shape, BF16) for shape in shapes],
        in_specs=[pl.BlockSpec(memory_space=pltpu.SMEM)] + [vmem] * (2 * count + len(firsts)) + [far] * 2,
        out_specs=[vmem] * len(shapes),
        scratch_shapes=[pltpu.VMEM((rows, width), BF16)] * 4
        + [
            pltpu.VMEM(gate_up.shape, BF16),
            pltpu.VMEM(down.shape, BF16),
            pltpu.SemaphoreType.DMA((2,)),
        ],
        compiler_params=pltpu.CompilerParams(vmem_limit_bytes=VMEM_BYTES),
        cost_estimate=pl.CostEstimate(
            flops=2 * 256 * 5 * width * units, bytes_accessed=3 * 2 * width * units, transcendentals=0
        ),
        name="expert_step",
    )(scal, *messages, *cotangents, *firsts, gate_up, down)
    return out[:3], out[3 : 3 + count], out[3 + count :]


def combine_kernel(experts, fanout, capacity, scal, meta, *refs):
    rows, out = refs[:-1], refs[-1]
    place = to_ring(scal[0], experts)
    table = meta[...].astype(F32).T
    picks = []
    for step in range(experts):
        expert = from_ring((place - step + experts) % experts, experts)
        picks.append(selection(table, expert, fanout, capacity)[0])
    onehot = jnp.concatenate(picks, axis=0).astype(BF16)
    out[...] = dot(onehot, jnp.concatenate([part[...] for part in rows], axis=0), (0, 0)).astype(BF16)


def combine(experts, fanout, capacity, scal, meta, rows):
    vmem = pl.BlockSpec(memory_space=pltpu.VMEM)
    tokens, width = meta.shape[0], rows[0].shape[1]
    return pl.pallas_call(
        functools.partial(combine_kernel, experts, fanout, capacity),
        out_shape=jax.ShapeDtypeStruct((tokens, width), BF16),
        in_specs=[pl.BlockSpec(memory_space=pltpu.SMEM)] + [vmem] * (len(rows) + 1),
        out_specs=vmem,
        compiler_params=pltpu.CompilerParams(vmem_limit_bytes=VMEM_BYTES),
        cost_estimate=pl.CostEstimate(
            flops=2 * experts * capacity * tokens * width, bytes_accessed=2 * experts * capacity * width, transcendentals=0
        ),
        name="token_sum",
    )(scal, meta, *rows)


def gradient_kernel(units, count, scal, *refs):
    ins, cots, grads = refs[: 2 * count], refs[2 * count : 4 * count], refs[4 * count : 6 * count]
    out = refs[6 * count]
    keep = scal[0] != scal[2]
    left = jnp.concatenate([ref[...] for ref in ins], axis=0)
    right = jnp.concatenate([ref[:, : 2 * units] for ref in grads], axis=0)
    out[0, :, : 2 * units] = jnp.where(keep, dot(left, right, (0, 0)), 0.0)
    left = jnp.concatenate([ref[...] for ref in cots], axis=0)
    right = jnp.concatenate([ref[:, 2 * units :] for ref in grads], axis=0)
    out[0, :, 2 * units :] = jnp.where(keep, dot(left, right, (0, 0)), 0.0)


def expert_gradient(units, scal, mine, packs, others):
    width, columns, count = mine[0].shape[1], 3 * units, len(mine)
    tile = 256
    tiles, skip = width // 2 // tile, columns // tile
    total = 2 * sum(part.shape[0] for part in mine)
    rows = mine + others

    def tiled(first):
        specs = [pl.BlockSpec((part.shape[0], tile), lambda i: (0, i + first)) for part in mine]
        return specs + [
            pl.BlockSpec((part.shape[0], tile), lambda i: (0, i + first + skip)) for part in others
        ]

    in_specs = [pl.BlockSpec(memory_space=pltpu.SMEM)] + tiled(0) + tiled(tiles)
    in_specs += [pl.BlockSpec((part.shape[0], columns), lambda i: (0, 0)) for part in packs + others]
    return pl.pallas_call(
        functools.partial(gradient_kernel, units, count),
        grid=(tiles,),
        out_shape=jax.ShapeDtypeStruct((1, width // 2, columns), F32),
        in_specs=in_specs,
        out_specs=pl.BlockSpec((1, tile, columns), lambda i: (0, i, 0)),
        compiler_params=pltpu.CompilerParams(vmem_limit_bytes=VMEM_BYTES),
        cost_estimate=pl.CostEstimate(
            flops=width * columns * total, bytes_accessed=3 * width * columns, transcendentals=0
        ),
        name="expert_gradient",
    )(scal, *rows, *rows, *packs, *others)


def message_kernel(fanout, tokens, routes, route_weight, ratio, clip, message, meta):
    count, width = tokens.shape
    message[:, :width] = tokens[...]
    weight = route_weight[...] * ratio[...] * clip[...].astype(F32)
    first = weight.astype(BF16).astype(F32)
    rest = weight - first
    second = rest.astype(BF16).astype(F32)
    lines = -(-4 * fanout // 8) * 8
    row = lax.broadcasted_iota(jnp.int32, (lines, count), 0)
    table = jnp.zeros((lines, count), F32)
    for number, part in enumerate([routes[...].astype(F32), first, second, rest - second]):
        for k in range(fanout):
            table = jnp.where(row == number * fanout + k, part[k : k + 1], table)
    table = jnp.concatenate([table, jnp.zeros((128 - lines, count), F32)], axis=0)
    columns = table.T.astype(BF16)
    message[:, width:] = columns
    meta[...] = columns


def build_message(tokens, routes, route_weight, ratio, clip):
    count, width = tokens.shape
    vmem = pl.BlockSpec(memory_space=pltpu.VMEM)
    return pl.pallas_call(
        functools.partial(message_kernel, routes.shape[1]),
        out_shape=[
            jax.ShapeDtypeStruct((count, width + 128), BF16),
            jax.ShapeDtypeStruct((count, 128), BF16),
        ],
        in_specs=[vmem] * 5,
        out_specs=[vmem] * 2,
        cost_estimate=pl.CostEstimate(flops=0, bytes_accessed=4 * count * width, transcendentals=0),
        name="ring_message",
    )(tokens, routes.T, route_weight.T, ratio[None], clip[None])


def order_kernel(plan, experts, capacity, scal, *refs):
    parts, mine, theirs = refs[:-2], refs[-2], refs[-1]
    shift = to_ring(scal[0], experts) - to_ring(scal[2], experts)
    width = mine.shape[1]
    for steps, part in zip(plan, parts):
        for at, step in enumerate(steps):
            place = slot_place((shift + step + 2 * experts) % experts, experts)
            there = pl.ds(pl.multiple_of(place * capacity, capacity), capacity)
            mine[there, :] = part[at * capacity : (at + 1) * capacity, :width]
            theirs[there, :] = part[at * capacity : (at + 1) * capacity, width:]


def ordered(plan, experts, capacity, scal, parts):
    vmem = pl.BlockSpec(memory_space=pltpu.VMEM)
    rows, width = experts * capacity, parts[0].shape[1] // 2
    return pl.pallas_call(
        functools.partial(order_kernel, plan, experts, capacity),
        out_shape=[jax.ShapeDtypeStruct((rows, width), BF16)] * 2,
        in_specs=[pl.BlockSpec(memory_space=pltpu.SMEM)] + [vmem] * len(parts),
        out_specs=[vmem] * 2,
        compiler_params=pltpu.CompilerParams(vmem_limit_bytes=VMEM_BYTES),
        cost_estimate=pl.CostEstimate(flops=0, bytes_accessed=8 * rows * width, transcendentals=0),
        name="hot_rows_ordered",
    )(scal, *parts)


def shadow_kernel(experts, scal, mine, theirs, hot_mine, hot_theirs, out):
    own = scal[0]
    taken = mine.shape[0]
    width = out.shape[1]
    gates = taken * experts * 2 // 3
    column = own * taken + lax.broadcasted_iota(jnp.int32, (taken, 1), 0)

    def product(first):
        columns = pl.ds(first, width)
        return dot(mine[...], hot_mine[:, columns], (1, 0)) + dot(theirs[...], hot_theirs[:, columns], (1, 0))

    @pl.when((own + 1) * taken <= gates)
    def _():
        out[...] = product(0)

    @pl.when(own * taken >= gates)
    def _():
        out[...] = product(width)

    @pl.when((own * taken < gates) & ((own + 1) * taken > gates))
    def _():
        out[...] = jnp.where(column < gates, product(0), product(width))


def shadow_gradient(experts, scal, mine, theirs, hot_mine, hot_theirs):
    taken, rows = mine.shape
    width = hot_mine.shape[1] // 2
    vmem = pl.BlockSpec(memory_space=pltpu.VMEM)
    return pl.pallas_call(
        functools.partial(shadow_kernel, experts),
        out_shape=jax.ShapeDtypeStruct((taken, width), F32),
        in_specs=[pl.BlockSpec(memory_space=pltpu.SMEM)] + [vmem] * 4,
        out_specs=vmem,
        compiler_params=pltpu.CompilerParams(vmem_limit_bytes=24 * 1024 * 1024),
        cost_estimate=pl.CostEstimate(
            flops=4 * taken * rows * width, bytes_accessed=4 * rows * width, transcendentals=0
        ),
        name="shadow_gradient",
    )(scal, mine, theirs, hot_mine, hot_theirs)


def on_device(
    tokens, cotangent, routes, route_weight, ratio_advantage, clip_mask, shadow_plan, gate_up, down
):
    experts = lax.axis_size("expert")
    tok_rows, width = tokens.shape
    fanout = routes.shape[1]
    units = down.shape[1]
    capacity = 2 * tok_rows * fanout // experts
    gate_up, down = gate_up[0], down[0]
    order = ring_order(experts)
    half = experts // 2

    def shift(block, step):
        pairs = [(order[i], order[(i + step) % experts]) for i in range(experts)]
        return lax.ppermute(block, "expert", pairs)

    def swap(block):
        return lax.ppermute(block, "dp", [(0, 1), (1, 0)])

    own = lax.axis_index("expert")
    hottest = shadow_plan[0]
    scal = jnp.stack([own, lax.axis_index("dp"), hottest]).astype(jnp.int32)
    message, meta = build_message(tokens, routes, route_weight, ratio_advantage, clip_mask)

    plan = distances(experts)
    mine, packs, hot, turned, late = [], [], [], [], []
    returned = {}
    up, below, held = [message, cotangent], [message, cotangent], [[message], [cotangent]]
    for number, steps in enumerate(plan):
        if number + 1 < half:
            up, below = [shift(part, 1) for part in up], [shift(part, -1) for part in below]
            following = [[up[0], below[0]], [up[1], below[1]]]
        elif number + 1 == half:
            following = [[shift(up[0], 1)], [shift(below[1], -1)]]
        if number > 1:
            sent, other = late[number - 2]
            held, other = lax.optimization_barrier((held, other))
            late[number - 2] = (sent, other)
        if number == half - 1:
            held, late[: half - 2] = lax.optimization_barrier((held, late[: half - 2]))
        (rows, pack, hot_rows), back, turn = run_step(
            steps,
            fanout,
            capacity,
            scal,
            *held,
            packs[0] if number == half else None,
            gate_up,
            down,
        )
        following[1], back = lax.optimization_barrier((following[1], back))
        if number + 1 < half:
            up, below = [[part[k] for part in following] for k in range(2)]
        if number < half:
            sent = [shift(part, step) if step else part for step, part in zip(steps, back)]
        else:
            sent = back
        late.append((sent, swap(pack)))
        mine.append(rows)
        packs.append(pack)
        hot.append(hot_rows)
        turned += turn
        held = following
    (back_behind, back_ahead), other = late[half - 1]
    hot_mine, hot_theirs = ordered(plan, experts, capacity, scal, hot)
    turned[-1], late[half - 2], hot_mine, hot_theirs = lax.optimization_barrier(
        (turned[-1], late[half - 2], hot_mine, hot_theirs)
    )

    taken = 3 * units // experts
    ring_hot = to_ring(hottest, experts)
    is_hot = own == hottest

    def chunk(distance):
        owner = from_ring((ring_hot + distance + experts) % experts, experts)
        parts = [lax.dynamic_slice_in_dim(part, owner * taken, taken, axis=0) for part in turned]
        return jnp.concatenate(parts, axis=1)

    lanes = experts * capacity // 2

    def halves(distance):
        columns = chunk(distance)
        return [columns[:, :lanes], columns[:, lanes:]]

    far = halves(half)
    (back_far,) = late[half][0]
    far, other, back_far = lax.optimization_barrier((far, other, back_far))
    back_far = shift(back_far, half)
    hot_theirs = swap(hot_theirs)
    far = [shift(far[0], 1), shift(far[1], -1)]
    others = [part for _, part in late[: half - 1]] + [other, late[half][1]]
    expert_grad = expert_gradient(units, scal, mine, packs, others)
    chunks = {distance: halves(distance) for distance in range(1 - half, half)}
    far, expert_grad, back_ahead, back_behind, back_far, chunks = lax.optimization_barrier(
        (far, expert_grad, back_ahead, back_behind, back_far, chunks)
    )
    ahead, behind = [far[0], None], [None, far[1]]

    def onward(kept, received, step):
        return shift(kept if received is None else jnp.where(is_hot, kept, received), step)

    for number in range(1, half):
        for k in range(2):
            ahead[k] = onward(chunks[half - number][k], ahead[k], 1)
            behind[k] = onward(chunks[number - half][k], behind[k], -1)
    sent = [rows for rows, _ in late[: half - 1]] + [[back_behind, back_ahead], [back_far]]
    for steps, parts in zip(plan, sent):
        for step, part in zip(steps, parts):
            returned[step % experts] = part
    token_grad = combine(experts, fanout, capacity, scal, meta, [returned[d] for d in range(experts)])
    ahead, behind, token_grad = lax.optimization_barrier((ahead, behind, token_grad))
    away = (to_ring(own, experts) - ring_hot + experts) % experts
    columns = [
        jnp.where(away == 0, chunks[0][k], jnp.where(away <= half - k, ahead[k], behind[k]))
        for k in range(2)
    ]
    columns = jnp.concatenate(columns, axis=1)
    shadow_grad = shadow_gradient(
        experts, scal, columns, swap(columns), hot_mine, hot_theirs
    ).T
    return (token_grad, expert_grad, shadow_grad)


def solution(mesh):
    placed = (
        P(("group", "expert", "dp"), None),
        P(("group", "expert", "dp"), None),
        P(("group", "expert", "dp"), None),
        P(("group", "expert", "dp"), None),
        P(("group", "expert", "dp")),
        P(("group", "expert", "dp")),
        P("group"),
        P("expert", None, None),
        P("expert", None, None),
    )
    return jax.shard_map(
        on_device,
        mesh=mesh,
        in_specs=placed,
        out_specs=(
            P(("group", "expert", "dp"), None),
            P(("group", "expert"), "dp", None),
            P(("group", "dp"), "expert"),
        ),
        check_vma=False,
    )
```
